32 devices in a mesh: fsdp: 8 (over y, x, core), tensor: 4 (over z).
Axes of the slice: x: 2, y: 2, z: 4, core: 2. Of those that a mesh axis runs over, the one named last changes fastest.
Arguments:
- tokens: bfloat16 [2048, 2048], P('fsdp'), may hold values from -6 to 6
- cotangent: bfloat16 [2048, 2048], P('fsdp'), may hold values from -6 to 6
- routes: int32 [2048, 8], P('fsdp'), may hold values from 0 to 63, all different within a row; in each aligned block of 256 rows (0 to 255, 256 to 511, ...) at most 40 rows name the same one
- w_query: bfloat16 [2048, 2048], P('fsdp', 'tensor'), may hold values from -0.125 to 0.125
- w_key: bfloat16 [2048, 2048], P('fsdp', 'tensor'), may hold values from -0.125 to 0.125
- w_value: bfloat16 [2048, 2048], P('fsdp', 'tensor'), may hold values from -0.125 to 0.125
- w_output: bfloat16 [2048, 2048], P('fsdp', 'tensor'), may hold values from -1.25 to 1.25
- w_router: bfloat16 [2048, 64], P('fsdp'), may hold values from -0.0625 to 0.0625
- attn_gain: bfloat16 [2048], P('fsdp'), may hold values from 0.25 to 1.75
- ffn_gain: bfloat16 [2048], P('fsdp'), may hold values from 0.25 to 1.75
- query_gain: bfloat16 [128], P('fsdp'), may hold values from 0.25 to 1.75
- key_gain: bfloat16 [128], P('fsdp'), may hold values from 0.25 to 1.75
- expert_weights: bfloat16 [64, 3, 2048, 1024], P('fsdp', None, None, 'tensor'), may hold values from -4 to 4
Outputs:
- layer_out: bfloat16 [2048, 2048], P('fsdp')
- grad_tokens: bfloat16 [2048, 2048], P('fsdp')
- grad_query: float32 [2048, 2048], P('fsdp', 'tensor')
- grad_key: float32 [2048, 2048], P('fsdp', 'tensor')
- grad_value: float32 [2048, 2048], P('fsdp', 'tensor')
- grad_output: float32 [2048, 2048], P('fsdp', 'tensor')
- grad_router: float32 [2048, 64], P('fsdp')
- grad_attn_gain: float32 [2048], P('fsdp')
- grad_ffn_gain: float32 [2048], P('fsdp')
- grad_query_gain: float32 [128], P('fsdp')
- grad_key_gain: float32 [128], P('fsdp')
- grad_experts: float32 [64, 3, 2048, 1024], P('fsdp', None, None, 'tensor')
The draws below stay inside these ranges and needn't reach their ends.
Inputs may be any that keep to these rules, and one draw needn't show every extreme that they name: `routes`: each row names 8 different experts. Among the 256 rows of one index of fsdp no expert is named more than 40 times, a bound that some expert reaches in some such block.
All inputs are finite; a program needn't handle non-finite values.
Results may differ from the reference program's by a relative error of at most 0.02.
Values may be sent and summed in bfloat16 or wider, within the bound.
No kernel may reach another device: no remote copies, remote signals or barrier semaphores. Data moves between devices by JAX's collectives and lax.ppermute only.
A program may use at most 320 MiB of HBM per device.

```python
import math
import jax
import jax.numpy as jnp
import numpy as np
from jax import lax

D = 2048
HEADS = 16
HD = 128
EXPERTS = 64
TOPK = 8
FF = 1024
SEQ = 256
CAP = 40
TOKENS = 2048


def draw_expert_weights(key, part):
    key = jax.random.fold_in(key, 11)
    full_shape = (EXPERTS, 3, D, FF)
    values = jax.random.truncated_normal(key, -4.0, 4.0, full_shape, jnp.float32)
    scales = jnp.array([D ** (-0.5), D ** (-0.5), (FF // 16) ** (-0.5)], jnp.float32)
    return (values * scales[None, :, None, None]).astype(jnp.bfloat16)


def block_scale(stream_key, shape, shards, low, largest):
    def one(dim, parts):
        draws = jax.random.uniform(jax.random.fold_in(jax.random.fold_in(stream_key, 6), dim), (parts,), jnp.float32, low / len(shards), largest / len(shards))
        return jnp.repeat(jnp.exp(draws), shape[dim] // parts).reshape((-1,) + (1,) * (len(shape) - dim - 1))

    level = one(*shards[0])
    for cut in shards[1:]:
        level = level * one(*cut)
    return level


def deal_out(rng, own, number, rows, count, top, reach, skew):
    sequence = jax.random.permutation(rng, count)
    packed, common = portions_of(count, rows * top, reach, skew, True), portions_of(count, rows * top, reach, skew, False)
    places = jnp.arange(count)

    def named(lengths, offset_by):
        used = int((lengths > 0).sum())
        fixed = max(1, used // 4)
        moved = fixed + (places - fixed + offset_by * (used - fixed)) % max(1, count - fixed)
        return jnp.zeros((count,), jnp.int32).at[sequence[jnp.where(places < fixed, places, moved)]].set(jnp.asarray(lengths, jnp.int32))

    lengths = jnp.where(number % 4 == 0, named(packed, number // 4), named(common, number - number // 4 - 1))
    mixed = jax.random.permutation(jax.random.fold_in(own, 3), count)
    giver, taker = mixed[0:count // 2 * 2:2], mixed[1:count // 2 * 2:2]
    slack = jnp.minimum(lengths[giver] - 1, reach - lengths[taker]) // 2
    slack = jnp.where((giver == sequence[0]) | (taker == sequence[0]) | (lengths[taker] == 0), 0, jnp.maximum(slack, 0))
    moved = jax.random.randint(jax.random.fold_in(own, 4), (count // 2,), 0, 1 << 20) % (slack + 1)
    lengths = lengths.at[giver].add(-moved).at[taker].add(moved)
    items = jnp.searchsorted(jnp.cumsum(lengths), jnp.arange(rows * top), side="right").astype(jnp.int32)
    listing = items.reshape(top, rows).T
    listing = listing[jax.random.permutation(jax.random.fold_in(own, 1), rows)]
    offset_by = jax.random.randint(jax.random.fold_in(own, 2), (rows, 1), 0, top)
    return jnp.take_along_axis(listing, (jnp.arange(top)[None, :] + offset_by) % top, axis=1)


def portions_of(amount, total, bound, skew, full):
    portions = [(1 << 20) // math.isqrt(grade ** skew) + 1 for grade in range(1, amount + 1)]
    largest = bound if full else min(bound, max(-(-total // amount), total * portions[0] // sum(portions)))
    least = 1 if total - largest >= amount - 1 else 0
    counts, rest = [largest] + [least] * (amount - 1), total - largest - least * (amount - 1)
    while rest > 0:
        candidates = [i for i in range(1, amount) if counts[i] < largest] or [i for i in range(1, amount) if counts[i] < bound]
        whole, left = sum([portions[i] for i in candidates]), rest
        for i in candidates:
            addition = min(bound - counts[i], max(1, left * portions[i] // whole), rest)
            counts[i] = counts[i] + addition
            rest = rest - addition
    return np.array(counts)


def normal_values(key, shape, deviation, limit, split=(), kind=jnp.bfloat16):
    values = jax.random.normal(key, shape, jnp.float32) * deviation
    if len(split) > 0:
        values = block_scale(key, shape, split, -0.22, 0.18) * values
    return jnp.clip(values, min=-limit, max=limit).astype(kind)


def setup_inputs(seed: int = 0) -> dict:
    key_of = jax.random.split(jax.random.key(seed), 14)
    tokens = normal_values(key_of[0], (TOKENS, D), 1.0, 6.0, ((0, 8),))
    cotangent = normal_values(key_of[1], (TOKENS, D), 1.0, 6.0, ((0, 8),))
    routes_keys = jax.random.split(jax.random.fold_in(key_of[2], 1), TOKENS // SEQ)
    routes_turns = jax.random.permutation(jax.random.fold_in(key_of[2], 3), TOKENS // SEQ)
    routes = jax.vmap(lambda own, number: deal_out(jax.random.fold_in(key_of[2], 2), own, number, SEQ, EXPERTS, TOPK, CAP, 0))(routes_keys, routes_turns).reshape((TOKENS, TOPK))
    w_query = normal_values(key_of[3], (D, D), D ** -0.5, 0.125, ((0, 8), (1, 4)))
    w_key = normal_values(key_of[4], (D, D), D ** -0.5, 0.125, ((0, 8), (1, 4)))
    w_value = normal_values(key_of[5], (D, D), D ** -0.5, 0.125, ((0, 8), (1, 4)))
    w_output = normal_values(key_of[6], (D, D), (max(1, 3 * D // SEQ)) ** -0.5, 1.25, ((0, 8), (1, 4)))
    w_router = normal_values(key_of[7], (D, EXPERTS), (4 * D) ** -0.5, 0.0625, ((0, 8),))
    attn_gain = jnp.clip(1.0 + 0.15 * jax.random.normal(key_of[8], (D,), jnp.float32), 0.25, 1.75).astype(jnp.bfloat16)
    ffn_gain = jnp.clip(1.0 + 0.15 * jax.random.normal(key_of[9], (D,), jnp.float32), 0.25, 1.75).astype(jnp.bfloat16)
    query_gain = jnp.clip(1.0 + 0.15 * jax.random.normal(key_of[10], (HD,), jnp.float32), 0.25, 1.75).astype(jnp.bfloat16)
    key_gain = jnp.clip(1.0 + 0.15 * jax.random.normal(key_of[11], (HD,), jnp.float32), 0.25, 1.75).astype(jnp.bfloat16)
    expert_weights = draw_expert_weights(jax.random.fold_in(key_of[13], 71), 0)
    return {"tokens": tokens, "cotangent": cotangent, "routes": routes, "w_query": w_query, "w_key": w_key, "w_value": w_value, "w_output": w_output, "w_router": w_router, "attn_gain": attn_gain, "ffn_gain": ffn_gain, "query_gain": query_gain, "key_gain": key_gain, "expert_weights": expert_weights}


EPSILON = 1e-06
ROPE_BASE = 10000.0
HIGHEST = lax.Precision.HIGHEST

@jax.custom_vjp
def low(v):
    return lax.optimization_barrier(v.astype(jnp.bfloat16)).astype(jnp.float32)

@jax.custom_vjp
def low_back(v):
    return v

def low_keep(v):
    return (low(v), None)

def low_pass(kept, grad):
    return (grad,)

def back_keep(v):
    return (v, None)

def back_low(kept, grad):
    return (low(grad),)
low.defvjp(low_keep, low_pass)
low_back.defvjp(back_keep, back_low)

def matmul(left, right):
    return jnp.dot(left, right, precision=HIGHEST)

def rms_normed(values, gain):
    return values * lax.rsqrt(lax.optimization_barrier(jnp.mean(values * values, axis=-1, keepdims=True)) + EPSILON) * gain

def rope_tables(length, head_width):
    half_width = head_width // 2
    position = jnp.arange(length, dtype=jnp.float32)[:, None]
    inverse = ROPE_BASE ** (-jnp.arange(half_width, dtype=jnp.float32) / half_width)
    angles = (position * inverse[None, :])[:, None, :]
    return (jnp.cos(angles), jnp.sin(angles))

def rotate(values, cosine, sine_part, direction):
    half_width = values.shape[-1] // 2
    front_half = values[..., :half_width]
    back_half = values[..., half_width:]
    return jnp.concatenate([front_half * cosine - direction * back_half * sine_part, back_half * cosine + direction * front_half * sine_part], axis=-1)

def slot_tables(route_ids, experts, capacity):
    pair_count = route_ids.shape[0] * route_ids.shape[1]
    chosen = route_ids.reshape(-1)
    onehot = (chosen[:, None] == jnp.arange(experts, dtype=jnp.int32)[None, :]).astype(jnp.int32)
    earlier = jnp.cumsum(onehot, axis=0) - onehot
    places = lax.optimization_barrier(jnp.sum(earlier * onehot, axis=1)).astype(jnp.int32)
    slot_ids = (chosen * capacity + places).astype(jnp.int32)
    owners = jnp.full((experts * capacity,), route_ids.shape[0], jnp.int32)
    owners = owners.at[slot_ids].set(jnp.arange(pair_count, dtype=jnp.int32) // route_ids.shape[1])
    return (slot_ids.reshape(route_ids.shape), owners)

def block_forward(residual, route_ids, w_query, w_key, w_value, w_output, w_router, attn_gain, ffn_gain, query_gain, key_gain, expert_weights):
    length = residual.shape[0]
    normed = low(rms_normed(residual, attn_gain))
    queries = low_back(matmul(normed, w_query)).reshape(length, HEADS, HD)
    keyset = low_back(matmul(normed, w_key)).reshape(length, HEADS, HD)
    values = low(low_back(matmul(normed, w_value))).reshape(length, HEADS, HD)
    cosine, sine_part = rope_tables(length, HD)
    queries = low(rotate(rms_normed(queries, query_gain), cosine, sine_part, 1.0))
    keyset = low(rotate(rms_normed(keyset, key_gain), cosine, sine_part, 1.0))
    block_rows = min(512, length)
    score_scale = HD ** (-0.5)

    def attend(query_block):
        scores = low_back(jnp.einsum('qhd,khd->hqk', query_block, keyset, precision=HIGHEST) * score_scale)
        probabilities = low(jax.nn.softmax(scores, axis=-1))
        return jnp.einsum('hqk,khd->qhd', probabilities, values, precision=HIGHEST)
    attended = lax.map(jax.checkpoint(attend), queries.reshape(length // block_rows, block_rows, HEADS, HD))
    attended = low(low_back(attended.reshape(length, HEADS * HD)))
    after_attn = residual + low_back(matmul(attended, w_output.T))
    normed_two = low(rms_normed(after_attn, ffn_gain))
    logits = low_back(matmul(normed_two, w_router))
    chosen = jnp.take_along_axis(logits, route_ids, axis=1)
    gate_values = jax.nn.softmax(chosen, axis=-1)
    slot_ids, owners = slot_tables(route_ids, EXPERTS, CAP)
    padded = jnp.concatenate([normed_two, jnp.zeros((1, D), normed_two.dtype)], axis=0)
    routed = padded[owners].reshape(EXPERTS, CAP, D)
    gate_pre = low_back(jnp.einsum('ecd,edf->ecf', routed, expert_weights[:, 0], precision=HIGHEST))
    up_pre = low_back(jnp.einsum('ecd,edf->ecf', routed, expert_weights[:, 1], precision=HIGHEST))
    hidden = low(gate_pre * jax.nn.sigmoid(gate_pre) * up_pre)
    result = low_back(jnp.einsum('ecf,edf->ecd', hidden, expert_weights[:, 2], precision=HIGHEST))
    result = result.reshape(EXPERTS * CAP, D)
    moe_out = lax.optimization_barrier(jnp.sum(gate_values[:, :, None] * result[slot_ids], axis=1))
    return after_attn + moe_out

def reference(tokens, cotangent, routes, w_query, w_key, w_value, w_output, w_router, attn_gain, ffn_gain, query_gain, key_gain, expert_weights):
    weights = tuple((weight_arg.astype(jnp.float32) for weight_arg in (w_query, w_key, w_value, w_output, w_router, attn_gain, ffn_gain, query_gain, key_gain, expert_weights)))
    seq_count = tokens.shape[0] // SEQ

    def one_sequence(running, inputs):
        seq_tokens, seq_cot, seq_routes = inputs

        def forward(residual, *params):
            return block_forward(residual, seq_routes, *params)
        output, pullback = jax.vjp(forward, seq_tokens.astype(jnp.float32), *weights)
        gradients = pullback(seq_cot.astype(jnp.float32))
        updated = tuple((running_sum + grad_part for running_sum, grad_part in zip(running, gradients[1:])))
        return (updated, (output.astype(jnp.bfloat16), gradients[0].astype(jnp.bfloat16)))
    zero_grads = tuple((jnp.zeros_like(weight_arg) for weight_arg in weights))
    totals, (layer_out, input_grad) = lax.scan(one_sequence, zero_grads, (tokens.reshape(seq_count, SEQ, D), cotangent.reshape(seq_count, SEQ, D), routes.reshape(seq_count, SEQ, TOPK)))
    return (layer_out.reshape(-1, D), input_grad.reshape(-1, D), totals[0], totals[1], totals[2], totals[3], totals[4], totals[5], totals[6], totals[7], totals[8], totals[9])
```

```python
import functools

import jax
import jax.numpy as jnp
from jax import lax
from jax.experimental import pallas as pl
from jax.experimental.pallas import tpu as pltpu
from jax.sharding import PartitionSpec as P

D = 2048
HD = 128
EXPERTS = 64
CAP = 40
SIDE = 128
EPSILON = 1e-06
ROPE_BASE = 10000.0

F32 = jnp.float32
BF16 = jnp.bfloat16
VMEM = pl.BlockSpec(memory_space=pltpu.VMEM)
SMEM = pl.BlockSpec(memory_space=pltpu.SMEM)
HBM = pl.BlockSpec(memory_space=pl.ANY)
VMEM_BYTES = 60 * 1024 * 1024


def shape(dims, dtype):
    return jax.ShapeDtypeStruct(tuple(dims), dtype)


def params(**more):
    return pltpu.CompilerParams(vmem_limit_bytes=VMEM_BYTES, **more)


def cost(flops, moved):
    return pl.CostEstimate(flops=int(flops), bytes_accessed=int(moved), transcendentals=0)


def dot(left, right):
    return jnp.dot(left, right, preferred_element_type=F32)


def dot_nt(left, right):
    return lax.dot_general(left, right, (((1,), (1,)), ((), ())), preferred_element_type=F32)


def dot_tn(left, right):
    return lax.dot_general(left, right, (((0,), (0,)), ((), ())), preferred_element_type=F32)


def rms_inverse(values):
    return lax.rsqrt(jnp.mean(values * values, axis=-1, keepdims=True) + EPSILON)


def norm_backward(values, inverse, gain, upstream):
    scaled = gain * upstream
    return inverse * scaled - values * (inverse * inverse * inverse) * jnp.mean(
        values * scaled, axis=-1, keepdims=True
    )


def half_turn(values):
    return pltpu.roll(values, HD // 2, 1)


def lanes(dims):
    return lax.broadcasted_iota(jnp.int32, dims, len(dims) - 1)


def swap(block, axis, size, step):
    return lax.ppermute(block, axis, [(i, i ^ step) for i in range(size)])


def plane_gather(block, size):
    if size != 8:
        return [(0, 0, block)] + [(p, 0, swap(block, "fsdp", size, p)) for p in range(1, size)]
    half = block.shape[0] // 2
    along_x = swap(block, "fsdp", size, 2)
    along_y = swap(block, "fsdp", size, 4)
    front = swap(along_y[:half], "fsdp", size, 2)
    back = swap(along_x[half:], "fsdp", size, 4)
    mine = [(0, 0, block), (2, 0, along_x), (4, 0, along_y), (6, 0, front), (6, half, back)]
    return mine + [(p + 1, row, swap(part, "fsdp", size, 1)) for p, row, part in mine]


def plane_reduce(keep, send, size):
    if size != 8:
        total = keep[0].astype(F32)
        for p in range(1, size):
            block = keep[p // 2] if p % 2 == 0 else send[p // 2]
            total = total + swap(block, "fsdp", size, p).astype(F32)
        return total
    got = swap(send, "fsdp", size, 1)
    half = keep.shape[1] // 2

    def both(q, rows):
        return keep[q, rows].astype(F32) + got[q, rows].astype(F32)

    front, back = slice(0, half), slice(half, None)
    front_got = swap(
        jnp.stack([both(1, front), both(3, front)]).astype(BF16), "fsdp", size, 2
    )
    back_got = swap(jnp.stack([both(2, back), both(3, back)]).astype(BF16), "fsdp", size, 4)
    front_last = swap((both(2, front) + front_got[1].astype(F32)).astype(BF16), "fsdp", size, 4)
    back_last = swap((both(1, back) + back_got[1].astype(F32)).astype(BF16), "fsdp", size, 2)
    front_sum = both(0, front) + front_got[0].astype(F32) + front_last.astype(F32)
    back_sum = both(0, back) + back_got[0].astype(F32) + back_last.astype(F32)
    return jnp.concatenate([front_sum, back_sum], axis=0)


def start_fetch(pieces, refs, place, sems):
    copies = []
    for k, (index, row, part) in enumerate(pieces):
        copy = pltpu.make_async_copy(refs[k], place(index, row, part.shape[0]), sems.at[k])
        copy.start()
        copies.append(copy)
    return copies


def attend_forward(pos, tokens, cosine, sine, pieces, nf, nt):
    length = tokens.shape[0]
    block = D // nf
    rows = length // nt
    columns = pieces[0][2].shape[1]
    width = (columns - SIDE) // 4
    heads = width // HD
    count = len(pieces)

    def kernel(pos_ref, x_ref, cos_ref, sin_ref, *refs):
        piece_refs, refs = refs[:count], refs[count:]
        n1_ref, qk_ref, rot_ref, v_ref, prob_ref, att_ref, side_ref, gain_ref, head_gain_ref = refs[:9]
        part_refs, (w, out, sems) = refs[9 : 9 + nt], refs[9 + nt :]
        f, t = pos_ref[0], pos_ref[1]

        def place(index, row, number):
            start = pl.multiple_of((f ^ index) * block + row, 16)
            return w.at[pl.ds(start, number), :]

        copies = start_fetch(pieces, piece_refs, place, sems)
        x = x_ref[...].astype(F32)
        normed = x * rms_inverse(x)
        for copy in copies:
            copy.wait()
        side_ref[...] = w[:, 4 * width :]
        turned = jnp.transpose(w[:, 4 * width :].astype(F32))
        gain_ref[...] = turned[EXPERTS : EXPERTS + 8]
        head_rows = turned[EXPERTS : EXPERTS + 8, :block]
        for p in range(1, nf):
            head_rows = head_rows + turned[EXPERTS : EXPERTS + 8, p * block : (p + 1) * block]
        head_gains = head_rows[:, :HD]
        head_gain_ref[...] = head_gains
        n1 = (normed * turned[EXPERTS : EXPERTS + 1]).astype(BF16)
        n1_ref[...] = n1
        raw = dot(n1, w[:, : 3 * width])
        qk_ref[...] = raw[:, : 2 * width]
        v_ref[...] = raw[:, 2 * width :].astype(BF16)
        cos, sin = cos_ref[...], sin_ref[...]
        for h in range(heads):
            span = slice(h * HD, (h + 1) * HD)
            turned_rows = []
            for which in range(2):
                values = raw[:, which * width + h * HD : which * width + (h + 1) * HD]
                scaled = values * rms_inverse(values) * head_gains[2 + which : 3 + which]
                low = (scaled * cos + half_turn(scaled) * sin).astype(BF16)
                rot_ref[:, which * width + h * HD : which * width + (h + 1) * HD] = low
                turned_rows.append(low)
            scores = dot_nt(turned_rows[0], turned_rows[1]) * (HD**-0.5)
            shifted = jnp.exp(scores - jnp.max(scores, axis=-1, keepdims=True))
            probs = shifted / jnp.sum(shifted, axis=-1, keepdims=True)
            prob_ref[h] = probs
            att_ref[:, span] = dot(probs.astype(BF16), v_ref[:, span]).astype(BF16)
        out[...] = dot_nt(att_ref[...], w[:, 3 * width : 4 * width]).astype(BF16)
        for d in range(nt):
            start = pl.multiple_of((t ^ d) * rows, 16)
            part_refs[d][...] = out[pl.ds(start, rows), :]

    results = pl.pallas_call(
        kernel,
        out_shape=[
            shape((length, D), BF16),
            shape((length, 2 * width), F32),
            shape((length, 2 * width), BF16),
            shape((length, width), BF16),
            shape((heads, length, length), F32),
            shape((length, width), BF16),
            shape((D, SIDE), BF16),
            shape((8, D), F32),
            shape((8, HD), F32),
        ]
        + [shape((rows, D), BF16)] * nt,
        in_specs=[SMEM, VMEM, VMEM, VMEM] + [HBM] * count,
        out_specs=[VMEM] * (9 + nt),
        scratch_shapes=[
            pltpu.VMEM((D, columns), BF16),
            pltpu.VMEM((length, D), BF16),
            pltpu.SemaphoreType.DMA((count,)),
        ],
        compiler_params=params(),
        cost_estimate=cost(2 * length * D * 4 * width, 2 * D * columns),
        name="attend_forward",
    )(pos, tokens, cosine, sine, *[part for _, _, part in pieces])
    return results[:9], results[9:]


def attend_backward(pos, grad_rows, pieces, saved, tokens, cosine, sine, nf, nt):
    _, qk, rot, values, probs, _, _, gains, head_gains = saved
    length = tokens.shape[0]
    block = D // nf
    rows = length // nt
    columns = pieces[0][2].shape[1]
    width = (columns - SIDE) // 4
    heads = width // HD
    count = len(pieces)

    def kernel(pos_ref, x_ref, cos_ref, sin_ref, qk_ref, rot_ref, v_ref, prob_ref, gain_ref, head_gain_ref, *refs):
        grad_refs, refs = refs[:nt], refs[nt:]
        piece_refs, refs = refs[:count], refs[count:]
        dqkv_ref, db_ref, row_ref, head_row_ref = refs[:4]
        part_refs, (w, out, sems) = refs[4 : 4 + nt], refs[4 + nt :]
        f, t = pos_ref[0], pos_ref[1]

        def place(index, row, number):
            start = pl.multiple_of((f ^ index) * block + row, 16)
            return w.at[pl.ds(start, number), :]

        copies = start_fetch(pieces, piece_refs, place, sems)
        for d in range(nt):
            start = pl.multiple_of((t ^ d) * rows, 16)
            db_ref[pl.ds(start, rows), :] = grad_refs[d][...]
        for copy in copies:
            copy.wait()
        cos, sin = cos_ref[...], sin_ref[...]
        head_gains = head_gain_ref[...]
        grad_att = dot(db_ref[...], w[:, 3 * width : 4 * width]).astype(BF16)
        gain_rows = [jnp.zeros((1, HD), F32), jnp.zeros((1, HD), F32)]
        for h in range(heads):
            span = slice(h * HD, (h + 1) * HD)
            query_low = rot_ref[:, span]
            key_low = rot_ref[:, width + h * HD : width + (h + 1) * HD]
            grad_out = grad_att[:, span]
            exact = prob_ref[h]
            grad_probs = dot_nt(grad_out, v_ref[:, span])
            row_terms = jnp.sum(exact * grad_probs, axis=-1, keepdims=True)
            grad_scores = (exact * (grad_probs - row_terms)).astype(BF16)
            dqkv_ref[:, 2 * width + h * HD : 2 * width + (h + 1) * HD] = dot_tn(
                exact.astype(BF16), grad_out
            ).astype(BF16)
            both = (dot(grad_scores, key_low), dot_tn(grad_scores, query_low))
            for which in range(2):
                span_w = slice(which * width + h * HD, which * width + (h + 1) * HD)
                grads = both[which] * (HD**-0.5)
                grads = grads * cos - half_turn(grads) * sin
                raw = qk_ref[:, span_w]
                inverse = rms_inverse(raw)
                gain_rows[which] = gain_rows[which] + jnp.sum(
                    grads * raw * inverse, axis=0, keepdims=True
                )
                dqkv_ref[:, span_w] = norm_backward(
                    raw, inverse, head_gains[2 + which : 3 + which], grads
                ).astype(BF16)
        head_row_ref[...] = jnp.concatenate(gain_rows + [jnp.zeros((6, HD), F32)], axis=0)
        grad_normed = dot_nt(dqkv_ref[...], w[:, : 3 * width])
        out[...] = grad_normed.astype(BF16)
        x = x_ref[...].astype(F32)
        row = jnp.sum(grad_normed * (x * rms_inverse(x)), axis=0, keepdims=True)
        row_ref[...] = jnp.broadcast_to(row, (8, D))
        for d in range(nt):
            start = pl.multiple_of((t ^ d) * rows, 16)
            part_refs[d][...] = out[pl.ds(start, rows), :]

    results = pl.pallas_call(
        kernel,
        out_shape=[
            shape((length, 3 * width), BF16),
            shape((length, D), BF16),
            shape((8, D), F32),
            shape((8, HD), F32),
        ]
        + [shape((rows, D), BF16)] * nt,
        in_specs=[SMEM] + [VMEM] * (9 + nt) + [HBM] * count,
        out_specs=[VMEM] * (4 + nt),
        scratch_shapes=[
            pltpu.VMEM((D, columns), BF16),
            pltpu.VMEM((length, D), BF16),
            pltpu.SemaphoreType.DMA((count,)),
        ],
        compiler_params=params(),
        cost_estimate=cost(2 * length * D * 4 * width, 2 * D * columns),
        name="attend_backward",
    )(
        pos, tokens, cosine, sine, qk, rot, values, probs, gains, head_gains,
        *grad_rows, *[part for _, _, part in pieces],
    )
    return results[:4], results[4:]


def projection_gradients(pos, normed, dqkv, grad_branch, attended, side_grads, attn_row, head_rows, group, nf):
    length = normed.shape[0]
    block = D // nf
    width = attended.shape[1]
    columns = 4 * width + SIDE

    def kernel(pos_ref, n1_ref, dqkv_ref, db_ref, att_ref, side_ref, row_ref, head_ref, keep_ref, send_ref):
        f = pos_ref[0]
        lane = lanes((block, SIDE))
        sub = lax.broadcasted_iota(jnp.int32, (block, SIDE), 0)
        for p in range(nf):
            owner = f ^ p
            start = pl.multiple_of(owner * block, 128)
            to = (keep_ref if p % 2 == 0 else send_ref).at[p // 2]
            to[:, : 3 * width] = dot_tn(n1_ref[:, pl.ds(start, block)], dqkv_ref[...]).astype(BF16)
            to[:, 3 * width : 4 * width] = dot_tn(
                db_ref[:, pl.ds(start, block)], att_ref[...]
            ).astype(BF16)
            side = side_ref[pl.ds(start, block), :]
            gain = jnp.transpose(jnp.broadcast_to(row_ref[0:1, pl.ds(start, block)], (SIDE, block)))
            side = jnp.where(lane == EXPERTS + 1, gain, side)
            mine = (lane == owner * group + sub) & (sub < group)
            for which in range(2):
                spread = jnp.where(mine, head_ref[which : which + 1, :], 0.0)
                side = jnp.where(
                    lane == EXPERTS + 2 + which, jnp.sum(spread, axis=1, keepdims=True), side
                )
            to[:, 4 * width :] = side.astype(BF16)

    return pl.pallas_call(
        kernel,
        out_shape=[shape((nf // 2, block, columns), BF16)] * 2,
        in_specs=[SMEM] + [VMEM] * 7,
        out_specs=[VMEM] * 2,
        compiler_params=params(),
        cost_estimate=cost(2 * length * D * 4 * width, 2 * D * columns),
        name="projection_gradients",
    )(pos, normed, dqkv, grad_branch, attended, side_grads, attn_row, head_rows)


def norm_and_route(pos, tokens, routes, parts, gains, side, nt):
    rows = tokens.shape[0] // nt
    top = routes.shape[1]

    def kernel(pos_ref, x_ref, route_ref, gain_ref, side_ref, *refs):
        part_refs, (h_ref, next_ref, gate_ref) = refs[:nt], refs[nt:]
        h = x_ref[...].astype(F32)
        for ref in part_refs:
            h = h + ref[...].astype(F32)
        h_ref[...] = h
        n2 = (h * rms_inverse(h) * gain_ref[1:2]).astype(BF16)
        next_ref[:, :D] = n2
        logits = dot(n2, side_ref[...])
        lane = lanes((rows, SIDE))
        chosen = route_ref[:, 0:1] == lane
        for j in range(1, top):
            chosen = chosen | (route_ref[:, j : j + 1] == lane)
        highest = jnp.max(jnp.where(chosen, logits, -jnp.inf), axis=-1, keepdims=True)
        shifted = jnp.where(chosen, jnp.exp(jnp.where(chosen, logits - highest, 0.0)), 0.0)
        gates = shifted / jnp.sum(shifted, axis=-1, keepdims=True)
        gate_ref[...] = gates
        first = gates.astype(BF16).astype(F32)
        rest = (gates - first).astype(BF16).astype(F32)
        next_ref[:, D:] = (first + pltpu.roll(rest, EXPERTS, 1)).astype(BF16)

    whole = lambda i, pos: (0, 0)
    mine = lambda i, pos: (pos[1], 0)
    return pl.pallas_call(
        kernel,
        out_shape=[shape((rows, D), F32), shape((rows, D + SIDE), BF16), shape((rows, SIDE), F32)],
        grid_spec=pltpu.PrefetchScalarGridSpec(
            num_scalar_prefetch=1,
            grid=(1,),
            in_specs=[
                pl.BlockSpec((rows, D), mine),
                pl.BlockSpec((rows, top), mine),
                pl.BlockSpec((8, D), whole),
                pl.BlockSpec((D, SIDE), whole),
            ]
            + [pl.BlockSpec((rows, D), whole)] * nt,
            out_specs=[
                pl.BlockSpec((rows, D), whole),
                pl.BlockSpec((rows, D + SIDE), whole),
                pl.BlockSpec((rows, SIDE), whole),
            ],
        ),
        compiler_params=params(),
        cost_estimate=cost(2 * rows * D * SIDE, 8 * rows * D),
        name="norm_and_route",
    )(pos, tokens, routes, gains, side, *parts)


def norm_back(pos, cotangent, parts, h, gates, normed, gains, side, nt):
    rows = h.shape[0]

    def kernel(pos_ref, cot_ref, h_ref, gate_ref, n2_ref, gain_ref, side_ref, *refs):
        part_refs, (dh_ref, db_ref, small_ref) = refs[:nt], refs[nt:]
        total = part_refs[0][...].astype(F32)
        for ref in part_refs[1:]:
            total = total + ref[...].astype(F32)
        pair = total[:, D:]
        pair = pair + pltpu.roll(pair, EXPERTS, 1)
        gates = gate_ref[...]
        grads = gates * (pair - jnp.sum(gates * pair, axis=-1, keepdims=True))
        low = grads.astype(BF16)
        dn2 = total[:, :D] + dot_nt(low, side_ref[...])
        h = h_ref[...]
        inverse = rms_inverse(h)
        gain_row = jnp.sum(dn2 * h * inverse, axis=0, keepdims=True)
        small = dot_tn(n2_ref[:, :D], low)
        column = jnp.transpose(jnp.broadcast_to(gain_row, (SIDE, D)))
        small_ref[...] = jnp.where(lanes((D, SIDE)) == EXPERTS, column, small)
        dh = cot_ref[...].astype(F32) + norm_backward(h, inverse, gain_ref[1:2], dn2)
        dh_ref[...] = dh
        db_ref[...] = dh.astype(BF16)

    whole = lambda i, pos: (0, 0)
    mine = lambda i, pos: (pos[1], 0)
    return pl.pallas_call(
        kernel,
        out_shape=[shape((rows, D), F32), shape((rows, D), BF16), shape((D, SIDE), F32)],
        grid_spec=pltpu.PrefetchScalarGridSpec(
            num_scalar_prefetch=1,
            grid=(1,),
            in_specs=[
                pl.BlockSpec((rows, D), mine),
                pl.BlockSpec((rows, D), whole),
                pl.BlockSpec((rows, SIDE), whole),
                pl.BlockSpec((rows, D + SIDE), whole),
                pl.BlockSpec((8, D), whole),
                pl.BlockSpec((D, SIDE), whole),
            ]
            + [pl.BlockSpec((rows, D + SIDE), whole)] * nt,
            out_specs=[
                pl.BlockSpec((rows, D), whole),
                pl.BlockSpec((rows, D), whole),
                pl.BlockSpec((D, SIDE), whole),
            ],
        ),
        compiler_params=params(),
        cost_estimate=cost(4 * rows * D * SIDE, 8 * rows * D),
        name="norm_back",
    )(pos, cotangent, h, gates, normed, gains, side, *parts)


def input_gradient(pos, tokens, parts, dh, gains, nt):
    rows = dh.shape[0]

    def kernel(pos_ref, x_ref, dh_ref, gain_ref, *refs):
        part_refs, out_ref = refs[:nt], refs[nt]
        total = part_refs[0][...].astype(F32)
        for ref in part_refs[1:]:
            total = total + ref[...].astype(F32)
        x = x_ref[...].astype(F32)
        out_ref[...] = (
            dh_ref[...] + norm_backward(x, rms_inverse(x), gain_ref[0:1], total)
        ).astype(BF16)

    whole = lambda i, pos: (0, 0)
    return pl.pallas_call(
        kernel,
        out_shape=shape((rows, D), BF16),
        grid_spec=pltpu.PrefetchScalarGridSpec(
            num_scalar_prefetch=1,
            grid=(1,),
            in_specs=[
                pl.BlockSpec((rows, D), lambda i, pos: (pos[1], 0)),
                pl.BlockSpec((rows, D), whole),
                pl.BlockSpec((8, D), whole),
            ]
            + [pl.BlockSpec((rows, D), whole)] * nt,
            out_specs=pl.BlockSpec((rows, D), whole),
        ),
        compiler_params=params(),
        name="input_gradient",
    )(pos, tokens, dh, gains, *parts)


def place_rows(pos, parts):
    rows, features = parts[0].shape
    nt = len(parts)

    def kernel(pos_ref, *refs):
        for d in range(nt):
            start = pl.multiple_of((pos_ref[1] ^ d) * rows, 16)
            refs[nt][pl.ds(start, rows), :] = refs[d][...]

    return pl.pallas_call(
        kernel,
        out_shape=shape((rows * nt, features), parts[0].dtype),
        in_specs=[SMEM] + [VMEM] * nt,
        out_specs=VMEM,
        compiler_params=params(),
        name="place_rows",
    )(pos, *parts)


def spread_rows(slots, source, target, pair, number, cut):
    for begin in range(0, source.shape[2], cut):
        span = slice(begin, min(begin + cut, source.shape[2]))
        two = [dot_tn(slots[2 * pair + k], source[2 * pair + k, :, span]) for k in range(2)]
        for e in range(number):
            joined = jnp.concatenate([rows[e * CAP : (e + 1) * CAP] for rows in two], axis=0)
            target(e, span, joined)


def sum_rows(slots, results, target, pair, number, total, cut):
    at = slice(pair * 2 * CAP, (pair + 1) * 2 * CAP)
    for begin in range(0, total, cut):
        span = slice(begin, min(begin + cut, total))
        blocks = [results[e, at, span].astype(F32) for e in range(number)]
        for k in range(2):
            rows = jnp.concatenate([b[k * CAP : (k + 1) * CAP] for b in blocks], axis=0)
            target[2 * pair + k, :, span] = dot(slots[2 * pair + k], rows.astype(BF16)).astype(BF16)


def route_cotangent(pos, pieces, weights, nf, top):
    number, _, _, width = weights.shape
    length = sum(part.shape[0] for index, _, part in pieces if index == 0)
    slots = number * CAP
    count = len(pieces)

    def kernel(pos_ref, w_ref, *refs):
        piece_refs, (slot_ref, rows_ref, down_ref, cot, spread, sems) = refs[:count], refs[count:]
        e = pl.program_id(0)
        f = pos_ref[0]

        @pl.when(e == 0)
        def _():
            copies = start_fetch(
                pieces, piece_refs, lambda i, row, n: cot.at[i, pl.ds(row, n), :], sems
            )
            column = lanes((length, slots))
            expert = jnp.zeros((length, slots), jnp.int32)
            for k in range(1, number):
                expert = expert + (column >= k * CAP).astype(jnp.int32)
            rank = (column - expert * CAP + 1).astype(F32)
            expert = (expert + f * number).astype(F32)
            lower = (
                lax.broadcasted_iota(jnp.int32, (length, length), 0) >= lanes((length, length))
            ).astype(F32).astype(BF16)
            for copy in copies:
                copy.wait()
            for s in range(nf):
                named = cot[s, :, D:].astype(F32)
                hit = named[:, 0:1] == expert
                for j in range(1, top):
                    hit = hit | (named[:, j : j + 1] == expert)
                hit = jnp.where(hit, 1.0, 0.0)
                so_far = dot(lower, hit.astype(BF16))
                slot_ref[s] = jnp.where((so_far == rank) & (hit > 0.0), 1.0, 0.0).astype(BF16)
            for pair in range(nf // 2):
                at = slice(pair * 2 * CAP, (pair + 1) * 2 * CAP)

                def put(k, span, rows):
                    spread[k, at, span] = rows.astype(BF16)

                spread_rows(slot_ref, cot.at[:, :, :D], put, pair, number, 512)

        rows = spread[e]
        rows_ref[0] = rows
        down_ref[0] = dot(rows, w_ref[0, 0])

    return pl.pallas_call(
        kernel,
        out_shape=[
            shape((nf, length, slots), BF16),
            shape((number, nf * CAP, D), BF16),
            shape((number, nf * CAP, width), F32),
        ],
        grid_spec=pltpu.PrefetchScalarGridSpec(
            num_scalar_prefetch=1,
            grid=(number,),
            in_specs=[pl.BlockSpec((1, 1, D, width), lambda e, pos: (e, 2, 0, 0))] + [HBM] * count,
            out_specs=[
                pl.BlockSpec((nf, length, slots), lambda e, pos: (0, 0, 0)),
                pl.BlockSpec((1, nf * CAP, D), lambda e, pos: (e, 0, 0)),
                pl.BlockSpec((1, nf * CAP, width), lambda e, pos: (e, 0, 0)),
            ],
            scratch_shapes=[
                pltpu.VMEM((nf, length, D + SIDE), BF16),
                pltpu.VMEM((number, nf * CAP, D), BF16),
                pltpu.SemaphoreType.DMA((count,)),
            ],
        ),
        compiler_params=params(),
        cost_estimate=cost(4 * slots * nf * D * 256, 8 * slots * nf * D),
        name="route_cotangent",
    )(pos, weights, *[part for _, _, part in pieces])


def run_experts(pos, pieces, slot_table, down, weights, nf):
    number, _, _, width = weights.shape
    length, slots = slot_table.shape[1:]
    filled = nf * CAP
    count = len(pieces)

    def kernel(pos_ref, slot_ref, down_ref, gate_w, up_w, *refs):
        piece_refs, refs = refs[:count], refs[count:]
        rows_ref, dg_ref, du_ref, hidden_ref, keep_ref, send_ref = refs[:6]
        wide, spread, gates, results, sems, out_sems = refs[6:]
        e = pl.program_id(0)
        f = pos_ref[0]

        @pl.when(e == 0)
        def _():
            copies = start_fetch(
                pieces, piece_refs, lambda i, row, n: wide.at[i, pl.ds(row, n), :], sems
            )
            for copy in copies:
                copy.wait()
            for pair in range(nf // 2):
                at = slice(pair * 2 * CAP, (pair + 1) * 2 * CAP)

                def put(k, span, rows):
                    if span.start < D:
                        spread[k, at, span] = rows.astype(BF16)
                    else:
                        lane = lanes((2 * CAP, SIDE))
                        own = f * number + k
                        gate = jnp.where((lane == own) | (lane == own + EXPERTS), rows, 0.0)
                        gates[k, at, :] = jnp.broadcast_to(
                            jnp.sum(gate, axis=-1, keepdims=True), (2 * CAP, SIDE)
                        )

                spread_rows(slot_ref, wide, put, pair, number, 512)

        rows = spread[e]
        rows_ref[0] = rows
        first, second = gate_w[0, 0], up_w[0, 0]
        gate_pre = dot(rows, first)
        up_pre = dot(rows, second)
        gate = gates[e][:, 0:1]
        sigma = jax.nn.sigmoid(gate_pre)
        swish = gate_pre * sigma
        hidden = (swish * up_pre).astype(BF16).astype(F32)
        hidden_ref[0] = (gate * hidden).astype(BF16)
        unscaled = down_ref[0]
        grad_hidden = gate * unscaled
        dg = (grad_hidden * up_pre * sigma * (1.0 + gate_pre * (1.0 - sigma))).astype(BF16)
        du = (grad_hidden * swish).astype(BF16)
        dg_ref[0] = dg
        du_ref[0] = du
        results[e, :, :D] = (dot_nt(dg, first) + dot_nt(du, second)).astype(BF16)
        pair_grad = jnp.sum(unscaled * hidden, axis=-1, keepdims=True)
        high = pair_grad.astype(BF16).astype(F32)
        lane = lanes((filled, SIDE))
        own = f * number + e
        results[e, :, D:] = jnp.where(
            lane == own, high, jnp.where(lane == own + EXPERTS, pair_grad - high, 0.0)
        ).astype(BF16)

        @pl.when(e == number - 1)
        def _():
            copies = []
            for pair in range(nf // 2):
                sum_rows(slot_ref, results, wide, pair, number, D + SIDE, 512)
                for k, to in enumerate((keep_ref, send_ref)):
                    index = 2 * pair + k
                    copy = pltpu.make_async_copy(wide.at[index], to.at[pair], out_sems.at[index])
                    copy.start()
                    copies.append(copy)
            for copy in copies:
                copy.wait()

    return pl.pallas_call(
        kernel,
        out_shape=[
            shape((number, filled, D), BF16),
            shape((number, filled, width), BF16),
            shape((number, filled, width), BF16),
            shape((number, filled, width), BF16),
            shape((nf // 2, length, D + SIDE), BF16),
            shape((nf // 2, length, D + SIDE), BF16),
        ],
        grid_spec=pltpu.PrefetchScalarGridSpec(
            num_scalar_prefetch=1,
            grid=(number,),
            in_specs=[
                pl.BlockSpec((nf, length, slots), lambda e, pos: (0, 0, 0)),
                pl.BlockSpec((1, filled, width), lambda e, pos: (e, 0, 0)),
                pl.BlockSpec((1, 1, D, width), lambda e, pos: (e, 0, 0, 0)),
                pl.BlockSpec((1, 1, D, width), lambda e, pos: (e, 1, 0, 0)),
            ]
            + [HBM] * count,
            out_specs=[
                pl.BlockSpec((1, filled, D), lambda e, pos: (e, 0, 0)),
                pl.BlockSpec((1, filled, width), lambda e, pos: (e, 0, 0)),
                pl.BlockSpec((1, filled, width), lambda e, pos: (e, 0, 0)),
                pl.BlockSpec((1, filled, width), lambda e, pos: (e, 0, 0)),
                HBM,
                HBM,
            ],
            scratch_shapes=[
                pltpu.VMEM((nf, length, D + SIDE), BF16),
                pltpu.VMEM((number, filled, D), BF16),
                pltpu.VMEM((number, filled, SIDE), F32),
                pltpu.VMEM((number, filled, D + SIDE), BF16),
                pltpu.SemaphoreType.DMA((count,)),
                pltpu.SemaphoreType.DMA((nf,)),
            ],
        ),
        compiler_params=params(),
        cost_estimate=cost(12 * slots * nf * D * 256, 8 * slots * nf * D),
        name="run_experts",
    )(pos, slot_table, down, weights, weights, *[part for _, _, part in pieces])


def expert_outputs(slot_table, hidden, weights):
    number, filled, width = hidden.shape
    nf, length, slots = slot_table.shape

    def kernel(slot_ref, hidden_ref, w_ref, keep_ref, send_ref, results, out, sems):
        e = pl.program_id(0)
        results[e] = dot_nt(hidden_ref[0], w_ref[0, 0]).astype(BF16)

        @pl.when(e == number - 1)
        def _():
            copies = []
            for pair in range(nf // 2):
                sum_rows(slot_ref, results, out, pair, number, D, 512)
                for k, to in enumerate((keep_ref, send_ref)):
                    index = 2 * pair + k
                    copy = pltpu.make_async_copy(out.at[index], to.at[pair], sems.at[index])
                    copy.start()
                    copies.append(copy)
            for copy in copies:
                copy.wait()

    return pl.pallas_call(
        kernel,
        out_shape=[shape((nf // 2, length, D), BF16)] * 2,
        grid=(number,),
        in_specs=[
            pl.BlockSpec((nf, length, slots), lambda e: (0, 0, 0)),
            pl.BlockSpec((1, filled, width), lambda e: (e, 0, 0)),
            pl.BlockSpec((1, 1, D, width), lambda e: (e, 2, 0, 0)),
        ],
        out_specs=[HBM, HBM],
        scratch_shapes=[
            pltpu.VMEM((number, filled, D), BF16),
            pltpu.VMEM((nf, length, D), BF16),
            pltpu.SemaphoreType.DMA((nf,)),
        ],
        compiler_params=params(),
        cost_estimate=cost(4 * slots * nf * D * 256, 8 * slots * nf * D),
        name="expert_outputs",
    )(slot_table, hidden, weights)


def expert_gradients(rows, grad_rows, dg, du, hidden):
    number, filled, width = dg.shape

    def kernel(rows_ref, grad_ref, dg_ref, du_ref, hidden_ref, out_ref):
        rows = rows_ref[0]
        out_ref[0, 0] = dot_tn(rows, dg_ref[0])
        out_ref[0, 1] = dot_tn(rows, du_ref[0])
        out_ref[0, 2] = dot_tn(grad_ref[0], hidden_ref[0])

    tall = pl.BlockSpec((1, filled, D), lambda e: (e, 0, 0))
    thin = pl.BlockSpec((1, filled, width), lambda e: (e, 0, 0))
    return pl.pallas_call(
        kernel,
        out_shape=shape((number, 3, D, width), F32),
        grid=(number,),
        in_specs=[tall, tall, thin, thin, thin],
        out_specs=pl.BlockSpec((1, 3, D, width), lambda e: (e, 0, 0, 0)),
        compiler_params=params(),
        cost_estimate=cost(6 * number * filled * D * width, 12 * number * D * width),
        name="expert_gradients",
    )(rows, grad_rows, dg, du, hidden)


def on_device(
    nf,
    nt,
    tokens,
    cotangent,
    routes,
    w_query,
    w_key,
    w_value,
    w_output,
    w_router,
    attn_gain,
    ffn_gain,
    query_gain,
    key_gain,
    expert_weights,
):
    length = tokens.shape[0]
    rows = length // nt
    block = D // nf
    group = query_gain.shape[0]
    top = routes.shape[1]
    f = lax.axis_index("fsdp").astype(jnp.int32)
    t = lax.axis_index("tensor").astype(jnp.int32)
    pos = jnp.stack([f, t])

    def placed(gain):
        return lax.dynamic_update_slice(jnp.zeros((block,), BF16), gain, (f * group,))[:, None]

    packed = jnp.concatenate(
        [
            w_query,
            w_key,
            w_value,
            w_output,
            w_router,
            attn_gain[:, None],
            ffn_gain[:, None],
            placed(query_gain),
            placed(key_gain),
            jnp.zeros((block, SIDE - EXPERTS - 4), BF16),
        ],
        axis=1,
    )
    weight_pieces = plane_gather(packed, nf)

    wide_cot = jnp.concatenate(
        [cotangent, routes.astype(BF16), jnp.zeros((length, SIDE - top), BF16)], axis=1
    )
    wide_cot = jnp.concatenate(
        [lax.dynamic_slice_in_dim(wide_cot, (t ^ d) * rows, rows, 0) for d in range(nt)], axis=0
    )
    cot_pieces = plane_gather(wide_cot, nf)

    position = jnp.arange(length, dtype=F32)[:, None]
    inverse = ROPE_BASE ** (-jnp.arange(HD // 2, dtype=F32) / (HD // 2))
    angles = position * inverse[None, :]
    cosine = jnp.concatenate([jnp.cos(angles)] * 2, axis=1)
    sine = jnp.concatenate([-jnp.sin(angles), jnp.sin(angles)], axis=1)

    saved, parts = attend_forward(pos, tokens, cosine, sine, weight_pieces, nf, nt)
    normed_one, _, _, _, _, attended, side, gains, _ = saved
    parts = [parts[0]] + [swap(parts[d], "tensor", nt, d) for d in range(1, nt)]
    h, normed_two, gates = norm_and_route(pos, tokens, routes, parts, gains, side, nt)

    others = [swap(normed_two, "tensor", nt, d) for d in range(1, nt)]
    n2_pieces = plane_gather(normed_two, nf) + [
        (index, row + rows, part)
        for index, row, part in plane_gather(jnp.concatenate(others, axis=0), nf)
    ]
    slot_table, cot_rows, down = route_cotangent(pos, cot_pieces, expert_weights, nf, top)
    n2_rows, dg, du, hidden, keep, send = run_experts(
        pos, n2_pieces, slot_table, down, expert_weights, nf
    )

    def over_tensor(total):
        low = total.astype(BF16)
        return [low[:rows]] + [
            swap(low[d * rows : (d + 1) * rows], "tensor", nt, d) for d in range(1, nt)
        ]

    grad_parts = over_tensor(plane_reduce(keep, send, nf))
    grad_experts = expert_gradients(n2_rows, cot_rows, dg, du, hidden)
    out_keep, out_send = expert_outputs(slot_table, hidden, expert_weights)
    dh, db, side_grads = norm_back(
        pos, cotangent, grad_parts, h, gates, normed_two, gains, side, nt
    )
    db_parts = [db] + [swap(db, "tensor", nt, d) for d in range(1, nt)]

    moe_parts = over_tensor(plane_reduce(out_keep, out_send, nf))
    layer_rows = h
    for part in moe_parts:
        layer_rows = layer_rows + part.astype(F32)
    layer_out = lax.all_gather(layer_rows.astype(BF16), "tensor", axis=0, tiled=True)

    (dqkv, grad_branch, attn_row, head_rows), parts = attend_backward(
        pos, db_parts, weight_pieces, saved, tokens, cosine, sine, nf, nt
    )
    parts = [parts[0]] + [swap(parts[d], "tensor", nt, d) for d in range(1, nt)]
    keep, send = projection_gradients(
        pos, normed_one, dqkv, grad_branch, attended, side_grads, attn_row, head_rows, group, nf
    )
    weight_grads = plane_reduce(keep, send, nf)
    token_rows = input_gradient(pos, tokens, parts, dh, gains, nt)
    grad_tokens = place_rows(
        pos, [token_rows] + [swap(token_rows, "tensor", nt, d) for d in range(1, nt)]
    )
    width = attended.shape[1]
    small = lax.psum(weight_grads[:, 4 * width :], "tensor")
    return (
        layer_out,
        grad_tokens,
        weight_grads[:, :width],
        weight_grads[:, width : 2 * width],
        weight_grads[:, 2 * width : 3 * width],
        weight_grads[:, 3 * width : 4 * width],
        small[:, :EXPERTS],
        small[:, EXPERTS + 1],
        small[:, EXPERTS],
        small[:group, EXPERTS + 2],
        small[:group, EXPERTS + 3],
        grad_experts,
    )


def solution(mesh):
    nf, nt = mesh.shape["fsdp"], mesh.shape["tensor"]
    rows, both, line = P("fsdp", None), P("fsdp", "tensor"), P("fsdp")
    experts = P("fsdp", None, None, "tensor")
    return jax.shard_map(
        functools.partial(on_device, nf, nt),
        mesh=mesh,
        in_specs=(rows, rows, rows, both, both, both, both, rows, line, line, line, line, experts),
        out_specs=(rows, rows, both, both, both, both, rows, line, line, line, line, experts),
        check_vma=False,
    )
```

```python
import functools

import jax
import jax.numpy as jnp
from jax import lax
from jax.experimental import pallas as pl
from jax.experimental.pallas import tpu as pltpu
from jax.sharding import PartitionSpec as P

D = 2048
HD = 128
EXPERTS = 64
CAP = 40
SIDE = 128
EPSILON = 1e-06
ROPE_BASE = 10000.0

F32 = jnp.float32
BF16 = jnp.bfloat16
VMEM = pl.BlockSpec(memory_space=pltpu.VMEM)
SMEM = pl.BlockSpec(memory_space=pltpu.SMEM)
HBM = pl.BlockSpec(memory_space=pl.ANY)
VMEM_BYTES = 60 * 1024 * 1024


def shape(dims, dtype):
    return jax.ShapeDtypeStruct(tuple(dims), dtype)


def params(**more):
    return pltpu.CompilerParams(vmem_limit_bytes=VMEM_BYTES, **more)


def cost(micros):
    return pl.CostEstimate(
        flops=int(micros * 1e9), bytes_accessed=int(micros * 3e6), transcendentals=0
    )


def dot(left, right):
    return jnp.dot(left, right, preferred_element_type=F32)


def dot_nt(left, right):
    return lax.dot_general(left, right, (((1,), (1,)), ((), ())), preferred_element_type=F32)


def dot_tn(left, right):
    return lax.dot_general(left, right, (((0,), (0,)), ((), ())), preferred_element_type=F32)


def rms_inverse(values):
    return lax.rsqrt(jnp.mean(values * values, axis=-1, keepdims=True) + EPSILON)


def norm_backward(values, inverse, gain, upstream):
    scaled = gain * upstream
    return inverse * scaled - values * (inverse * inverse * inverse) * jnp.mean(
        values * scaled, axis=-1, keepdims=True
    )


def half_turn(values):
    return pltpu.roll(values, HD // 2, 1)


def lanes(dims):
    return lax.broadcasted_iota(jnp.int32, dims, len(dims) - 1)


def swap(block, axis, size, step):
    return lax.ppermute(block, axis, [(i, i ^ step) for i in range(size)])


def without(kernel, at, number):
    def body(*refs):
        kernel(*refs[:at], *refs[at + number :])

    return body


def through(moves, buffer, sems):
    arriving, leaving, row = [], [], 0
    for k, (source, target) in enumerate(moves):
        here = buffer.at[pl.ds(row, source.shape[0]), :]
        arriving.append(pltpu.make_async_copy(source, here, sems.at[2 * k]))
        leaving.append(pltpu.make_async_copy(here, target, sems.at[2 * k + 1]))
        arriving[-1].start()
        row += source.shape[0]
    for arrives, leaves in zip(arriving, leaving):
        arrives.wait()
        leaves.start()
    for leaves in leaving:
        leaves.wait()


def joins(groups, deps=()):
    parts = [part for group in groups for part in group]
    count = len(parts)
    features, dtype = parts[0].shape[1], parts[0].dtype
    totals = [sum(part.shape[0] for part in group) for group in groups]

    def kernel(*refs):
        out_refs, (buffer, sems) = refs[count:-2], refs[-2:]
        moves, k = [], 0
        for out_ref, group in zip(out_refs, groups):
            row = 0
            for part in group:
                moves.append((refs[k], out_ref.at[pl.ds(row, part.shape[0]), :]))
                row, k = row + part.shape[0], k + 1
        through(moves, buffer, sems)

    return pl.pallas_call(
        without(kernel, count, len(deps)),
        out_shape=[shape((total, features), dtype) for total in totals],
        in_specs=[HBM] * (count + len(deps)),
        out_specs=[HBM] * len(groups),
        scratch_shapes=[
            pltpu.VMEM((sum(totals), features), dtype),
            pltpu.SemaphoreType.DMA((2 * count,)),
        ],
        compiler_params=params(),
        cost_estimate=cost(0.1),
        name="joins",
    )(*parts, *deps)


def join(parts, deps=()):
    return joins([parts], deps)[0]


def relay(parts, deps):
    return joins([[part] for part in parts], deps)


def halves(upper_of, lower_of, deps=()):
    rows, features = upper_of.shape
    half = rows // 2

    def kernel(upper_ref, lower_ref, upper_out, lower_out, buffer, sems):
        through(
            [
                (upper_ref.at[pl.ds(0, half), :], upper_out),
                (lower_ref.at[pl.ds(half, half), :], lower_out),
            ],
            buffer,
            sems,
        )

    return pl.pallas_call(
        without(kernel, 2, len(deps)),
        out_shape=[shape((half, features), upper_of.dtype)] * 2,
        in_specs=[HBM] * (2 + len(deps)),
        out_specs=[HBM] * 2,
        scratch_shapes=[
            pltpu.VMEM((rows, features), upper_of.dtype),
            pltpu.SemaphoreType.DMA((4,)),
        ],
        compiler_params=params(),
        cost_estimate=cost(0.1),
        name="halves",
    )(upper_of, lower_of, *deps)


def gather_near(block, size):
    if size != 8:
        return [swap(block, "fsdp", size, p) for p in range(1, size)]
    return [swap(block, "fsdp", size, 2), swap(block, "fsdp", size, 4)]


def gather_rest(block, near, size, deps=()):
    rows = block.shape[0]
    if size != 8:
        return [(p, 0, part, 0, rows) for p, part in enumerate([block] + near)]
    half = rows // 2
    upper, lower = halves(near[1], near[0], deps)
    front = swap(upper, "fsdp", size, 2)
    back = swap(lower, "fsdp", size, 4)
    pieces = []
    for k, part in enumerate([block] + near):
        pieces.append((2 * k, 0, part, 0, rows))
        pieces.append((2 * k + 1, 0, swap(part, "fsdp", size, 1), 0, rows))
    for row, part in ((0, front), (half, back)):
        pieces.append((6, row, part, 0, half))
        pieces.append((7, row, swap(part, "fsdp", size, 1), 0, half))
    return pieces


def gather_two(blocks, near, size, sources=None):
    pieces = []
    start = 0
    sources = sources or [near[0][1], near[1][0]]
    for block, (along_x, along_y), source, step in zip(blocks, near, sources, (2, 4)):
        rows = block.shape[0]
        last = swap(source, "fsdp", size, step)
        for index, part in ((0, block), (2, along_x), (4, along_y), (6, last)):
            pieces.append((index, start, part, 0, rows))
            pieces.append((index + 1, start, swap(part, "fsdp", size, 1), 0, rows))
        start += rows
    return pieces


def arrays_of(pieces):
    found = []
    for _, _, part, _, _ in pieces:
        if not any(part is other for other in found):
            found.append(part)
    return found


def start_fetch(pieces, refs, place, sems, own=None):
    arrays = arrays_of(pieces)
    copies = []
    for k, (index, row, part, at, rows) in enumerate(pieces):
        ref = next(ref for other, ref in zip(arrays, refs) if other is part)
        if at is None:
            at = pl.multiple_of((own ^ index) * rows, 16)
        copy = pltpu.make_async_copy(
            ref.at[pl.ds(at, rows), :], place(index, row, rows), sems.at[k]
        )
        copy.start()
        copies.append(copy)
    return copies


def pair_sums(keep, got, deps=()):
    _, rows, columns = keep.shape
    half = rows // 2

    def kernel(keep_x, got_x, keep_y, got_y, out_x, out_y):
        out_x[...] = (keep_x[...].astype(F32) + got_x[...].astype(F32)).astype(BF16)
        out_y[...] = (keep_y[...].astype(F32) + got_y[...].astype(F32)).astype(BF16)

    block = (1, half, columns)
    along_x = pl.BlockSpec(block, lambda j: (2 * j + 1, 0, 0))
    along_y = pl.BlockSpec(block, lambda j: (2 + j, 1, 0))
    return pl.pallas_call(
        without(kernel, 4, len(deps)),
        out_shape=[shape((2, half, columns), BF16)] * 2,
        grid=(2,),
        in_specs=[along_x, along_x, along_y, along_y] + [HBM] * len(deps),
        out_specs=[pl.BlockSpec(block, lambda j: (j, 0, 0))] * 2,
        compiler_params=params(),
        cost_estimate=cost(0.1),
        name="pair_sums",
    )(keep, got, keep, got, *deps)


def next_sums(keep, got, from_x, from_y, deps, micros):
    _, rows, columns = keep.shape
    half = rows // 2
    part = half // 2

    def kernel(keep_x, got_x, new_x, keep_y, got_y, new_y, out_x, out_y):
        out_x[...] = (
            keep_x[0].astype(F32) + got_x[0].astype(F32) + new_x[0].astype(F32)
        ).astype(BF16)
        out_y[...] = (
            keep_y[0].astype(F32) + got_y[0].astype(F32) + new_y[0].astype(F32)
        ).astype(BF16)

    block = (1, part, columns)
    upper = pl.BlockSpec(block, lambda j: (2, j, 0))
    lower = pl.BlockSpec(block, lambda j: (1, j + 2, 0))
    new = pl.BlockSpec(block, lambda j: (1, j, 0))
    return pl.pallas_call(
        without(kernel, 6, len(deps)),
        out_shape=[shape((half, columns), BF16)] * 2,
        grid=(2,),
        in_specs=[upper, upper, new, lower, lower, new] + [HBM] * len(deps),
        out_specs=[pl.BlockSpec((part, columns), lambda j: (j, 0))] * 2,
        compiler_params=params(),
        cost_estimate=cost(micros),
        name="next_sums",
    )(keep, got, from_x, keep, got, from_y, *deps)


def last_sums(keep, got, from_x, from_y, last_x, last_y, count, deps=()):
    _, rows, columns = keep.shape
    half = rows // 2
    part = rows // count
    each = half // part

    def kernel(keep_x, got_x, new_x, end_x, keep_y, got_y, new_y, end_y, *out_refs):
        for k in range(count):
            refs = (keep_x, got_x, new_x, end_x) if k < each else (keep_y, got_y, new_y, end_y)
            span = slice((k % each) * part, (k % each + 1) * part)
            total = refs[0][0, span].astype(F32)
            for ref in refs[1:3]:
                total = total + ref[0, span].astype(F32)
            out_refs[k][...] = (total + refs[3][span].astype(F32)).astype(BF16)

    block = (1, half, columns)
    first = pl.BlockSpec(block, lambda j: (0, 0, 0))
    second = pl.BlockSpec(block, lambda j: (0, 1, 0))
    end = pl.BlockSpec((half, columns), lambda j: (0, 0))
    return pl.pallas_call(
        without(kernel, 8, len(deps)),
        out_shape=[shape((part, columns), BF16)] * count,
        grid=(1,),
        in_specs=[first, first, first, end, second, second, first, end] + [HBM] * len(deps),
        out_specs=[pl.BlockSpec((part, columns), lambda j: (0, 0))] * count,
        compiler_params=params(),
        cost_estimate=cost(20),
        name="last_sums",
    )(keep, got, from_x, last_x, keep, got, from_y, last_y, *deps)


class Reduce:
    def __init__(self, keep, send, size):
        self.keep, self.send, self.size = keep, send, size
        if size == 8:
            self.got = swap(send, "fsdp", size, 1)

    def first(self, deps=()):
        if self.size != 8:
            return []
        self.pair = pair_sums(self.keep, self.got, deps)
        self.from_x = swap(self.pair[0], "fsdp", self.size, 2)
        self.from_y = swap(self.pair[1], "fsdp", self.size, 4)
        return list(self.pair[:1])

    def second(self, deps=(), micros=0.1):
        if self.size != 8:
            return []
        sums = next_sums(self.keep, self.got, self.from_x, self.from_y, deps, micros)
        self.last_x = swap(sums[0], "fsdp", self.size, 4)
        self.last_y = swap(sums[1], "fsdp", self.size, 2)
        return list(sums[:1])

    def total(self):
        if self.size != 8:
            total = self.keep[0].astype(F32)
            for p in range(1, self.size):
                block = self.keep[p // 2] if p % 2 == 0 else self.send[p // 2]
                total = total + swap(block, "fsdp", self.size, p).astype(F32)
            return total
        half = self.keep.shape[1] // 2
        sums = []
        for rows, new, last in (
            (slice(0, half), self.from_x, self.last_x),
            (slice(half, None), self.from_y, self.last_y),
        ):
            sums.append(
                self.keep[0, rows].astype(F32)
                + self.got[0, rows].astype(F32)
                + new[0].astype(F32)
                + last.astype(F32)
            )
        return jnp.concatenate(sums, axis=0)

    def rows(self, count, deps=()):
        if self.size != 8:
            return jnp.split(self.total().astype(BF16), count, axis=0)
        return last_sums(
            self.keep, self.got, self.from_x, self.from_y, self.last_x, self.last_y, count, deps
        )


def attend_forward(pos, tokens, cosine, sine, pieces, nf, nt, deps=()):
    length = tokens.shape[0]
    block = D // nf
    rows = length // nt
    columns = pieces[0][2].shape[1]
    width = (columns - SIDE) // 4
    heads = width // HD
    arrays = arrays_of(pieces)
    count = len(arrays)

    def kernel(pos_ref, x_ref, cos_ref, sin_ref, *refs):
        piece_refs, refs = refs[:count], refs[count:]
        n1_ref, qk_ref, rot_ref, v_ref, prob_ref, att_ref, side_ref, gain_ref, head_gain_ref = refs[:9]
        part_refs, (w, out, sems) = refs[9 : 9 + nt], refs[9 + nt :]
        f, t = pos_ref[0], pos_ref[1]

        def place(index, row, number):
            start = pl.multiple_of((f ^ index) * block + row, 16)
            return w.at[pl.ds(start, number), :]

        copies = start_fetch(pieces, piece_refs, place, sems)
        x = x_ref[...].astype(F32)
        normed = x * rms_inverse(x)
        for copy in copies:
            copy.wait()
        side_ref[...] = w[:, 4 * width :]
        turned = jnp.transpose(w[:, 4 * width :].astype(F32))
        gain_ref[...] = turned[EXPERTS : EXPERTS + 8]
        head_rows = turned[EXPERTS : EXPERTS + 8, :block]
        for p in range(1, nf):
            head_rows = head_rows + turned[EXPERTS : EXPERTS + 8, p * block : (p + 1) * block]
        head_gains = head_rows[:, :HD]
        head_gain_ref[...] = head_gains
        n1 = (normed * turned[EXPERTS : EXPERTS + 1]).astype(BF16)
        n1_ref[...] = n1
        raw = dot(n1, w[:, : 3 * width])
        qk_ref[...] = raw[:, : 2 * width]
        v_ref[...] = raw[:, 2 * width :].astype(BF16)
        cos, sin = cos_ref[...], sin_ref[...]
        for h in range(heads):
            span = slice(h * HD, (h + 1) * HD)
            turned_rows = []
            for which in range(2):
                values = raw[:, which * width + h * HD : which * width + (h + 1) * HD]
                scaled = values * rms_inverse(values) * head_gains[2 + which : 3 + which]
                low = (scaled * cos + half_turn(scaled) * sin).astype(BF16)
                rot_ref[:, which * width + h * HD : which * width + (h + 1) * HD] = low
                turned_rows.append(low)
            scores = dot_nt(turned_rows[0], turned_rows[1]) * (HD**-0.5)
            shifted = jnp.exp(scores - jnp.max(scores, axis=-1, keepdims=True))
            probs = shifted / jnp.sum(shifted, axis=-1, keepdims=True)
            prob_ref[h] = probs
            att_ref[:, span] = dot(probs.astype(BF16), v_ref[:, span]).astype(BF16)
        out[...] = dot_nt(att_ref[...], w[:, 3 * width : 4 * width]).astype(BF16)
        for d in range(nt):
            start = pl.multiple_of((t ^ d) * rows, 16)
            part_refs[d][...] = out[pl.ds(start, rows), :]

    results = pl.pallas_call(
        without(kernel, 4 + count, len(deps)),
        out_shape=[
            shape((length, D), BF16),
            shape((length, 2 * width), F32),
            shape((length, 2 * width), BF16),
            shape((length, width), BF16),
            shape((heads, length, length), F32),
            shape((length, width), BF16),
            shape((D, SIDE), BF16),
            shape((8, D), F32),
            shape((8, HD), F32),
        ]
        + [shape((rows, D), BF16)] * nt,
        in_specs=[SMEM, VMEM, VMEM, VMEM] + [HBM] * (count + len(deps)),
        out_specs=[VMEM] * (9 + nt),
        scratch_shapes=[
            pltpu.VMEM((D, columns), BF16),
            pltpu.VMEM((length, D), BF16),
            pltpu.SemaphoreType.DMA((len(pieces),)),
        ],
        compiler_params=params(),
        cost_estimate=cost(5),
        name="attend_forward",
    )(pos, tokens, cosine, sine, *arrays, *deps)
    return results[:9], results[9:]


def attend_backward(pos, grad_rows, ffn_row, pieces, saved, tokens, cosine, sine, nf, nt, deps=()):
    _, qk, rot, values, probs, _, _, gains, head_gains = saved
    length = tokens.shape[0]
    block = D // nf
    rows = length // nt
    columns = pieces[0][2].shape[1]
    width = (columns - SIDE) // 4
    heads = width // HD
    more = gain_columns(rows)
    arrays = arrays_of(pieces)
    count = len(arrays)

    def kernel(pos_ref, x_ref, cos_ref, sin_ref, qk_ref, rot_ref, v_ref, prob_ref, gain_ref, head_gain_ref, ffn_ref, *refs):
        grad_refs, refs = refs[:nt], refs[nt:]
        piece_refs, refs = refs[:count], refs[count:]
        dqkv_ref = refs[0]
        part_refs, (w, out, db_ref, sems) = refs[1:3], refs[3:]
        f, t = pos_ref[0], pos_ref[1]

        def place(index, row, number):
            start = pl.multiple_of((f ^ index) * block + row, 16)
            return w.at[pl.ds(start, number), :]

        copies = start_fetch(pieces, piece_refs, place, sems)
        for d in range(nt):
            start = pl.multiple_of((t ^ d) * rows, 16)
            db_ref[pl.ds(start, rows), :] = grad_refs[d][:, :D]
        for copy in copies:
            copy.wait()
        cos, sin = cos_ref[...], sin_ref[...]
        head_gains = head_gain_ref[...]
        grad_att = dot(db_ref[...], w[:, 3 * width : 4 * width]).astype(BF16)
        gain_rows = [jnp.zeros((1, HD), F32), jnp.zeros((1, HD), F32)]
        for h in range(heads):
            span = slice(h * HD, (h + 1) * HD)
            query_low = rot_ref[:, span]
            key_low = rot_ref[:, width + h * HD : width + (h + 1) * HD]
            grad_out = grad_att[:, span]
            exact = prob_ref[h]
            grad_probs = dot_nt(grad_out, v_ref[:, span])
            row_terms = jnp.sum(exact * grad_probs, axis=-1, keepdims=True)
            grad_scores = (exact * (grad_probs - row_terms)).astype(BF16)
            dqkv_ref[:, 2 * width + h * HD : 2 * width + (h + 1) * HD] = dot_tn(
                exact.astype(BF16), grad_out
            ).astype(BF16)
            both = (dot(grad_scores, key_low), dot_tn(grad_scores, query_low))
            for which in range(2):
                span_w = slice(which * width + h * HD, which * width + (h + 1) * HD)
                grads = both[which] * (HD**-0.5)
                grads = grads * cos - half_turn(grads) * sin
                raw = qk_ref[:, span_w]
                inverse = rms_inverse(raw)
                gain_rows[which] = gain_rows[which] + jnp.sum(
                    grads * raw * inverse, axis=0, keepdims=True
                )
                dqkv_ref[:, span_w] = norm_backward(
                    raw, inverse, head_gains[2 + which : 3 + which], grads
                ).astype(BF16)
        grad_normed = dot_nt(dqkv_ref[...], w[:, : 3 * width])
        out[...] = grad_normed.astype(BF16)
        x = x_ref[...].astype(F32)
        row = jnp.sum(grad_normed * (x * rms_inverse(x)), axis=0, keepdims=True)
        lines = [row[:, k * SIDE : (k + 1) * SIDE] for row in (ffn_ref[0:1, :], row) for k in range(D // SIDE)]
        lines = lines + gain_rows
        gain_blocks = []
        for k in range(more // SIDE):
            own = lines[k * rows : (k + 1) * rows]
            blank = [jnp.zeros((rows - len(own), SIDE), F32)] if len(own) < rows else []
            gain_blocks.append(jnp.concatenate(own + blank, axis=0).astype(BF16))
        for d in range(nt):
            start = pl.multiple_of((t ^ d) * rows, 16)
            to = part_refs[d % 2]
            span = slice(d // 2 * rows, (d // 2 + 1) * rows)
            to[span, :D] = out[pl.ds(start, rows), :]
            for k, gain_block in enumerate(gain_blocks):
                to[span, D + k * SIDE : D + (k + 1) * SIDE] = gain_block

    results = pl.pallas_call(
        without(kernel, 11 + nt + count, len(deps)),
        out_shape=[
            shape((length, 3 * width), BF16),
        ]
        + [shape((nt // 2 * rows, D + more), BF16)] * 2,
        in_specs=[SMEM] + [VMEM] * (10 + nt) + [HBM] * (count + len(deps)),
        out_specs=[VMEM] * 3,
        scratch_shapes=[
            pltpu.VMEM((D, columns), BF16),
            pltpu.VMEM((length, D), BF16),
            pltpu.VMEM((length, D), BF16),
            pltpu.SemaphoreType.DMA((len(pieces),)),
        ],
        compiler_params=params(),
        cost_estimate=cost(0.1),
        name="attend_backward",
    )(
        pos, tokens, cosine, sine, qk, rot, values, probs, gains, head_gains, ffn_row,
        *grad_rows, *arrays, *deps,
    )
    return results


def projection_gradients(pos, normed, dqkv, nf, deps=()):
    length = normed.shape[0]
    block = D // nf
    width = dqkv.shape[1]

    def kernel(pos_ref, n1_ref, dqkv_ref, keep_ref, send_ref):
        for p in range(nf):
            start = pl.multiple_of((pos_ref[0] ^ p) * block, 128)
            to = (keep_ref if p % 2 == 0 else send_ref).at[p // 2]
            to[...] = dot_tn(n1_ref[:, pl.ds(start, block)], dqkv_ref[...]).astype(BF16)

    return pl.pallas_call(
        without(kernel, 3, len(deps)),
        out_shape=[shape((nf // 2, block, width), BF16)] * 2,
        in_specs=[SMEM, VMEM, VMEM] + [HBM] * len(deps),
        out_specs=[VMEM] * 2,
        compiler_params=params(),
        cost_estimate=cost(0.1),
        name="projection_gradients",
    )(pos, normed, dqkv, *deps)


def output_gradients(pos, attended, grad_parts, normed_parts, gain_parts, group, nf, nt, deps=()):
    length, width = attended.shape
    rows = length // nt
    block = D // nf
    columns = width + SIDE
    more = gain_columns(rows)
    count = D // SIDE

    def kernel(pos_ref, att_ref, *refs):
        grad_refs, normed_refs, part_refs = refs[:nt], refs[nt : 2 * nt], refs[2 * nt : 2 * nt + 2]
        keep_ref, send_ref, db, n2, gain_ref = refs[2 * nt + 2 :]
        f, t = pos_ref[0], pos_ref[1]
        for d in range(nt):
            start = pl.multiple_of((t ^ d) * rows, 16)
            db[pl.ds(start, rows), :] = grad_refs[d][...]
            n2[pl.ds(start, rows), :] = normed_refs[d][:, :D]
        total = part_refs[0][:, D:].astype(F32) + part_refs[1][:, D:].astype(F32)
        for line in range(2 * count + 2):
            column, at = line // rows * SIDE, line % rows
            to = line // count if line < 2 * count else line - 2 * count + 2
            lane = line % count * SIDE if line < 2 * count else 0
            gain_ref[to : to + 1, lane : lane + SIDE] = total[at : at + 1, column : column + SIDE]
        lane = lanes((block, SIDE))
        sub = lax.broadcasted_iota(jnp.int32, (block, SIDE), 0)
        for p in range(nf):
            owner = f ^ p
            start = pl.multiple_of(owner * block, 128)
            to = (keep_ref if p % 2 == 0 else send_ref).at[p // 2]
            to[:, :width] = dot_tn(db[:, pl.ds(start, block)], att_ref[...]).astype(BF16)
            side = dot_tn(n2[:, pl.ds(start, block)], db[:, D:])
            for which in range(2):
                row = gain_ref[which : which + 1, pl.ds(start, block)]
                column = jnp.transpose(jnp.broadcast_to(row, (SIDE, block)))
                side = jnp.where(lane == EXPERTS + which, column, side)
            mine = (lane == owner * group + sub) & (sub < group)
            for which in range(2, 4):
                spread = jnp.where(mine, gain_ref[which : which + 1, :HD], 0.0)
                column = jnp.sum(spread, axis=1, keepdims=True)
                side = jnp.where(lane == EXPERTS + which, column, side)
            to[:, width:] = side.astype(BF16)

    return pl.pallas_call(
        without(kernel, 4 + 2 * nt, len(deps)),
        out_shape=[shape((nf // 2, block, columns), BF16)] * 2,
        in_specs=[SMEM] + [VMEM] * (3 + 2 * nt) + [HBM] * len(deps),
        out_specs=[VMEM] * 2,
        scratch_shapes=[
            pltpu.VMEM((length, D + SIDE), BF16),
            pltpu.VMEM((length, D), BF16),
            pltpu.VMEM((8, D), F32),
        ],
        compiler_params=params(),
        cost_estimate=cost(0.1),
        name="output_gradients",
    )(pos, attended, *grad_parts, *normed_parts, *gain_parts, *deps)


def gain_columns(rows):
    return SIDE * -(-(2 * D // SIDE + 2) // rows)


def norm_and_route(pos, tokens, routes, parts, gains, side, nt, deps=()):
    rows = tokens.shape[0] // nt
    top = routes.shape[1]

    def kernel(pos_ref, x_ref, route_ref, gain_ref, side_ref, *refs):
        part_refs, (h_ref, next_ref, gate_ref) = refs[:nt], refs[nt:]
        h = x_ref[...].astype(F32)
        for ref in part_refs:
            h = h + ref[...].astype(F32)
        h_ref[...] = h
        n2 = (h * rms_inverse(h) * gain_ref[1:2]).astype(BF16)
        next_ref[:, :D] = n2
        logits = dot(n2, side_ref[...])
        lane = lanes((rows, SIDE))
        chosen = route_ref[:, 0:1] == lane
        for j in range(1, top):
            chosen = chosen | (route_ref[:, j : j + 1] == lane)
        highest = jnp.max(jnp.where(chosen, logits, -jnp.inf), axis=-1, keepdims=True)
        shifted = jnp.where(chosen, jnp.exp(jnp.where(chosen, logits - highest, 0.0)), 0.0)
        gates = shifted / jnp.sum(shifted, axis=-1, keepdims=True)
        gate_ref[...] = gates
        first = gates.astype(BF16).astype(F32)
        rest = (gates - first).astype(BF16).astype(F32)
        next_ref[:, D:] = (first + pltpu.roll(rest, EXPERTS, 1)).astype(BF16)

    whole = lambda i, pos: (0, 0)
    mine = lambda i, pos: (pos[1], 0)
    return pl.pallas_call(
        without(kernel, 5 + nt, len(deps)),
        out_shape=[shape((rows, D), F32), shape((rows, D + SIDE), BF16), shape((rows, SIDE), F32)],
        grid_spec=pltpu.PrefetchScalarGridSpec(
            num_scalar_prefetch=1,
            grid=(1,),
            in_specs=[
                pl.BlockSpec((rows, D), mine),
                pl.BlockSpec((rows, top), mine),
                pl.BlockSpec((8, D), whole),
                pl.BlockSpec((D, SIDE), whole),
            ]
            + [pl.BlockSpec((rows, D), whole)] * nt
            + [HBM] * len(deps),
            out_specs=[
                pl.BlockSpec((rows, D), whole),
                pl.BlockSpec((rows, D + SIDE), whole),
                pl.BlockSpec((rows, SIDE), whole),
            ],
        ),
        compiler_params=params(),
        cost_estimate=cost(100),
        name="norm_and_route",
    )(pos, tokens, routes, gains, side, *parts, *deps)


def norm_back(pos, cotangent, parts, h, gates, gains, side, nt, deps=()):
    rows = h.shape[0]

    def kernel(pos_ref, cot_ref, h_ref, gate_ref, gain_ref, side_ref, *refs):
        part_refs, (dh_ref, db_ref, row_ref) = refs[:nt], refs[nt:]
        total = part_refs[0][...].astype(F32)
        for ref in part_refs[1:]:
            total = total + ref[...].astype(F32)
        pair = total[:, D:]
        pair = pair + pltpu.roll(pair, EXPERTS, 1)
        gates = gate_ref[...]
        grads = gates * (pair - jnp.sum(gates * pair, axis=-1, keepdims=True))
        low = grads.astype(BF16)
        dn2 = total[:, :D] + dot_nt(low, side_ref[...])
        h = h_ref[...]
        inverse = rms_inverse(h)
        gain_row = jnp.sum(dn2 * h * inverse, axis=0, keepdims=True)
        row_ref[...] = jnp.broadcast_to(gain_row, (8, D))
        dh = cot_ref[...].astype(F32) + norm_backward(h, inverse, gain_ref[1:2], dn2)
        dh_ref[...] = dh
        db_ref[:, :D] = dh.astype(BF16)
        db_ref[:, D:] = low

    whole = lambda i, pos: (0, 0)
    mine = lambda i, pos: (pos[1], 0)
    return pl.pallas_call(
        without(kernel, 6 + nt, len(deps)),
        out_shape=[shape((rows, D), F32), shape((rows, D + SIDE), BF16), shape((8, D), F32)],
        grid_spec=pltpu.PrefetchScalarGridSpec(
            num_scalar_prefetch=1,
            grid=(1,),
            in_specs=[
                pl.BlockSpec((rows, D), mine),
                pl.BlockSpec((rows, D), whole),
                pl.BlockSpec((rows, SIDE), whole),
                pl.BlockSpec((8, D), whole),
                pl.BlockSpec((D, SIDE), whole),
            ]
            + [pl.BlockSpec((rows, D + SIDE), whole)] * nt
            + [HBM] * len(deps),
            out_specs=[
                pl.BlockSpec((rows, D), whole),
                pl.BlockSpec((rows, D + SIDE), whole),
                pl.BlockSpec((8, D), whole),
            ],
        ),
        compiler_params=params(),
        cost_estimate=cost(100),
        name="norm_back",
    )(pos, cotangent, h, gates, gains, side, *parts, *deps)


def input_gradient(pos, tokens, parts, dh, gains, deps=()):
    rows = dh.shape[0]

    def kernel(pos_ref, x_ref, dh_ref, gain_ref, *refs):
        part_refs, out_ref = refs[:2], refs[2]
        total = part_refs[0][...].astype(F32)
        for ref in part_refs[1:]:
            total = total + ref[...].astype(F32)
        x = x_ref[...].astype(F32)
        out_ref[...] = (
            dh_ref[...] + norm_backward(x, rms_inverse(x), gain_ref[0:1], total)
        ).astype(BF16)

    whole = lambda i, pos: (0, 0)
    return pl.pallas_call(
        without(kernel, 6, len(deps)),
        out_shape=shape((rows, D), BF16),
        grid_spec=pltpu.PrefetchScalarGridSpec(
            num_scalar_prefetch=1,
            grid=(1,),
            in_specs=[
                pl.BlockSpec((rows, D), lambda i, pos: (pos[1], 0)),
                pl.BlockSpec((rows, D), whole),
                pl.BlockSpec((8, D), whole),
            ]
            + [pl.BlockSpec((rows, D), whole)] * 2
            + [HBM] * len(deps),
            out_specs=pl.BlockSpec((rows, D), whole),
        ),
        compiler_params=params(),
        cost_estimate=cost(0.1),
        name="input_gradient",
    )(pos, tokens, dh, gains, *parts, *deps)


def fold(kept, received, rows, deps=()):
    total, columns = kept.shape

    def kernel(kept_ref, received_ref, even_ref, odd_ref):
        for k in range(total // rows):
            span = slice(k * rows, (k + 1) * rows)
            to = (even_ref, odd_ref)[k % 2]
            to[k // 2 * rows : (k // 2 + 1) * rows, :] = (
                kept_ref[span, :].astype(F32) + received_ref[span, :].astype(F32)
            ).astype(BF16)

    return pl.pallas_call(
        without(kernel, 2, len(deps)),
        out_shape=[shape((total // 2, columns), BF16)] * 2,
        in_specs=[VMEM] * 2 + [HBM] * len(deps),
        out_specs=[VMEM] * 2,
        compiler_params=params(),
        cost_estimate=cost(0.1),
        name="fold",
    )(kept, received, *deps)


def pick_rows(pos, array, nt, deps=()):
    total, features = array.shape
    rows = total // nt

    def kernel(pos_ref, array_ref, *out_refs):
        for d in range(nt):
            start = pl.multiple_of((pos_ref[1] ^ d) * rows, 16)
            out_refs[d][...] = array_ref[pl.ds(start, rows), :]

    return pl.pallas_call(
        without(kernel, 2, len(deps)),
        out_shape=[shape((rows, features), array.dtype)] * nt,
        in_specs=[SMEM, VMEM] + [HBM] * len(deps),
        out_specs=[VMEM] * nt,
        compiler_params=params(),
        cost_estimate=cost(0.1),
        name="pick_rows",
    )(pos, array, *deps)


def place_rows(pos, arrays, order, rows, deps=()):
    features = arrays[0].shape[1]
    blocks = [(n, k) for n, array in enumerate(arrays) for k in range(array.shape[0] // rows)]

    def kernel(pos_ref, *refs):
        for (n, k), d in zip(blocks, order):
            start = pl.multiple_of((pos_ref[1] ^ d) * rows, 16)
            refs[-1][pl.ds(start, rows), :] = refs[n][k * rows : (k + 1) * rows, :]

    return pl.pallas_call(
        without(kernel, 1 + len(arrays), len(deps)),
        out_shape=shape((rows * len(order), features), arrays[0].dtype),
        in_specs=[SMEM] + [VMEM] * len(arrays) + [HBM] * len(deps),
        out_specs=VMEM,
        compiler_params=params(),
        cost_estimate=cost(0.1),
        name="place_rows",
    )(pos, *arrays, *deps)


def spread_rows(slots, source, target, pair, number, cut):
    for begin in range(0, source.shape[2], cut):
        span = slice(begin, min(begin + cut, source.shape[2]))
        two = [dot_tn(slots[2 * pair + k], source[2 * pair + k, :, span]) for k in range(2)]
        for e in range(number):
            joined = jnp.concatenate([rows[e * CAP : (e + 1) * CAP] for rows in two], axis=0)
            target(e, span, joined)


def sum_rows(slots, results, target, pair, number, total, cut):
    at = slice(pair * 2 * CAP, (pair + 1) * 2 * CAP)
    for begin in range(0, total, cut):
        span = slice(begin, min(begin + cut, total))
        blocks = [results[e, at, span].astype(F32) for e in range(number)]
        for k in range(2):
            rows = jnp.concatenate([b[k * CAP : (k + 1) * CAP] for b in blocks], axis=0)
            target[2 * pair + k, :, span] = dot(slots[2 * pair + k], rows.astype(BF16)).astype(BF16)


def route_cotangent(pos, pieces, weights, nf, top, deps=()):
    number = weights.shape[0]
    length = sum(rows for index, _, _, _, rows in pieces if index == 0)
    slots = number * CAP
    arrays = arrays_of(pieces)
    count = len(arrays)

    def kernel(pos_ref, *refs):
        piece_refs, (slot_ref, rows_ref, cot, spread, sems) = refs[:count], refs[count:]
        e = pl.program_id(0)
        f = pos_ref[0]

        @pl.when(e == 0)
        def _():
            copies = start_fetch(
                pieces, piece_refs, lambda i, row, n: cot.at[i, pl.ds(row, n), :], sems, f
            )
            column = lanes((length, slots))
            expert = jnp.zeros((length, slots), jnp.int32)
            for k in range(1, number):
                expert = expert + (column >= k * CAP).astype(jnp.int32)
            rank = (column - expert * CAP + 1).astype(F32)
            expert = (expert + f * number).astype(F32)
            lower = (
                lax.broadcasted_iota(jnp.int32, (length, length), 0) >= lanes((length, length))
            ).astype(F32).astype(BF16)
            for copy in copies:
                copy.wait()
            for s in range(nf):
                named = cot[s, :, D:].astype(F32)
                hit = named[:, 0:1] == expert
                for j in range(1, top):
                    hit = hit | (named[:, j : j + 1] == expert)
                hit = jnp.where(hit, 1.0, 0.0)
                so_far = dot(lower, hit.astype(BF16))
                slot_ref[s] = jnp.where((so_far == rank) & (hit > 0.0), 1.0, 0.0).astype(BF16)
            for pair in range(nf // 2):
                at = slice(pair * 2 * CAP, (pair + 1) * 2 * CAP)

                def put(k, span, rows):
                    spread[k, at, span] = rows.astype(BF16)

                spread_rows(slot_ref, cot.at[:, :, :D], put, pair, number, 512)

        rows_ref[0] = spread[e]

    return pl.pallas_call(
        without(kernel, 1 + count, len(deps)),
        out_shape=[
            shape((nf, length, slots), BF16),
            shape((number, nf * CAP, D), BF16),
        ],
        grid_spec=pltpu.PrefetchScalarGridSpec(
            num_scalar_prefetch=1,
            grid=(number,),
            in_specs=[HBM] * (count + len(deps)),
            out_specs=[
                pl.BlockSpec((nf, length, slots), lambda e, pos: (0, 0, 0)),
                pl.BlockSpec((1, nf * CAP, D), lambda e, pos: (e, 0, 0)),
            ],
            scratch_shapes=[
                pltpu.VMEM((nf, length, D + SIDE), BF16),
                pltpu.VMEM((number, nf * CAP, D), BF16),
                pltpu.SemaphoreType.DMA((len(pieces),)),
            ],
        ),
        compiler_params=params(),
        cost_estimate=cost(0.1),
        name="route_cotangent",
    )(pos, *arrays, *deps)


def down_back(grad_rows, weights, deps=()):
    number, filled, _ = grad_rows.shape
    width = weights.shape[3]

    def kernel(rows_ref, w_ref, out_ref):
        out_ref[0] = dot(rows_ref[0], w_ref[0, 0])

    return pl.pallas_call(
        without(kernel, 2, len(deps)),
        out_shape=shape((number, filled, width), F32),
        grid=(number,),
        in_specs=[
            pl.BlockSpec((1, filled, D), lambda e: (e, 0, 0)),
            pl.BlockSpec((1, 1, D, width), lambda e: (e, 2, 0, 0)),
        ]
        + [HBM] * len(deps),
        out_specs=pl.BlockSpec((1, filled, width), lambda e: (e, 0, 0)),
        compiler_params=params(),
        cost_estimate=cost(0.1),
        name="down_back",
    )(grad_rows, weights, *deps)


def run_experts(pos, pieces, slot_table, down, weights, nf, cut):
    number, _, _, width = weights.shape
    length, slots = slot_table.shape[1:]
    filled = nf * CAP
    arrays = arrays_of(pieces)
    count = len(arrays)

    def kernel(pos_ref, slot_ref, down_ref, gate_w, up_w, *refs):
        piece_refs, refs = refs[:count], refs[count:]
        rows_ref, dg_ref, du_ref, hidden_ref = refs[:4]
        sums_refs = (refs[4:6], refs[6:8])
        wide, spread, gates, results, sems, out_sems = refs[8:]
        e = pl.program_id(0)
        f = pos_ref[0]

        @pl.when(e == 0)
        def _():
            copies = start_fetch(
                pieces, piece_refs, lambda i, row, n: wide.at[i, pl.ds(row, n), :], sems
            )
            for copy in copies:
                copy.wait()
            for pair in range(nf // 2):
                at = slice(pair * 2 * CAP, (pair + 1) * 2 * CAP)

                def put(k, span, rows):
                    if span.start < D:
                        spread[k, at, span] = rows.astype(BF16)
                    else:
                        lane = lanes((2 * CAP, SIDE))
                        own = f * number + k
                        gate = jnp.where((lane == own) | (lane == own + EXPERTS), rows, 0.0)
                        gates[k, at, :] = jnp.broadcast_to(
                            jnp.sum(gate, axis=-1, keepdims=True), (2 * CAP, SIDE)
                        )

                spread_rows(slot_ref, wide, put, pair, number, 512)

        rows = spread[e]
        rows_ref[0] = rows
        first, second = gate_w[0, 0], up_w[0, 0]
        gate_pre = dot(rows, first)
        up_pre = dot(rows, second)
        gate = gates[e][:, 0:1]
        sigma = jax.nn.sigmoid(gate_pre)
        swish = gate_pre * sigma
        hidden = (swish * up_pre).astype(BF16).astype(F32)
        hidden_ref[0] = (gate * hidden).astype(BF16)
        unscaled = down_ref[0]
        grad_hidden = gate * unscaled
        dg = (grad_hidden * up_pre * sigma * (1.0 + gate_pre * (1.0 - sigma))).astype(BF16)
        du = (grad_hidden * swish).astype(BF16)
        dg_ref[0] = dg
        du_ref[0] = du
        results[e, :, :D] = (dot_nt(dg, first) + dot_nt(du, second)).astype(BF16)
        pair_grad = jnp.sum(unscaled * hidden, axis=-1, keepdims=True)
        high = pair_grad.astype(BF16).astype(F32)
        lane = lanes((filled, SIDE))
        own = f * number + e
        results[e, :, D:] = jnp.where(
            lane == own, high, jnp.where(lane == own + EXPERTS, pair_grad - high, 0.0)
        ).astype(BF16)

        @pl.when(e == number - 1)
        def _():
            copies = []
            for pair in range(nf // 2):
                sum_rows(slot_ref, results, wide, pair, number, D + SIDE, 512)
                for k, to in enumerate(sums_refs):
                    index = 2 * pair + k
                    for g, span in enumerate((pl.ds(0, cut), pl.ds(cut, length - cut))):
                        copy = pltpu.make_async_copy(
                            wide.at[index, span, :], to[g].at[pair], out_sems.at[2 * index + g]
                        )
                        copy.start()
                        copies.append(copy)
            for copy in copies:
                copy.wait()

    return pl.pallas_call(
        kernel,
        out_shape=[
            shape((number, filled, D), BF16),
            shape((number, filled, width), BF16),
            shape((number, filled, width), BF16),
            shape((number, filled, width), BF16),
        ]
        + [shape((nf // 2, number, D + SIDE), BF16) for number in (cut, length - cut)] * 2,
        grid_spec=pltpu.PrefetchScalarGridSpec(
            num_scalar_prefetch=1,
            grid=(number,),
            in_specs=[
                pl.BlockSpec((nf, length, slots), lambda e, pos: (0, 0, 0)),
                pl.BlockSpec((1, filled, width), lambda e, pos: (e, 0, 0)),
                pl.BlockSpec((1, 1, D, width), lambda e, pos: (e, 0, 0, 0)),
                pl.BlockSpec((1, 1, D, width), lambda e, pos: (e, 1, 0, 0)),
            ]
            + [HBM] * count,
            out_specs=[
                pl.BlockSpec((1, filled, D), lambda e, pos: (e, 0, 0)),
                pl.BlockSpec((1, filled, width), lambda e, pos: (e, 0, 0)),
                pl.BlockSpec((1, filled, width), lambda e, pos: (e, 0, 0)),
                pl.BlockSpec((1, filled, width), lambda e, pos: (e, 0, 0)),
            ]
            + [HBM] * 4,
            scratch_shapes=[
                pltpu.VMEM((nf, length, D + SIDE), BF16),
                pltpu.VMEM((number, filled, D), BF16),
                pltpu.VMEM((number, filled, SIDE), F32),
                pltpu.VMEM((number, filled, D + SIDE), BF16),
                pltpu.SemaphoreType.DMA((len(pieces),)),
                pltpu.SemaphoreType.DMA((2 * nf,)),
            ],
        ),
        compiler_params=params(),
        cost_estimate=cost(5),
        name="run_experts",
    )(pos, slot_table, down, weights, weights, *arrays)


def expert_outputs(pos, slot_table, hidden, weights, nt, deps=()):
    number, filled, width = hidden.shape
    nf, length, slots = slot_table.shape

    rows = length // nt

    def kernel(pos_ref, slot_ref, hidden_ref, w_ref, out_ref, results, out, sems):
        e = pl.program_id(0)
        results[e] = dot_nt(hidden_ref[0], w_ref[0, 0]).astype(BF16)

        @pl.when(e == number - 1)
        def _():
            copies = []
            for pair in range(nf // 2):
                sum_rows(slot_ref, results, out, pair, number, D, 512)
                for index in (2 * pair, 2 * pair + 1):
                    for d in range(nt):
                        start = pl.multiple_of((pos_ref[1] ^ d) * rows, 16)
                        copy = pltpu.make_async_copy(
                            out.at[index, pl.ds(d * rows, rows), :],
                            out_ref.at[pos_ref[0] ^ index, pl.ds(start, rows), :],
                            sems.at[index * nt + d],
                        )
                        copy.start()
                        copies.append(copy)
            for copy in copies:
                copy.wait()

    return pl.pallas_call(
        without(kernel, 4, len(deps)),
        out_shape=shape((nf, length, D), BF16),
        grid_spec=pltpu.PrefetchScalarGridSpec(
            num_scalar_prefetch=1,
            grid=(number,),
            in_specs=[
                pl.BlockSpec((nf, length, slots), lambda e, pos: (0, 0, 0)),
                pl.BlockSpec((1, filled, width), lambda e, pos: (e, 0, 0)),
                pl.BlockSpec((1, 1, D, width), lambda e, pos: (e, 2, 0, 0)),
            ]
            + [HBM] * len(deps),
            out_specs=HBM,
            scratch_shapes=[
                pltpu.VMEM((number, filled, D), BF16),
                pltpu.VMEM((nf, length, D), BF16),
                pltpu.SemaphoreType.DMA((nf * nt,)),
            ],
        ),
        compiler_params=params(),
        cost_estimate=cost(0.1),
        name="expert_outputs",
    )(pos, slot_table, hidden, weights, *deps)


def expert_gradients(rows, grad_rows, dg, du, hidden, first, number, so_far=None, deps=()):
    everyone, filled, width = dg.shape

    def kernel(rows_ref, grad_ref, dg_ref, du_ref, hidden_ref, *refs):
        out_ref, done_ref = refs
        done_ref[...] = jnp.zeros_like(done_ref)
        rows = rows_ref[0]
        out_ref[0, 0] = dot_tn(rows, dg_ref[0])
        out_ref[0, 1] = dot_tn(rows, du_ref[0])
        out_ref[0, 2] = dot_tn(grad_ref[0], hidden_ref[0])

    tall = pl.BlockSpec((1, filled, D), lambda e: (first + e, 0, 0))
    thin = pl.BlockSpec((1, filled, width), lambda e: (first + e, 0, 0))
    before = [] if so_far is None else [so_far]
    return pl.pallas_call(
        without(kernel, 5, len(before) + len(deps)),
        out_shape=[shape((everyone, 3, D, width), F32), shape((8, SIDE), F32)],
        grid=(number,),
        in_specs=[tall, tall, thin, thin, thin] + [HBM] * (len(before) + len(deps)),
        out_specs=[
            pl.BlockSpec((1, 3, D, width), lambda e: (first + e, 0, 0, 0)),
            pl.BlockSpec((8, SIDE), lambda e: (0, 0)),
        ],
        input_output_aliases={5: 0} if before else {},
        compiler_params=params(),
        cost_estimate=cost(0.1),
        name="expert_gradients",
    )(rows, grad_rows, dg, du, hidden, *before, *deps)


def on_device(
    nf,
    nt,
    tokens,
    cotangent,
    routes,
    w_query,
    w_key,
    w_value,
    w_output,
    w_router,
    attn_gain,
    ffn_gain,
    query_gain,
    key_gain,
    expert_weights,
):
    length = tokens.shape[0]
    rows = length // nt
    block = D // nf
    group = query_gain.shape[0]
    top = routes.shape[1]
    f = lax.axis_index("fsdp").astype(jnp.int32)
    t = lax.axis_index("tensor").astype(jnp.int32)
    pos = jnp.stack([f, t])

    def placed(gain):
        return lax.dynamic_update_slice(jnp.zeros((block,), BF16), gain, (f * group,))[:, None]

    columns = [
        w_query,
        w_key,
        w_value,
        w_output,
        w_router,
        attn_gain[:, None],
        ffn_gain[:, None],
        placed(query_gain),
        placed(key_gain),
        jnp.zeros((block, SIDE - EXPERTS - 4), BF16),
    ]
    number = expert_weights.shape[0]
    cut = 2 * rows

    def around(block):
        return [block] + [swap(block, "tensor", nt, d) for d in range(1, nt)]

    def sent(parts):
        return [parts[0]] + [swap(parts[d], "tensor", nt, d) for d in range(1, nt)]

    if nf == 8:
        packed = [
            jnp.concatenate([part[half : half + block // 2] for part in columns], axis=1)
            for half in (0, block // 2)
        ]
        weights_near = [gather_near(part, nf) for part in packed]
    else:
        packed = jnp.concatenate(columns, axis=1)

    wide_cot = jnp.concatenate(
        [cotangent, routes.astype(BF16), jnp.zeros((length, SIDE - top), BF16)], axis=1
    )
    wide_cot = jnp.concatenate(
        [lax.dynamic_slice_in_dim(wide_cot, (t ^ d) * rows, rows, 0) for d in range(nt)], axis=0
    )
    position = jnp.arange(length, dtype=F32)[:, None]
    inverse = ROPE_BASE ** (-jnp.arange(HD // 2, dtype=F32) / (HD // 2))
    angles = position * inverse[None, :]
    cosine = jnp.concatenate([jnp.cos(angles)] * 2, axis=1)
    sine = jnp.concatenate([-jnp.sin(angles), jnp.sin(angles)], axis=1)

    if nf == 8:
        weights = gather_two(packed, weights_near, nf)
        wide_cot = join(
            [wide_cot],
            weights_near[0] + weights_near[1] + [w[2] for w in weights if w[0] == nf - 2],
        )
    else:
        weights = gather_rest(packed, gather_near(packed, nf), nf)
    all_cot = lax.all_gather(wide_cot, "fsdp", axis=0, tiled=True)
    cot = [(p, 0, all_cot, None, length) for p in range(nf)]
    saved, parts = attend_forward(pos, tokens, cosine, sine, weights, nf, nt)
    normed_one, _, _, _, _, attended, side, gains, _ = saved
    parts = sent(parts)
    h, normed_two, gates = norm_and_route(pos, tokens, routes, parts, gains, side, nt)

    normed_parts = around(normed_two)
    if nf == 8:
        blocks = [join(normed_parts[:2])]
        near = [gather_near(blocks[0], nf)]
        slot_table, cot_rows = route_cotangent(pos, cot, expert_weights, nf, top, deps=blocks)
        blocks.append(join(normed_parts[2:], deps=[slot_table]))
        near.append(gather_near(blocks[1], nf))
        down = down_back(cot_rows, expert_weights, deps=blocks[1:])
        sources = [near[0][1]] + list(relay(near[1][:1], [down]))
        n2_pieces = gather_two(blocks, near, nf, sources)
    else:
        slot_table, cot_rows = route_cotangent(pos, cot, expert_weights, nf, top)
        down = down_back(cot_rows, expert_weights)
        joined = join(normed_parts)
        n2_pieces = gather_rest(joined, gather_near(joined, nf), nf)
    n2_rows, dg, du, hidden, keep_near, keep_far, send_near, send_far = run_experts(
        pos, n2_pieces, slot_table, down, expert_weights, nf, cut
    )

    far, near = Reduce(keep_far, send_far, nf), Reduce(keep_near, send_near, nf)
    began = far.first() + near.first()
    outputs = expert_outputs(pos, slot_table, hidden, expert_weights, nt, deps=began)
    layer_sum = lax.psum_scatter(
        outputs.reshape(nf * length, D), "fsdp", scatter_dimension=0, tiled=True
    )
    went = far.second(deps=[outputs], micros=20)
    near.second(deps=went, micros=20)
    far_rows = list(far.rows(nt - 2))
    near_rows = list(near.rows(2, deps=far_rows[:1]))
    grad_parts = sent(near_rows + far_rows)
    each = number // 4

    def expert_part(k, deps=()):
        return expert_gradients(
            n2_rows, cot_rows, dg, du, hidden, k * each, each, grad_experts, deps
        )

    grad_experts = None
    grad_experts, done = expert_part(0, near_rows[:1])
    dh, db, ffn_row = norm_back(
        pos, cotangent, grad_parts, h, gates, gains, side, nt, deps=[done]
    )
    db_parts = around(db)
    grad_experts, done = expert_part(1, [db])
    dqkv, kept, sent_on = attend_backward(
        pos, db_parts, ffn_row, weights, saved, tokens, cosine, sine, nf, nt,
        deps=[done],
    )
    layer_parts = list(pick_rows(pos, layer_sum, nt, deps=[kept]))
    layer_rows = h
    for part in sent(layer_parts):
        layer_rows = layer_rows + part.astype(F32)
    layer_blocks = around(layer_rows.astype(BF16))
    for k in (2, 3):
        grad_experts, done = expert_part(k, [kept])
    step, deps = 1, [done]
    while step < nt // 2:
        kept, sent_on = fold(kept, swap(sent_on, "tensor", nt, step), rows, deps)
        step, deps = 2 * step, []
    keep, send = projection_gradients(pos, normed_one, dqkv, nf, deps=[kept])
    projections = Reduce(keep, send, nf)
    parts = [kept, swap(sent_on, "tensor", nt, step)]
    token_rows = input_gradient(pos, tokens, parts, dh, gains)
    pairs = projections.first(deps=[token_rows])
    blocks, order = [token_rows], [0]
    while step > 0:
        mine = blocks[0] if len(blocks) == 1 else join(blocks)
        blocks = [mine, swap(mine, "tensor", nt, step)]
        order, step = order + [d ^ step for d in order], step // 2
    grad_tokens = place_rows(pos, blocks, order, rows)
    layer_out = place_rows(pos, layer_blocks, range(nt), rows, deps=blocks[:1])
    keep, send = output_gradients(
        pos, attended, db_parts, normed_parts, parts, group, nf, nt, deps=pairs + layer_blocks[:1]
    )
    output = Reduce(keep, send, nf)
    projections.second()
    output.first()
    output.second()
    width = attended.shape[1]
    weight_grads, out_sum = projections.total(), output.total()
    return (
        layer_out,
        grad_tokens,
        weight_grads[:, :width],
        weight_grads[:, width : 2 * width],
        weight_grads[:, 2 * width :],
        out_sum[:, :width],
        out_sum[:, width : width + EXPERTS],
        out_sum[:, width + EXPERTS + 1],
        out_sum[:, width + EXPERTS],
        out_sum[:group, width + EXPERTS + 2],
        out_sum[:group, width + EXPERTS + 3],
        grad_experts,
    )


def solution(mesh):
    nf, nt = mesh.shape["fsdp"], mesh.shape["tensor"]
    rows, both, line = P("fsdp", None), P("fsdp", "tensor"), P("fsdp")
    experts = P("fsdp", None, None, "tensor")
    return jax.shard_map(
        functools.partial(on_device, nf, nt),
        mesh=mesh,
        in_specs=(rows, rows, rows, both, both, both, both, rows, line, line, line, line, experts),
        out_specs=(rows, rows, both, both, both, both, rows, line, line, line, line, experts),
        check_vma=False,
    )
```

```python
import functools

import jax
import jax.numpy as jnp
from jax import lax
from jax.experimental import pallas as pl
from jax.experimental.pallas import tpu as pltpu
from jax.sharding import PartitionSpec as P

D = 2048
HD = 128
EXPERTS = 64
CAP = 40
SIDE = 128
EPSILON = 1e-06
ROPE_BASE = 10000.0

F32 = jnp.float32
BF16 = jnp.bfloat16
VMEM = pl.BlockSpec(memory_space=pltpu.VMEM)
SMEM = pl.BlockSpec(memory_space=pltpu.SMEM)
HBM = pl.BlockSpec(memory_space=pl.ANY)
VMEM_BYTES = 60 * 1024 * 1024


def shape(dims, dtype):
    return jax.ShapeDtypeStruct(tuple(dims), dtype)


def params(**more):
    return pltpu.CompilerParams(vmem_limit_bytes=VMEM_BYTES, **more)


def cost(micros):
    return pl.CostEstimate(
        flops=int(micros * 1e9), bytes_accessed=int(micros * 3e6), transcendentals=0
    )


def dot(left, right):
    return jnp.dot(left, right, preferred_element_type=F32)


def dot_nt(left, right):
    return lax.dot_general(left, right, (((1,), (1,)), ((), ())), preferred_element_type=F32)


def dot_tn(left, right):
    return lax.dot_general(left, right, (((0,), (0,)), ((), ())), preferred_element_type=F32)


def rms_inverse(values):
    return lax.rsqrt(jnp.mean(values * values, axis=-1, keepdims=True) + EPSILON)


def norm_backward(values, inverse, gain, upstream):
    scaled = gain * upstream
    return inverse * scaled - values * (inverse * inverse * inverse) * jnp.mean(
        values * scaled, axis=-1, keepdims=True
    )


def half_turn(values):
    return pltpu.roll(values, HD // 2, 1)


def lanes(dims):
    return lax.broadcasted_iota(jnp.int32, dims, len(dims) - 1)


def swap(block, axis, size, step):
    return lax.ppermute(block, axis, [(i, i ^ step) for i in range(size)])


def without(kernel, at, number):
    def body(*refs):
        kernel(*refs[:at], *refs[at + number :])

    return body


def through(moves, buffer, sems):
    arriving, leaving, row = [], [], 0
    for k, (source, target) in enumerate(moves):
        here = buffer.at[pl.ds(row, source.shape[0]), :]
        arriving.append(pltpu.make_async_copy(source, here, sems.at[2 * k]))
        leaving.append(pltpu.make_async_copy(here, target, sems.at[2 * k + 1]))
        arriving[-1].start()
        row += source.shape[0]
    for arrives, leaves in zip(arriving, leaving):
        arrives.wait()
        leaves.start()
    for leaves in leaving:
        leaves.wait()


def joins(groups, deps=()):
    parts = [part for group in groups for part in group]
    count = len(parts)
    features, dtype = parts[0].shape[1], parts[0].dtype
    totals = [sum(part.shape[0] for part in group) for group in groups]

    def kernel(*refs):
        out_refs, (buffer, sems) = refs[count:-2], refs[-2:]
        moves, k = [], 0
        for out_ref, group in zip(out_refs, groups):
            row = 0
            for part in group:
                moves.append((refs[k], out_ref.at[pl.ds(row, part.shape[0]), :]))
                row, k = row + part.shape[0], k + 1
        through(moves, buffer, sems)

    return pl.pallas_call(
        without(kernel, count, len(deps)),
        out_shape=[shape((total, features), dtype) for total in totals],
        in_specs=[HBM] * (count + len(deps)),
        out_specs=[HBM] * len(groups),
        scratch_shapes=[
            pltpu.VMEM((sum(totals), features), dtype),
            pltpu.SemaphoreType.DMA((2 * count,)),
        ],
        compiler_params=params(),
        cost_estimate=cost(0.1),
        name="joins",
    )(*parts, *deps)


def join(parts, deps=()):
    return joins([parts], deps)[0]


def relay(parts, deps):
    return joins([[part] for part in parts], deps)


def halves(upper_of, lower_of, deps=()):
    rows, features = upper_of.shape
    half = rows // 2

    def kernel(upper_ref, lower_ref, upper_out, lower_out, buffer, sems):
        through(
            [
                (upper_ref.at[pl.ds(0, half), :], upper_out),
                (lower_ref.at[pl.ds(half, half), :], lower_out),
            ],
            buffer,
            sems,
        )

    return pl.pallas_call(
        without(kernel, 2, len(deps)),
        out_shape=[shape((half, features), upper_of.dtype)] * 2,
        in_specs=[HBM] * (2 + len(deps)),
        out_specs=[HBM] * 2,
        scratch_shapes=[
            pltpu.VMEM((rows, features), upper_of.dtype),
            pltpu.SemaphoreType.DMA((4,)),
        ],
        compiler_params=params(),
        cost_estimate=cost(0.1),
        name="halves",
    )(upper_of, lower_of, *deps)


def gather_near(block, size):
    if size != 8:
        return [swap(block, "fsdp", size, p) for p in range(1, size)]
    return [swap(block, "fsdp", size, 2), swap(block, "fsdp", size, 4)]


def gather_rest(block, near, size, deps=()):
    rows = block.shape[0]
    if size != 8:
        return [(p, 0, part, 0, rows) for p, part in enumerate([block] + near)]
    half = rows // 2
    upper, lower = halves(near[1], near[0], deps)
    front = swap(upper, "fsdp", size, 2)
    back = swap(lower, "fsdp", size, 4)
    pieces = []
    for k, part in enumerate([block] + near):
        pieces.append((2 * k, 0, part, 0, rows))
        pieces.append((2 * k + 1, 0, swap(part, "fsdp", size, 1), 0, rows))
    for row, part in ((0, front), (half, back)):
        pieces.append((6, row, part, 0, half))
        pieces.append((7, row, swap(part, "fsdp", size, 1), 0, half))
    return pieces


def gather_two(blocks, near, size, sources=None):
    pieces = []
    start = 0
    sources = sources or [near[0][1], near[1][0]]
    for block, (along_x, along_y), source, step in zip(blocks, near, sources, (2, 4)):
        rows = block.shape[0]
        last = swap(source, "fsdp", size, step)
        for index, part in ((0, block), (2, along_x), (4, along_y), (6, last)):
            pieces.append((index, start, part, 0, rows))
            pieces.append((index + 1, start, swap(part, "fsdp", size, 1), 0, rows))
        start += rows
    return pieces


def arrays_of(pieces):
    found = []
    for _, _, part, _, _ in pieces:
        if not any(part is other for other in found):
            found.append(part)
    return found


def start_fetch(pieces, refs, place, sems, own=None):
    arrays = arrays_of(pieces)
    copies = []
    for k, (index, row, part, at, rows) in enumerate(pieces):
        ref = next(ref for other, ref in zip(arrays, refs) if other is part)
        if at is None:
            at = pl.multiple_of((own ^ index) * rows, 16)
        copy = pltpu.make_async_copy(
            ref.at[pl.ds(at, rows), :], place(index, row, rows), sems.at[k]
        )
        copy.start()
        copies.append(copy)
    return copies


def pair_sums(keep, got, deps=()):
    _, rows, columns = keep.shape
    half = rows // 2

    def kernel(keep_x, got_x, keep_y, got_y, out_x, out_y):
        out_x[...] = (keep_x[...].astype(F32) + got_x[...].astype(F32)).astype(BF16)
        out_y[...] = (keep_y[...].astype(F32) + got_y[...].astype(F32)).astype(BF16)

    block = (1, half, columns)
    along_x = pl.BlockSpec(block, lambda j: (2 * j + 1, 0, 0))
    along_y = pl.BlockSpec(block, lambda j: (2 + j, 1, 0))
    return pl.pallas_call(
        without(kernel, 4, len(deps)),
        out_shape=[shape((2, half, columns), BF16)] * 2,
        grid=(2,),
        in_specs=[along_x, along_x, along_y, along_y] + [HBM] * len(deps),
        out_specs=[pl.BlockSpec(block, lambda j: (j, 0, 0))] * 2,
        compiler_params=params(),
        cost_estimate=cost(0.1),
        name="pair_sums",
    )(keep, got, keep, got, *deps)


def next_sums(keep, got, from_x, from_y, deps, micros):
    _, rows, columns = keep.shape
    half = rows // 2
    part = half // 2

    def kernel(keep_x, got_x, new_x, keep_y, got_y, new_y, out_x, out_y):
        out_x[...] = (
            keep_x[0].astype(F32) + got_x[0].astype(F32) + new_x[0].astype(F32)
        ).astype(BF16)
        out_y[...] = (
            keep_y[0].astype(F32) + got_y[0].astype(F32) + new_y[0].astype(F32)
        ).astype(BF16)

    block = (1, part, columns)
    upper = pl.BlockSpec(block, lambda j: (2, j, 0))
    lower = pl.BlockSpec(block, lambda j: (1, j + 2, 0))
    new = pl.BlockSpec(block, lambda j: (1, j, 0))
    return pl.pallas_call(
        without(kernel, 6, len(deps)),
        out_shape=[shape((half, columns), BF16)] * 2,
        grid=(2,),
        in_specs=[upper, upper, new, lower, lower, new] + [HBM] * len(deps),
        out_specs=[pl.BlockSpec((part, columns), lambda j: (j, 0))] * 2,
        compiler_params=params(),
        cost_estimate=cost(micros),
        name="next_sums",
    )(keep, got, from_x, keep, got, from_y, *deps)


def last_sums(keep, got, from_x, from_y, last_x, last_y, count, deps=()):
    _, rows, columns = keep.shape
    half = rows // 2
    part = rows // count
    each = half // part

    def kernel(keep_x, got_x, new_x, end_x, keep_y, got_y, new_y, end_y, *out_refs):
        for k in range(count):
            refs = (keep_x, got_x, new_x, end_x) if k < each else (keep_y, got_y, new_y, end_y)
            span = slice((k % each) * part, (k % each + 1) * part)
            total = refs[0][0, span].astype(F32)
            for ref in refs[1:3]:
                total = total + ref[0, span].astype(F32)
            out_refs[k][...] = (total + refs[3][span].astype(F32)).astype(BF16)

    block = (1, half, columns)
    first = pl.BlockSpec(block, lambda j: (0, 0, 0))
    second = pl.BlockSpec(block, lambda j: (0, 1, 0))
    end = pl.BlockSpec((half, columns), lambda j: (0, 0))
    return pl.pallas_call(
        without(kernel, 8, len(deps)),
        out_shape=[shape((part, columns), BF16)] * count,
        grid=(1,),
        in_specs=[first, first, first, end, second, second, first, end] + [HBM] * len(deps),
        out_specs=[pl.BlockSpec((part, columns), lambda j: (0, 0))] * count,
        compiler_params=params(),
        cost_estimate=cost(20),
        name="last_sums",
    )(keep, got, from_x, last_x, keep, got, from_y, last_y, *deps)


def column_sums(keep, got, from_x, from_y, last_x, last_y, widths, turned):
    _, rows, columns = keep.shape
    half = rows // 2

    def kernel(keep_x, got_x, new_x, end_x, keep_y, got_y, new_y, end_y, *out_refs):
        for k, refs in enumerate(((keep_x, got_x, new_x, end_x), (keep_y, got_y, new_y, end_y))):
            span = slice(k * half, (k + 1) * half)
            total = refs[0][0].astype(F32)
            for ref in refs[1:3]:
                total = total + ref[0].astype(F32)
            total = total + refs[3][...].astype(F32)
            column = 0
            for width, out_ref in zip(widths, out_refs):
                out_ref[span, :] = total[:, column : column + width]
                column += width
            if turned:
                out_refs[-1][:, span] = jnp.transpose(total[:, column : column + turned])

    block = (1, half, columns)
    first = pl.BlockSpec(block, lambda j: (0, 0, 0))
    second = pl.BlockSpec(block, lambda j: (0, 1, 0))
    end = pl.BlockSpec((half, columns), lambda j: (0, 0))
    shapes = [(rows, width) for width in widths] + [(turned, rows)] * (turned > 0)
    return pl.pallas_call(
        kernel,
        out_shape=[shape(dims, F32) for dims in shapes],
        grid=(1,),
        in_specs=[first, first, first, end, second, second, first, end],
        out_specs=[pl.BlockSpec(dims, lambda j: (0, 0)) for dims in shapes],
        compiler_params=params(),
        cost_estimate=cost(0.1),
        name="column_sums",
    )(keep, got, from_x, last_x, keep, got, from_y, last_y)


def halve(array, deps=()):
    rows, columns = array.shape
    half = columns // 2

    def kernel(ref, left_ref, right_ref):
        left_ref[...] = ref[:, :half]
        right_ref[...] = ref[:, half:]

    return pl.pallas_call(
        without(kernel, 1, len(deps)),
        out_shape=[shape((rows, half), array.dtype)] * 2,
        grid=(2,),
        in_specs=[pl.BlockSpec((rows // 2, columns), lambda j: (j, 0))] + [HBM] * len(deps),
        out_specs=[pl.BlockSpec((rows // 2, half), lambda j: (j, 0))] * 2,
        compiler_params=params(),
        cost_estimate=cost(0.1),
        name="halve",
    )(array, *deps)


class Reduce:
    def __init__(self, keep, send, size):
        self.keep, self.send, self.size = keep, send, size
        if size == 8:
            self.got = swap(send, "fsdp", size, 1)

    def first(self, deps=()):
        if self.size != 8:
            return []
        self.pair = pair_sums(self.keep, self.got, deps)
        self.from_x = swap(self.pair[0], "fsdp", self.size, 2)
        self.from_y = swap(self.pair[1], "fsdp", self.size, 4)
        return list(self.pair[:1])

    def second(self, deps=(), micros=0.1):
        if self.size != 8:
            return []
        sums = next_sums(self.keep, self.got, self.from_x, self.from_y, deps, micros)
        self.last_x = swap(sums[0], "fsdp", self.size, 4)
        self.last_y = swap(sums[1], "fsdp", self.size, 2)
        return list(sums[:1])

    def total(self):
        if self.size != 8:
            total = self.keep[0].astype(F32)
            for p in range(1, self.size):
                block = self.keep[p // 2] if p % 2 == 0 else self.send[p // 2]
                total = total + swap(block, "fsdp", self.size, p).astype(F32)
            return total
        half = self.keep.shape[1] // 2
        sums = []
        for rows, new, last in (
            (slice(0, half), self.from_x, self.last_x),
            (slice(half, None), self.from_y, self.last_y),
        ):
            sums.append(
                self.keep[0, rows].astype(F32)
                + self.got[0, rows].astype(F32)
                + new[0].astype(F32)
                + last.astype(F32)
            )
        return jnp.concatenate(sums, axis=0)

    def columns(self, widths, turned=0):
        if self.size == 8:
            return column_sums(
                self.keep, self.got, self.from_x, self.from_y, self.last_x, self.last_y, widths, turned
            )
        total, found, column = self.total(), [], 0
        for width in widths:
            found.append(total[:, column : column + width])
            column += width
        return found + [total[:, column : column + turned].T] * (turned > 0)

    def rows(self, count, deps=()):
        if self.size != 8:
            return jnp.split(self.total().astype(BF16), count, axis=0)
        return last_sums(
            self.keep, self.got, self.from_x, self.from_y, self.last_x, self.last_y, count, deps
        )


def attend_forward(pos, tokens, cosine, sine, pieces, nf, nt, deps=()):
    length = tokens.shape[0]
    block = D // nf
    rows = length // nt
    columns = pieces[0][2].shape[1]
    width = (columns - SIDE) // 4
    heads = width // HD
    arrays = arrays_of(pieces)
    count = len(arrays)

    def kernel(pos_ref, x_ref, cos_ref, sin_ref, *refs):
        piece_refs, refs = refs[:count], refs[count:]
        n1_ref, qk_ref, rot_ref, v_ref, prob_ref, att_ref, side_ref, gain_ref, head_gain_ref = refs[:9]
        part_refs, (w, out, sems) = refs[9 : 9 + nt], refs[9 + nt :]
        f, t = pos_ref[0], pos_ref[1]

        def place(index, row, number):
            start = pl.multiple_of((f ^ index) * block + row, 16)
            return w.at[pl.ds(start, number), :]

        copies = start_fetch(pieces, piece_refs, place, sems)
        x = x_ref[...].astype(F32)
        normed = x * rms_inverse(x)
        for copy in copies:
            copy.wait()
        side_ref[...] = w[:, 4 * width :]
        turned = jnp.transpose(w[:, 4 * width :].astype(F32))
        gain_ref[...] = turned[EXPERTS : EXPERTS + 8]
        head_rows = turned[EXPERTS : EXPERTS + 8, :block]
        for p in range(1, nf):
            head_rows = head_rows + turned[EXPERTS : EXPERTS + 8, p * block : (p + 1) * block]
        head_gains = head_rows[:, :HD]
        head_gain_ref[...] = head_gains
        n1 = (normed * turned[EXPERTS : EXPERTS + 1]).astype(BF16)
        n1_ref[...] = n1
        raw = dot(n1, w[:, : 3 * width])
        qk_ref[...] = raw[:, : 2 * width]
        v_ref[...] = raw[:, 2 * width :].astype(BF16)
        cos, sin = cos_ref[...], sin_ref[...]
        for h in range(heads):
            span = slice(h * HD, (h + 1) * HD)
            turned_rows = []
            for which in range(2):
                values = raw[:, which * width + h * HD : which * width + (h + 1) * HD]
                scaled = values * rms_inverse(values) * head_gains[2 + which : 3 + which]
                low = (scaled * cos + half_turn(scaled) * sin).astype(BF16)
                rot_ref[:, which * width + h * HD : which * width + (h + 1) * HD] = low
                turned_rows.append(low)
            scores = dot_nt(turned_rows[0], turned_rows[1]) * (HD**-0.5)
            shifted = jnp.exp(scores - jnp.max(scores, axis=-1, keepdims=True))
            probs = shifted / jnp.sum(shifted, axis=-1, keepdims=True)
            prob_ref[h] = probs
            att_ref[:, span] = dot(probs.astype(BF16), v_ref[:, span]).astype(BF16)
        out[...] = dot_nt(att_ref[...], w[:, 3 * width : 4 * width]).astype(BF16)
        for d in range(nt):
            start = pl.multiple_of((t ^ d) * rows, 16)
            part_refs[d][...] = out[pl.ds(start, rows), :]

    results = pl.pallas_call(
        without(kernel, 4 + count, len(deps)),
        out_shape=[
            shape((length, D), BF16),
            shape((length, 2 * width), F32),
            shape((length, 2 * width), BF16),
            shape((length, width), BF16),
            shape((heads, length, length), F32),
            shape((length, width), BF16),
            shape((D, SIDE), BF16),
            shape((8, D), F32),
            shape((8, HD), F32),
        ]
        + [shape((rows, D), BF16)] * nt,
        in_specs=[SMEM, VMEM, VMEM, VMEM] + [HBM] * (count + len(deps)),
        out_specs=[VMEM] * (9 + nt),
        scratch_shapes=[
            pltpu.VMEM((D, columns), BF16),
            pltpu.VMEM((length, D), BF16),
            pltpu.SemaphoreType.DMA((len(pieces),)),
        ],
        compiler_params=params(),
        cost_estimate=cost(5),
        name="attend_forward",
    )(pos, tokens, cosine, sine, *arrays, *deps)
    return results[:9], results[9:]


def attend_backward(pos, grad_rows, ffn_row, layer_sum, pieces, saved, tokens, cosine, sine, nf, nt, deps=()):
    _, qk, rot, values, probs, _, _, gains, head_gains = saved
    length = tokens.shape[0]
    block = D // nf
    rows = length // nt
    columns = pieces[0][2].shape[1]
    width = (columns - SIDE) // 4
    heads = width // HD
    more = gain_columns(rows)
    arrays = arrays_of(pieces)
    count = len(arrays)

    def kernel(pos_ref, x_ref, cos_ref, sin_ref, qk_ref, rot_ref, v_ref, prob_ref, gain_ref, head_gain_ref, ffn_ref, layer_ref, *refs):
        grad_refs, refs = refs[:nt], refs[nt:]
        piece_refs, refs = refs[:count], refs[count:]
        dqkv_ref = refs[0]
        part_refs, (w, out, db_ref, sems) = refs[1 : 1 + nt], refs[1 + nt :]
        f, t = pos_ref[0], pos_ref[1]

        def place(index, row, number):
            start = pl.multiple_of((f ^ index) * block + row, 16)
            return w.at[pl.ds(start, number), :]

        copies = start_fetch(pieces, piece_refs, place, sems)
        for d in range(nt):
            start = pl.multiple_of((t ^ d) * rows, 16)
            db_ref[pl.ds(start, rows), :] = grad_refs[d][:, :D]
        for copy in copies:
            copy.wait()
        cos, sin = cos_ref[...], sin_ref[...]
        head_gains = head_gain_ref[...]
        grad_att = dot(db_ref[...], w[:, 3 * width : 4 * width]).astype(BF16)
        gain_rows = [jnp.zeros((1, HD), F32), jnp.zeros((1, HD), F32)]
        for h in range(heads):
            span = slice(h * HD, (h + 1) * HD)
            query_low = rot_ref[:, span]
            key_low = rot_ref[:, width + h * HD : width + (h + 1) * HD]
            grad_out = grad_att[:, span]
            exact = prob_ref[h]
            grad_probs = dot_nt(grad_out, v_ref[:, span])
            row_terms = jnp.sum(exact * grad_probs, axis=-1, keepdims=True)
            grad_scores = (exact * (grad_probs - row_terms)).astype(BF16)
            dqkv_ref[:, 2 * width + h * HD : 2 * width + (h + 1) * HD] = dot_tn(
                exact.astype(BF16), grad_out
            ).astype(BF16)
            both = (dot(grad_scores, key_low), dot_tn(grad_scores, query_low))
            for which in range(2):
                span_w = slice(which * width + h * HD, which * width + (h + 1) * HD)
                grads = both[which] * (HD**-0.5)
                grads = grads * cos - half_turn(grads) * sin
                raw = qk_ref[:, span_w]
                inverse = rms_inverse(raw)
                gain_rows[which] = gain_rows[which] + jnp.sum(
                    grads * raw * inverse, axis=0, keepdims=True
                )
                dqkv_ref[:, span_w] = norm_backward(
                    raw, inverse, head_gains[2 + which : 3 + which], grads
                ).astype(BF16)
        grad_normed = dot_nt(dqkv_ref[...], w[:, : 3 * width])
        out[...] = grad_normed.astype(BF16)
        x = x_ref[...].astype(F32)
        row = jnp.sum(grad_normed * (x * rms_inverse(x)), axis=0, keepdims=True)
        lines = [row[:, k * SIDE : (k + 1) * SIDE] for row in (ffn_ref[0:1, :], row) for k in range(D // SIDE)]
        lines = lines + gain_rows
        gain_blocks = []
        for k in range(more // SIDE):
            own = lines[k * rows : (k + 1) * rows]
            blank = [jnp.zeros((rows - len(own), SIDE), F32)] if len(own) < rows else []
            gain_blocks.append(jnp.concatenate(own + blank, axis=0).astype(BF16))
        for d in range(nt):
            start = pl.multiple_of((t ^ d) * rows, 16)
            part_refs[d][:, :D] = out[pl.ds(start, rows), :]
            for k, gain_block in enumerate(gain_blocks):
                part_refs[d][:, D + k * SIDE : D + (k + 1) * SIDE] = gain_block
            part_refs[d][:, D + more :] = layer_ref[pl.ds(start, rows), :]

    results = pl.pallas_call(
        without(kernel, 12 + nt + count, len(deps)),
        out_shape=[
            shape((length, 3 * width), BF16),
        ]
        + [shape((rows, 2 * D + more), BF16)] * nt,
        in_specs=[SMEM] + [VMEM] * (11 + nt) + [HBM] * (count + len(deps)),
        out_specs=[VMEM] * (1 + nt),
        scratch_shapes=[
            pltpu.VMEM((D, columns), BF16),
            pltpu.VMEM((length, D), BF16),
            pltpu.VMEM((length, D), BF16),
            pltpu.SemaphoreType.DMA((len(pieces),)),
        ],
        compiler_params=params(),
        cost_estimate=cost(0.1),
        name="attend_backward",
    )(
        pos, tokens, cosine, sine, qk, rot, values, probs, gains, head_gains, ffn_row, layer_sum,
        *grad_rows, *arrays, *deps,
    )
    return results[0], results[1:]


def projection_gradients(pos, normed, dqkv, nf, deps=()):
    length = normed.shape[0]
    block = D // nf
    width = dqkv.shape[1]

    def kernel(pos_ref, n1_ref, dqkv_ref, keep_ref, send_ref):
        for p in range(nf):
            start = pl.multiple_of((pos_ref[0] ^ p) * block, 128)
            to = (keep_ref if p % 2 == 0 else send_ref).at[p // 2]
            to[...] = dot_tn(n1_ref[:, pl.ds(start, block)], dqkv_ref[...]).astype(BF16)

    return pl.pallas_call(
        without(kernel, 3, len(deps)),
        out_shape=[shape((nf // 2, block, width), BF16)] * 2,
        in_specs=[SMEM, VMEM, VMEM] + [HBM] * len(deps),
        out_specs=[VMEM] * 2,
        compiler_params=params(),
        cost_estimate=cost(0.1),
        name="projection_gradients",
    )(pos, normed, dqkv, *deps)


def output_gradients(pos, attended, grad_parts, normed_parts, gain_parts, group, nf, nt, deps=()):
    length, width = attended.shape
    rows = length // nt
    block = D // nf
    columns = width + SIDE
    more = gain_columns(rows)
    count = D // SIDE

    def kernel(pos_ref, att_ref, *refs):
        grad_refs, normed_refs, part_refs = refs[:nt], refs[nt : 2 * nt], refs[2 * nt : 3 * nt]
        keep_ref, send_ref, db, n2, held, gain_ref = refs[3 * nt :]
        f, t = pos_ref[0], pos_ref[1]
        for d in range(nt):
            start = pl.multiple_of((t ^ d) * rows, 16)
            db[pl.ds(start, rows), :] = grad_refs[d][...]
            n2[pl.ds(start, rows), :] = normed_refs[d][:, :D]
            held[t ^ d] = part_refs[d][:, D : D + more].astype(F32)
        total = held[0]
        for k in range(1, nt):
            total = total + held[k]
        for line in range(2 * count + 2):
            column, at = line // rows * SIDE, line % rows
            to = line // count if line < 2 * count else line - 2 * count + 2
            lane = line % count * SIDE if line < 2 * count else 0
            gain_ref[to : to + 1, lane : lane + SIDE] = total[at : at + 1, column : column + SIDE]
        lane = lanes((block, SIDE))
        sub = lax.broadcasted_iota(jnp.int32, (block, SIDE), 0)
        for p in range(nf):
            owner = f ^ p
            start = pl.multiple_of(owner * block, 128)
            to = (keep_ref if p % 2 == 0 else send_ref).at[p // 2]
            to[:, :width] = dot_tn(db[:, pl.ds(start, block)], att_ref[...]).astype(BF16)
            side = dot_tn(n2[:, pl.ds(start, block)], db[:, D:])
            for which in range(2):
                row = gain_ref[which : which + 1, pl.ds(start, block)]
                column = jnp.transpose(jnp.broadcast_to(row, (SIDE, block)))
                side = jnp.where(lane == EXPERTS + which, column, side)
            mine = (lane == owner * group + sub) & (sub < group)
            for which in range(2, 4):
                spread = jnp.where(mine, gain_ref[which : which + 1, :HD], 0.0)
                column = jnp.sum(spread, axis=1, keepdims=True)
                side = jnp.where(lane == EXPERTS + which, column, side)
            to[:, width:] = side.astype(BF16)

    return pl.pallas_call(
        without(kernel, 2 + 3 * nt, len(deps)),
        out_shape=[shape((nf // 2, block, columns), BF16)] * 2,
        in_specs=[SMEM] + [VMEM] * (1 + 3 * nt) + [HBM] * len(deps),
        out_specs=[VMEM] * 2,
        scratch_shapes=[
            pltpu.VMEM((length, D + SIDE), BF16),
            pltpu.VMEM((length, D), BF16),
            pltpu.VMEM((nt, rows, more), F32),
            pltpu.VMEM((8, D), F32),
        ],
        compiler_params=params(),
        cost_estimate=cost(0.1),
        name="output_gradients",
    )(pos, attended, *grad_parts, *normed_parts, *gain_parts, *deps)


def gain_columns(rows):
    return SIDE * -(-(2 * D // SIDE + 2) // rows)


def norm_and_route(pos, tokens, routes, parts, gains, side, nt, deps=()):
    rows = tokens.shape[0] // nt
    top = routes.shape[1]

    def kernel(pos_ref, x_ref, route_ref, gain_ref, side_ref, *refs):
        part_refs, (h_ref, next_ref, gate_ref) = refs[:nt], refs[nt:]
        h = x_ref[...].astype(F32)
        for ref in part_refs:
            h = h + ref[...].astype(F32)
        h_ref[...] = h
        n2 = (h * rms_inverse(h) * gain_ref[1:2]).astype(BF16)
        next_ref[:, :D] = n2
        logits = dot(n2, side_ref[...])
        lane = lanes((rows, SIDE))
        chosen = route_ref[:, 0:1] == lane
        for j in range(1, top):
            chosen = chosen | (route_ref[:, j : j + 1] == lane)
        highest = jnp.max(jnp.where(chosen, logits, -jnp.inf), axis=-1, keepdims=True)
        shifted = jnp.where(chosen, jnp.exp(jnp.where(chosen, logits - highest, 0.0)), 0.0)
        gates = shifted / jnp.sum(shifted, axis=-1, keepdims=True)
        gate_ref[...] = gates
        first = gates.astype(BF16).astype(F32)
        rest = (gates - first).astype(BF16).astype(F32)
        next_ref[:, D:] = (first + pltpu.roll(rest, EXPERTS, 1)).astype(BF16)

    whole = lambda i, pos: (0, 0)
    mine = lambda i, pos: (pos[1], 0)
    return pl.pallas_call(
        without(kernel, 5 + nt, len(deps)),
        out_shape=[shape((rows, D), F32), shape((rows, D + SIDE), BF16), shape((rows, SIDE), F32)],
        grid_spec=pltpu.PrefetchScalarGridSpec(
            num_scalar_prefetch=1,
            grid=(1,),
            in_specs=[
                pl.BlockSpec((rows, D), mine),
                pl.BlockSpec((rows, top), mine),
                pl.BlockSpec((8, D), whole),
                pl.BlockSpec((D, SIDE), whole),
            ]
            + [pl.BlockSpec((rows, D), whole)] * nt
            + [HBM] * len(deps),
            out_specs=[
                pl.BlockSpec((rows, D), whole),
                pl.BlockSpec((rows, D + SIDE), whole),
                pl.BlockSpec((rows, SIDE), whole),
            ],
        ),
        compiler_params=params(),
        cost_estimate=cost(100),
        name="norm_and_route",
    )(pos, tokens, routes, gains, side, *parts, *deps)


def norm_back(pos, cotangent, parts, h, gates, gains, side, nt, deps=()):
    rows = h.shape[0]

    def kernel(pos_ref, cot_ref, h_ref, gate_ref, gain_ref, side_ref, *refs):
        part_refs, (dh_ref, db_ref, row_ref) = refs[:nt], refs[nt:]
        total = part_refs[0][...].astype(F32)
        for ref in part_refs[1:]:
            total = total + ref[...].astype(F32)
        pair = total[:, D:]
        pair = pair + pltpu.roll(pair, EXPERTS, 1)
        gates = gate_ref[...]
        grads = gates * (pair - jnp.sum(gates * pair, axis=-1, keepdims=True))
        low = grads.astype(BF16)
        dn2 = total[:, :D] + dot_nt(low, side_ref[...])
        h = h_ref[...]
        inverse = rms_inverse(h)
        gain_row = jnp.sum(dn2 * h * inverse, axis=0, keepdims=True)
        row_ref[...] = jnp.broadcast_to(gain_row, (8, D))
        dh = cot_ref[...].astype(F32) + norm_backward(h, inverse, gain_ref[1:2], dn2)
        dh_ref[...] = dh
        db_ref[:, :D] = dh.astype(BF16)
        db_ref[:, D:] = low

    whole = lambda i, pos: (0, 0)
    mine = lambda i, pos: (pos[1], 0)
    return pl.pallas_call(
        without(kernel, 6 + nt, len(deps)),
        out_shape=[shape((rows, D), F32), shape((rows, D + SIDE), BF16), shape((8, D), F32)],
        grid_spec=pltpu.PrefetchScalarGridSpec(
            num_scalar_prefetch=1,
            grid=(1,),
            in_specs=[
                pl.BlockSpec((rows, D), mine),
                pl.BlockSpec((rows, D), whole),
                pl.BlockSpec((rows, SIDE), whole),
                pl.BlockSpec((8, D), whole),
                pl.BlockSpec((D, SIDE), whole),
            ]
            + [pl.BlockSpec((rows, D + SIDE), whole)] * nt
            + [HBM] * len(deps),
            out_specs=[
                pl.BlockSpec((rows, D), whole),
                pl.BlockSpec((rows, D + SIDE), whole),
                pl.BlockSpec((8, D), whole),
            ],
        ),
        compiler_params=params(),
        cost_estimate=cost(100),
        name="norm_back",
    )(pos, cotangent, h, gates, gains, side, *parts, *deps)


def last_rows(pos, tokens, parts, dh, h, gains, nt, deps=()):
    rows = dh.shape[0]
    columns = parts[0].shape[1]

    def kernel(pos_ref, x_ref, dh_ref, h_ref, gain_ref, *refs):
        part_refs, out_ref = refs[:nt], refs[nt]
        total = part_refs[0][:, :D].astype(F32)
        layer = h_ref[...] + part_refs[0][:, columns - D :].astype(F32)
        for ref in part_refs[1:]:
            total = total + ref[:, :D].astype(F32)
            layer = layer + ref[:, columns - D :].astype(F32)
        x = x_ref[...].astype(F32)
        out_ref[:, :D] = (
            dh_ref[...] + norm_backward(x, rms_inverse(x), gain_ref[0:1], total)
        ).astype(BF16)
        out_ref[:, D:] = layer.astype(BF16)

    whole = lambda i, pos: (0, 0)
    return pl.pallas_call(
        without(kernel, 5 + nt, len(deps)),
        out_shape=shape((rows, 2 * D), BF16),
        grid_spec=pltpu.PrefetchScalarGridSpec(
            num_scalar_prefetch=1,
            grid=(1,),
            in_specs=[
                pl.BlockSpec((rows, D), lambda i, pos: (pos[1], 0)),
                pl.BlockSpec((rows, D), whole),
                pl.BlockSpec((rows, D), whole),
                pl.BlockSpec((8, D), whole),
            ]
            + [pl.BlockSpec((rows, columns), whole)] * nt
            + [HBM] * len(deps),
            out_specs=pl.BlockSpec((rows, 2 * D), whole),
        ),
        compiler_params=params(),
        cost_estimate=cost(100),
        name="last_rows",
    )(pos, tokens, dh, h, gains, *parts, *deps)


def place_rows(pos, parts):
    nt = len(parts)
    rows, columns = parts[0].shape
    half = columns // 2

    def kernel(pos_ref, *refs):
        left_ref, right_ref = refs[nt:]
        for d in range(nt):
            start = pl.multiple_of((pos_ref[1] ^ d) * rows, 16)
            left_ref[pl.ds(start, rows), :] = refs[d][:, :half]
            right_ref[pl.ds(start, rows), :] = refs[d][:, half:]

    return pl.pallas_call(
        kernel,
        out_shape=[shape((rows * nt, half), parts[0].dtype)] * 2,
        in_specs=[SMEM] + [VMEM] * nt,
        out_specs=[VMEM] * 2,
        compiler_params=params(),
        cost_estimate=cost(0.1),
        name="place_rows",
    )(pos, *parts)


def spread_rows(slots, source, target, pair, number, cut):
    for begin in range(0, source.shape[2], cut):
        span = slice(begin, min(begin + cut, source.shape[2]))
        two = [dot_tn(slots[2 * pair + k], source[2 * pair + k, :, span]) for k in range(2)]
        for e in range(number):
            joined = jnp.concatenate([rows[e * CAP : (e + 1) * CAP] for rows in two], axis=0)
            target(e, span, joined)


def sum_rows(slots, results, target, pair, number, total, cut):
    at = slice(pair * 2 * CAP, (pair + 1) * 2 * CAP)
    for begin in range(0, total, cut):
        span = slice(begin, min(begin + cut, total))
        blocks = [results[e, at, span].astype(F32) for e in range(number)]
        for k in range(2):
            rows = jnp.concatenate([b[k * CAP : (k + 1) * CAP] for b in blocks], axis=0)
            target[2 * pair + k, :, span] = dot(slots[2 * pair + k], rows.astype(BF16)).astype(BF16)


def route_cotangent(pos, pieces, weights, nf, top, deps=()):
    number = weights.shape[0]
    length = sum(rows for index, _, _, _, rows in pieces if index == 0)
    slots = number * CAP
    arrays = arrays_of(pieces)
    count = len(arrays)

    def kernel(pos_ref, *refs):
        piece_refs, (slot_ref, rows_ref, cot, spread, sems, out_sems) = refs[:count], refs[count:]
        f = pos_ref[0]
        copies = start_fetch(
            pieces, piece_refs, lambda i, row, n: cot.at[i, pl.ds(row, n), :], sems, f
        )
        column = lanes((length, slots))
        expert = jnp.zeros((length, slots), jnp.int32)
        for k in range(1, number):
            expert = expert + (column >= k * CAP).astype(jnp.int32)
        rank = (column - expert * CAP + 1).astype(F32)
        expert = (expert + f * number).astype(F32)
        lower = (
            lax.broadcasted_iota(jnp.int32, (length, length), 0) >= lanes((length, length))
        ).astype(F32).astype(BF16)
        for copy in copies:
            copy.wait()

        def leave(pair):
            span = pl.ds(pl.multiple_of(pair * 2 * CAP, 16), 2 * CAP)
            return pltpu.make_async_copy(
                spread.at[:, span, :], rows_ref.at[:, span, :], out_sems.at[pair]
            )

        @pl.loop(0, nf // 2)
        def _(pair):
            for s in (2 * pair, 2 * pair + 1):
                named = cot[s, :, D:].astype(F32)
                hit = named[:, 0:1] == expert
                for j in range(1, top):
                    hit = hit | (named[:, j : j + 1] == expert)
                hit = jnp.where(hit, 1.0, 0.0)
                so_far = dot(lower, hit.astype(BF16))
                slot_ref[s] = jnp.where((so_far == rank) & (hit > 0.0), 1.0, 0.0).astype(BF16)
            at = pl.ds(pl.multiple_of(pair * 2 * CAP, 16), 2 * CAP)

            def put(k, span, rows):
                spread[k, at, span] = rows.astype(BF16)

            spread_rows(slot_ref, cot.at[:, :, :D], put, pair, number, 512)
            leave(pair).start()

        for pair in range(nf // 2):
            leave(pair).wait()

    return pl.pallas_call(
        without(kernel, 1 + count, len(deps)),
        out_shape=[
            shape((nf, length, slots), BF16),
            shape((number, nf * CAP, D), BF16),
        ],
        in_specs=[SMEM] + [HBM] * (count + len(deps)),
        out_specs=[VMEM, HBM],
        scratch_shapes=[
            pltpu.VMEM((nf, length, D + SIDE), BF16),
            pltpu.VMEM((number, nf * CAP, D), BF16),
            pltpu.SemaphoreType.DMA((len(pieces),)),
            pltpu.SemaphoreType.DMA((nf // 2,)),
        ],
        compiler_params=params(),
        cost_estimate=cost(0.1),
        name="route_cotangent",
    )(pos, *arrays, *deps)


def down_back(grad_rows, weights, deps=()):
    number, filled, _ = grad_rows.shape
    width = weights.shape[3]

    def kernel(rows_ref, w_ref, out_ref):
        for k in range(2):
            out_ref[k] = dot(rows_ref[k], w_ref[k, 0])

    return pl.pallas_call(
        without(kernel, 2, len(deps)),
        out_shape=shape((number, filled, width), F32),
        grid=(number // 2,),
        in_specs=[
            pl.BlockSpec((2, filled, D), lambda e: (e, 0, 0)),
            pl.BlockSpec((2, 1, D, width), lambda e: (e, 2, 0, 0)),
        ]
        + [HBM] * len(deps),
        out_specs=pl.BlockSpec((2, filled, width), lambda e: (e, 0, 0)),
        compiler_params=params(),
        cost_estimate=cost(0.1),
        name="down_back",
    )(grad_rows, weights, *deps)


def run_experts(pos, pieces, slot_table, down, weights, nf, cut):
    number, _, _, width = weights.shape
    length, slots = slot_table.shape[1:]
    filled = nf * CAP
    arrays = arrays_of(pieces)
    count = len(arrays)

    def kernel(pos_ref, slot_ref, down_ref, gate_w, up_w, *refs):
        piece_refs, refs = refs[:count], refs[count:]
        rows_ref, dg_ref, du_ref, hidden_ref = refs[:4]
        sums_refs = (refs[4:6], refs[6:8])
        wide, spread, gates, results, sems, rows_sem, out_sems = refs[8:]
        e = pl.program_id(0)
        f = pos_ref[0]
        rows_out = pltpu.make_async_copy(spread, rows_ref, rows_sem)

        @pl.when(e == 0)
        def _():
            copies = start_fetch(
                pieces, piece_refs, lambda i, row, n: wide.at[i, pl.ds(row, n), :], sems
            )
            for pair in range(nf // 2):
                for (index, _, _, _, _), copy in zip(pieces, copies):
                    if index // 2 == pair:
                        copy.wait()
                at = slice(pair * 2 * CAP, (pair + 1) * 2 * CAP)

                def put(k, span, rows):
                    if span.start < D:
                        spread[k, at, span] = rows.astype(BF16)
                    else:
                        lane = lanes((2 * CAP, SIDE))
                        own = f * number + k
                        gate = jnp.where((lane == own) | (lane == own + EXPERTS), rows, 0.0)
                        gates[k, at, :] = jnp.broadcast_to(
                            jnp.sum(gate, axis=-1, keepdims=True), (2 * CAP, SIDE)
                        )

                spread_rows(slot_ref, wide, put, pair, number, 512)
            rows_out.start()

        for k in range(2):
            index = 2 * e + k
            rows = spread[index]
            first, second = gate_w[k, 0], up_w[k, 0]
            gate_pre = dot(rows, first)
            up_pre = dot(rows, second)
            gate = gates[index][:, 0:1]
            sigma = jax.nn.sigmoid(gate_pre)
            swish = gate_pre * sigma
            hidden = (swish * up_pre).astype(BF16).astype(F32)
            hidden_ref[k] = (gate * hidden).astype(BF16)
            unscaled = down_ref[k]
            grad_hidden = gate * unscaled
            dg = (grad_hidden * up_pre * sigma * (1.0 + gate_pre * (1.0 - sigma))).astype(BF16)
            du = (grad_hidden * swish).astype(BF16)
            dg_ref[k] = dg
            du_ref[k] = du
            results[index, :, :D] = (dot_nt(dg, first) + dot_nt(du, second)).astype(BF16)
            pair_grad = jnp.sum(unscaled * hidden, axis=-1, keepdims=True)
            high = pair_grad.astype(BF16).astype(F32)
            lane = lanes((filled, SIDE))
            own = f * number + index
            results[index, :, D:] = jnp.where(
                lane == own, high, jnp.where(lane == own + EXPERTS, pair_grad - high, 0.0)
            ).astype(BF16)

        @pl.when(e == number // 2 - 1)
        def _():
            copies = []
            for pair in range(nf // 2):
                sum_rows(slot_ref, results, wide, pair, number, D + SIDE, 512)
                for k, to in enumerate(sums_refs):
                    index = 2 * pair + k
                    for g, span in enumerate((pl.ds(0, cut), pl.ds(cut, length - cut))):
                        copy = pltpu.make_async_copy(
                            wide.at[index, span, :], to[g].at[pair], out_sems.at[2 * index + g]
                        )
                        copy.start()
                        copies.append(copy)
            for copy in copies:
                copy.wait()
            rows_out.wait()

    return pl.pallas_call(
        kernel,
        out_shape=[
            shape((number, filled, D), BF16),
            shape((number, filled, width), BF16),
            shape((number, filled, width), BF16),
            shape((number, filled, width), BF16),
        ]
        + [shape((nf // 2, number, D + SIDE), BF16) for number in (cut, length - cut)] * 2,
        grid_spec=pltpu.PrefetchScalarGridSpec(
            num_scalar_prefetch=1,
            grid=(number // 2,),
            in_specs=[
                pl.BlockSpec((nf, length, slots), lambda e, pos: (0, 0, 0)),
                pl.BlockSpec((2, filled, width), lambda e, pos: (e, 0, 0)),
                pl.BlockSpec((2, 1, D, width), lambda e, pos: (e, 0, 0, 0)),
                pl.BlockSpec((2, 1, D, width), lambda e, pos: (e, 1, 0, 0)),
            ]
            + [HBM] * count,
            out_specs=[
                HBM,
                pl.BlockSpec((2, filled, width), lambda e, pos: (e, 0, 0)),
                pl.BlockSpec((2, filled, width), lambda e, pos: (e, 0, 0)),
                pl.BlockSpec((2, filled, width), lambda e, pos: (e, 0, 0)),
            ]
            + [HBM] * 4,
            scratch_shapes=[
                pltpu.VMEM((nf, length, D + SIDE), BF16),
                pltpu.VMEM((number, filled, D), BF16),
                pltpu.VMEM((number, filled, SIDE), F32),
                pltpu.VMEM((number, filled, D + SIDE), BF16),
                pltpu.SemaphoreType.DMA((len(pieces),)),
                pltpu.SemaphoreType.DMA,
                pltpu.SemaphoreType.DMA((2 * nf,)),
            ],
        ),
        compiler_params=params(),
        cost_estimate=cost(5),
        name="run_experts",
    )(pos, slot_table, down, weights, weights, *arrays)


def expert_outputs(pos, slot_table, hidden, weights, nt, deps=()):
    number, filled, width = hidden.shape
    nf, length, slots = slot_table.shape

    rows = length // nt

    def kernel(pos_ref, slot_ref, hidden_ref, w_ref, out_ref, results, out, sems):
        e = pl.program_id(0)
        for k in range(2):
            results[2 * e + k] = dot_nt(hidden_ref[k], w_ref[k, 0]).astype(BF16)

        @pl.when(e == number // 2 - 1)
        def _():
            copies = []
            for pair in range(nf // 2):
                sum_rows(slot_ref, results, out, pair, number, D, 512)
                for index in (2 * pair, 2 * pair + 1):
                    for d in range(nt):
                        start = pl.multiple_of((pos_ref[1] ^ d) * rows, 16)
                        copy = pltpu.make_async_copy(
                            out.at[index, pl.ds(d * rows, rows), :],
                            out_ref.at[pos_ref[0] ^ index, pl.ds(start, rows), :],
                            sems.at[index * nt + d],
                        )
                        copy.start()
                        copies.append(copy)
            for copy in copies:
                copy.wait()

    return pl.pallas_call(
        without(kernel, 4, len(deps)),
        out_shape=shape((nf, length, D), BF16),
        grid_spec=pltpu.PrefetchScalarGridSpec(
            num_scalar_prefetch=1,
            grid=(number // 2,),
            in_specs=[
                pl.BlockSpec((nf, length, slots), lambda e, pos: (0, 0, 0)),
                pl.BlockSpec((2, filled, width), lambda e, pos: (e, 0, 0)),
                pl.BlockSpec((2, 1, D, width), lambda e, pos: (e, 2, 0, 0)),
            ]
            + [HBM] * len(deps),
            out_specs=HBM,
            scratch_shapes=[
                pltpu.VMEM((number, filled, D), BF16),
                pltpu.VMEM((nf, length, D), BF16),
                pltpu.SemaphoreType.DMA((nf * nt,)),
            ],
        ),
        compiler_params=params(),
        cost_estimate=cost(0.1),
        name="expert_outputs",
    )(pos, slot_table, hidden, weights, *deps)


def expert_gradients(rows, grad_rows, dg, du, hidden, first, number, so_far=None, deps=()):
    everyone, filled, width = dg.shape

    def kernel(rows_ref, grad_ref, dg_ref, du_ref, hidden_ref, *refs):
        out_ref, done_ref = refs
        done_ref[...] = jnp.zeros_like(done_ref)
        rows = rows_ref[0]
        out_ref[0, 0] = dot_tn(rows, dg_ref[0])
        out_ref[0, 1] = dot_tn(rows, du_ref[0])
        out_ref[0, 2] = dot_tn(grad_ref[0], hidden_ref[0])

    tall = pl.BlockSpec((1, filled, D), lambda e: (first + e, 0, 0))
    thin = pl.BlockSpec((1, filled, width), lambda e: (first + e, 0, 0))
    before = [] if so_far is None else [so_far]
    return pl.pallas_call(
        without(kernel, 5, len(before) + len(deps)),
        out_shape=[shape((everyone, 3, D, width), F32), shape((8, SIDE), F32)],
        grid=(number,),
        in_specs=[tall, tall, thin, thin, thin] + [HBM] * (len(before) + len(deps)),
        out_specs=[
            pl.BlockSpec((1, 3, D, width), lambda e: (first + e, 0, 0, 0)),
            pl.BlockSpec((8, SIDE), lambda e: (0, 0)),
        ],
        input_output_aliases={5: 0} if before else {},
        compiler_params=params(),
        cost_estimate=cost(0.1),
        name="expert_gradients",
    )(rows, grad_rows, dg, du, hidden, *before, *deps)


def on_device(
    nf,
    nt,
    tokens,
    cotangent,
    routes,
    w_query,
    w_key,
    w_value,
    w_output,
    w_router,
    attn_gain,
    ffn_gain,
    query_gain,
    key_gain,
    expert_weights,
):
    length = tokens.shape[0]
    rows = length // nt
    block = D // nf
    group = query_gain.shape[0]
    top = routes.shape[1]
    f = lax.axis_index("fsdp").astype(jnp.int32)
    t = lax.axis_index("tensor").astype(jnp.int32)
    pos = jnp.stack([f, t])

    def placed(gain):
        return lax.dynamic_update_slice(jnp.zeros((block,), BF16), gain, (f * group,))[:, None]

    columns = [
        w_query,
        w_key,
        w_value,
        w_output,
        w_router,
        attn_gain[:, None],
        ffn_gain[:, None],
        placed(query_gain),
        placed(key_gain),
        jnp.zeros((block, SIDE - EXPERTS - 4), BF16),
    ]
    number = expert_weights.shape[0]
    cut = 2 * rows

    def around(block):
        return [block] + [swap(block, "tensor", nt, d) for d in range(1, nt)]

    def sent(parts):
        return [parts[0]] + [swap(parts[d], "tensor", nt, d) for d in range(1, nt)]

    if nf == 8:
        packed = [
            jnp.concatenate([part[half : half + block // 2] for part in columns], axis=1)
            for half in (0, block // 2)
        ]
        weights_near = [gather_near(part, nf) for part in packed]
    else:
        packed = jnp.concatenate(columns, axis=1)

    wide_cot = jnp.concatenate(
        [cotangent, routes.astype(BF16), jnp.zeros((length, SIDE - top), BF16)], axis=1
    )
    wide_cot = jnp.concatenate(
        [lax.dynamic_slice_in_dim(wide_cot, (t ^ d) * rows, rows, 0) for d in range(nt)], axis=0
    )
    position = jnp.arange(length, dtype=F32)[:, None]
    inverse = ROPE_BASE ** (-jnp.arange(HD // 2, dtype=F32) / (HD // 2))
    angles = position * inverse[None, :]
    cosine = jnp.concatenate([jnp.cos(angles)] * 2, axis=1)
    sine = jnp.concatenate([-jnp.sin(angles), jnp.sin(angles)], axis=1)

    if nf == 8:
        weights = gather_two(packed, weights_near, nf)
        wide_cot = join(
            [wide_cot],
            weights_near[0] + weights_near[1] + [w[2] for w in weights if w[0] == nf - 2],
        )
    else:
        weights = gather_rest(packed, gather_near(packed, nf), nf)
    all_cot = lax.all_gather(wide_cot, "fsdp", axis=0, tiled=True)
    cot = [(p, 0, all_cot, None, length) for p in range(nf)]
    saved, parts = attend_forward(pos, tokens, cosine, sine, weights, nf, nt)
    normed_one, _, _, _, _, attended, side, gains, _ = saved
    parts = sent(parts)
    h, normed_two, gates = norm_and_route(pos, tokens, routes, parts, gains, side, nt)

    normed_parts = around(normed_two)
    if nf == 8:
        blocks = [join(normed_parts[:2])]
        near = [gather_near(blocks[0], nf)]
        slot_table, cot_rows = route_cotangent(pos, cot, expert_weights, nf, top, deps=blocks)
        blocks.append(join(normed_parts[2:], deps=[slot_table]))
        near.append(gather_near(blocks[1], nf))
        down = down_back(cot_rows, expert_weights, deps=blocks[1:])
        sources = [near[0][1]] + list(relay(near[1][:1], [down]))
        n2_pieces = gather_two(blocks, near, nf, sources)
    else:
        slot_table, cot_rows = route_cotangent(pos, cot, expert_weights, nf, top)
        down = down_back(cot_rows, expert_weights)
        joined = join(normed_parts)
        n2_pieces = gather_rest(joined, gather_near(joined, nf), nf)
    n2_rows, dg, du, hidden, keep_near, keep_far, send_near, send_far = run_experts(
        pos, n2_pieces, slot_table, down, expert_weights, nf, cut
    )

    far, near = Reduce(keep_far, send_far, nf), Reduce(keep_near, send_near, nf)
    began = far.first() + near.first()
    outputs = expert_outputs(pos, slot_table, hidden, expert_weights, nt, deps=began)
    layer_sum = lax.psum_scatter(
        outputs.reshape(nf * length, D), "fsdp", scatter_dimension=0, tiled=True
    )
    went = far.second(deps=[outputs], micros=20)
    near.second(deps=went, micros=20)
    far_rows = list(far.rows(nt - 2))
    near_rows = list(near.rows(2, deps=far_rows[:1]))
    grad_parts = sent(near_rows + far_rows)
    each = number // 2

    def expert_part(k, deps=()):
        return expert_gradients(
            n2_rows, cot_rows, dg, du, hidden, k * each, each, grad_experts, deps
        )

    grad_experts = None
    grad_experts, done = expert_part(0, near_rows[:1])
    dh, db, ffn_row = norm_back(
        pos, cotangent, grad_parts, h, gates, gains, side, nt, deps=[done]
    )
    db_parts = around(db)
    grad_experts, done = expert_part(1, [db])
    dqkv, parts = attend_backward(
        pos, db_parts, ffn_row, layer_sum, weights, saved, tokens, cosine, sine, nf, nt,
        deps=[done],
    )
    parts = sent(parts)
    keep, send = projection_gradients(pos, normed_one, dqkv, nf)
    projections = Reduce(keep, send, nf)
    both_rows = last_rows(pos, tokens, parts, dh, h, gains, nt, deps=[keep])
    gathered = lax.all_gather(both_rows, "tensor", axis=0, tiled=True)
    pairs = projections.first(deps=[both_rows])
    keep, send = output_gradients(
        pos, attended, db_parts, normed_parts, parts, group, nf, nt, deps=pairs
    )
    output = Reduce(keep, send, nf)
    output.first()
    projections.second()
    output.second()
    width = attended.shape[1]
    grad_query, grad_key, grad_value = projections.columns([width] * 3)
    grad_output, side_grads = output.columns([width], SIDE)
    grad_tokens, layer_out = halve(gathered, deps=[grad_output, grad_query])
    return (
        layer_out,
        grad_tokens,
        grad_query,
        grad_key,
        grad_value,
        grad_output,
        side_grads[:EXPERTS].T,
        side_grads[EXPERTS + 1],
        side_grads[EXPERTS],
        side_grads[EXPERTS + 2, :group],
        side_grads[EXPERTS + 3, :group],
        grad_experts,
    )


def solution(mesh):
    nf, nt = mesh.shape["fsdp"], mesh.shape["tensor"]
    rows, both, line = P("fsdp", None), P("fsdp", "tensor"), P("fsdp")
    experts = P("fsdp", None, None, "tensor")
    return jax.shard_map(
        functools.partial(on_device, nf, nt),
        mesh=mesh,
        in_specs=(rows, rows, rows, both, both, both, both, rows, line, line, line, line, experts),
        out_specs=(rows, rows, both, both, both, both, rows, line, line, line, line, experts),
        check_vma=False,
    )
```

```python
import functools

import jax
import jax.numpy as jnp
from jax import lax
from jax.experimental import pallas as pl
from jax.experimental.pallas import tpu as pltpu
from jax.sharding import PartitionSpec as P

D = 2048
HD = 128
EXPERTS = 64
CAP = 40
SIDE = 128
EPSILON = 1e-06
ROPE_BASE = 10000.0

F32 = jnp.float32
BF16 = jnp.bfloat16
VMEM = pl.BlockSpec(memory_space=pltpu.VMEM)
SMEM = pl.BlockSpec(memory_space=pltpu.SMEM)
HBM = pl.BlockSpec(memory_space=pltpu.HBM)
MIB = 1024 * 1024


def shape(dims, dtype):
    return jax.ShapeDtypeStruct(tuple(dims), dtype)


def params(mebibytes=16):
    return pltpu.CompilerParams(vmem_limit_bytes=mebibytes * MIB)


def near_core(array):
    return pltpu.with_memory_space_constraint(array, pltpu.VMEM)


def cost(micros):
    return pl.CostEstimate(
        flops=int(micros * 1e9), bytes_accessed=int(micros * 3e6), transcendentals=0
    )


def in_hbm(arrays):
    return [pltpu.with_memory_space_constraint(array, pltpu.HBM) for array in arrays]


def dot(left, right):
    return jnp.dot(left, right, preferred_element_type=F32)


def dot_nt(left, right):
    return lax.dot_general(left, right, (((1,), (1,)), ((), ())), preferred_element_type=F32)


def dot_tn(left, right):
    return lax.dot_general(left, right, (((0,), (0,)), ((), ())), preferred_element_type=F32)


def rms_inverse(values):
    return lax.rsqrt(jnp.mean(values * values, axis=-1, keepdims=True) + EPSILON)


def norm_backward(values, inverse, gain, upstream):
    scaled = gain * upstream
    return inverse * scaled - values * (inverse * inverse * inverse) * jnp.mean(
        values * scaled, axis=-1, keepdims=True
    )


def half_turn(values):
    return pltpu.roll(values, HD // 2, 1)


def lanes(dims):
    return lax.broadcasted_iota(jnp.int32, dims, len(dims) - 1)


def swap(block, axis, size, step):
    return lax.ppermute(block, axis, [(i, i ^ step) for i in range(size)])


def without(kernel, at, number):
    def body(*refs):
        kernel(*refs[:at], *refs[at + number :])

    return body


def through(moves, buffer, sems):
    arriving, leaving, row = [], [], 0
    for k, (source, target) in enumerate(moves):
        here = buffer.at[pl.ds(row, source.shape[0]), :]
        arriving.append(pltpu.make_async_copy(source, here, sems.at[2 * k]))
        leaving.append(pltpu.make_async_copy(here, target, sems.at[2 * k + 1]))
        arriving[-1].start()
        row += source.shape[0]
    for arrives, leaves in zip(arriving, leaving):
        arrives.wait()
        leaves.start()
    for leaves in leaving:
        leaves.wait()


def joins(groups, deps=()):
    parts = [part for group in groups for part in group]
    count = len(parts)
    features, dtype = parts[0].shape[1], parts[0].dtype
    totals = [sum(part.shape[0] for part in group) for group in groups]

    def kernel(*refs):
        out_refs, (buffer, sems) = refs[count:-2], refs[-2:]
        moves, k = [], 0
        for out_ref, group in zip(out_refs, groups):
            row = 0
            for part in group:
                moves.append((refs[k], out_ref.at[pl.ds(row, part.shape[0]), :]))
                row, k = row + part.shape[0], k + 1
        through(moves, buffer, sems)

    return pl.pallas_call(
        without(kernel, count, len(deps)),
        out_shape=[shape((total, features), dtype) for total in totals],
        in_specs=[HBM] * (count + len(deps)),
        out_specs=[HBM] * len(groups),
        scratch_shapes=[
            pltpu.VMEM((sum(totals), features), dtype),
            pltpu.SemaphoreType.DMA((2 * count,)),
        ],
        compiler_params=params(60),
        cost_estimate=cost(0.1),
        name="joins",
    )(*parts, *deps)


def join(parts, deps=()):
    return joins([parts], deps)[0]


def relay(parts, deps):
    return joins([[part] for part in parts], deps)


def halves(upper_of, lower_of, deps=()):
    rows, features = upper_of.shape
    half = rows // 2

    def kernel(upper_ref, lower_ref, upper_out, lower_out, buffer, sems):
        through(
            [
                (upper_ref.at[pl.ds(0, half), :], upper_out),
                (lower_ref.at[pl.ds(half, half), :], lower_out),
            ],
            buffer,
            sems,
        )

    return pl.pallas_call(
        without(kernel, 2, len(deps)),
        out_shape=[shape((half, features), upper_of.dtype)] * 2,
        in_specs=[HBM] * (2 + len(deps)),
        out_specs=[HBM] * 2,
        scratch_shapes=[
            pltpu.VMEM((rows, features), upper_of.dtype),
            pltpu.SemaphoreType.DMA((4,)),
        ],
        compiler_params=params(),
        cost_estimate=cost(0.1),
        name="halves",
    )(upper_of, lower_of, *deps)


def gather_near(block, size):
    if size != 8:
        return [swap(block, "fsdp", size, p) for p in range(1, size)]
    return [swap(block, "fsdp", size, 2), swap(block, "fsdp", size, 4)]


def gather_rest(block, near, size, deps=()):
    rows = block.shape[0]
    if size != 8:
        return [(p, 0, part, 0, rows) for p, part in enumerate([block] + near)]
    half = rows // 2
    upper, lower = halves(near[1], near[0], deps)
    front = swap(upper, "fsdp", size, 2)
    back = swap(lower, "fsdp", size, 4)
    pieces = []
    for k, part in enumerate([block] + near):
        pieces.append((2 * k, 0, part, 0, rows))
        pieces.append((2 * k + 1, 0, swap(part, "fsdp", size, 1), 0, rows))
    for row, part in ((0, front), (half, back)):
        pieces.append((6, row, part, 0, half))
        pieces.append((7, row, swap(part, "fsdp", size, 1), 0, half))
    return pieces


def gather_two(blocks, near, size, sources=None):
    pieces = []
    start = 0
    sources = sources or [near[0][1], near[1][0]]
    for block, (along_x, along_y), source, step in zip(blocks, near, sources, (2, 4)):
        rows = block.shape[0]
        last = swap(source, "fsdp", size, step)
        for index, part in ((0, block), (2, along_x), (4, along_y), (6, last)):
            pieces.append((index, start, part, 0, rows))
            pieces.append((index + 1, start, swap(part, "fsdp", size, 1), 0, rows))
        start += rows
    return pieces


def arrays_of(pieces):
    found = []
    for _, _, part, _, _ in pieces:
        if not any(part is other for other in found):
            found.append(part)
    return found


def start_fetch(pieces, refs, place, sems, own=None):
    arrays = arrays_of(pieces)
    copies = []
    for k, (index, row, part, at, rows) in enumerate(pieces):
        ref = next(ref for other, ref in zip(arrays, refs) if other is part)
        if at is None:
            at = pl.multiple_of((own ^ index) * rows, 16)
        copy = pltpu.make_async_copy(
            ref.at[pl.ds(at, rows), :], place(index, row, rows), sems.at[k]
        )
        copy.start()
        copies.append(copy)
    return copies


def pair_sums(keep, got, deps=()):
    _, rows, columns = keep.shape
    half = rows // 2

    def kernel(keep_ref, got_ref, out_x, out_y, held, sems):
        upper, lower = pl.ds(0, half), pl.ds(half, half)
        places = [(1, upper), (3, upper), (2, lower), (3, lower)]
        copies = fetch_parts([keep_ref.at[place] for place in places], held, sems)
        for k, place in enumerate(places):
            copies[k].wait()
            (out_x, out_y)[k // 2][k % 2] = (
                held[k].astype(F32) + got_ref[place].astype(F32)
            ).astype(BF16)

    return pl.pallas_call(
        without(kernel, 2, len(deps)),
        out_shape=[shape((2, half, columns), BF16)] * 2,
        in_specs=[HBM, VMEM] + [HBM] * len(deps),
        out_specs=[VMEM] * 2,
        scratch_shapes=[pltpu.VMEM((4, half, columns), BF16), pltpu.SemaphoreType.DMA((4,))],
        compiler_params=params(),
        cost_estimate=cost(0.1),
        name="pair_sums",
    )(*in_hbm([keep]), near_core(got), *in_hbm(deps))


def fetch_parts(parts, buffer, sems):
    copies = []
    for k, part in enumerate(parts):
        copies.append(pltpu.make_async_copy(part, buffer.at[k], sems.at[k]))
        copies[-1].start()
    return copies


def next_sums(keep, got, from_x, from_y, deps, micros):
    _, rows, columns = keep.shape
    half = rows // 2

    def kernel(keep_ref, got_ref, new_x, new_y, out_x, out_y, held, sems):
        upper, lower = pl.ds(0, half), pl.ds(half, half)
        places = [(2, upper), (1, lower)]
        copies = fetch_parts([keep_ref.at[place] for place in places], held, sems)
        for k, (new, out) in enumerate(((new_x, out_x), (new_y, out_y))):
            copies[k].wait()
            out[...] = (
                held[k].astype(F32) + got_ref[places[k]].astype(F32) + new[1].astype(F32)
            ).astype(BF16)

    return pl.pallas_call(
        without(kernel, 4, len(deps)),
        out_shape=[shape((half, columns), BF16)] * 2,
        in_specs=[HBM, VMEM, VMEM, VMEM] + [HBM] * len(deps),
        out_specs=[VMEM] * 2,
        scratch_shapes=[pltpu.VMEM((2, half, columns), BF16), pltpu.SemaphoreType.DMA((2,))],
        compiler_params=params(),
        cost_estimate=cost(micros),
        name="next_sums",
    )(*in_hbm([keep]), near_core(got), near_core(from_x), near_core(from_y), *in_hbm(deps))


def last_sums(keep, got, from_x, from_y, last_x, last_y, count, deps=()):
    _, rows, columns = keep.shape
    half = rows // 2
    part = rows // count
    each = half // part

    def kernel(keep_ref, got_ref, new_x, end_x, new_y, end_y, *refs):
        out_refs, (held, sems) = refs[:count], refs[count:]
        upper, lower = pl.ds(0, half), pl.ds(half, half)
        places = [(0, upper), (0, lower)]
        copies = fetch_parts([keep_ref.at[place] for place in places], held, sems)
        for k in range(count):
            side = k // each
            new, end = (new_x, end_x) if side == 0 else (new_y, end_y)
            if k % each == 0:
                copies[side].wait()
            first = (k % each) * part
            span = slice(first, first + part)
            from_got = slice(side * half + first, side * half + first + part)
            total = held[side, span].astype(F32) + got_ref[0, from_got].astype(F32)
            total = total + new[0, span].astype(F32) + end[span].astype(F32)
            out_refs[k][...] = total.astype(BF16)

    return pl.pallas_call(
        without(kernel, 6, len(deps)),
        out_shape=[shape((part, columns), BF16)] * count,
        in_specs=[HBM] + [VMEM] * 5 + [HBM] * len(deps),
        out_specs=[VMEM] * count,
        scratch_shapes=[pltpu.VMEM((2, half, columns), BF16), pltpu.SemaphoreType.DMA((2,))],
        compiler_params=params(),
        cost_estimate=cost(20),
        name="last_sums",
    )(
        *in_hbm([keep]), near_core(got), near_core(from_x), near_core(last_x), near_core(from_y), near_core(last_y),
        *in_hbm(deps),
    )


def column_sums(keep, got, from_x, from_y, last_x, last_y, widths, turned):
    _, rows, columns = keep.shape
    half = rows // 2

    def kernel(keep_x, got_x, new_x, end_x, keep_y, got_y, new_y, end_y, *out_refs):
        for k, refs in enumerate(((keep_x, got_x, new_x, end_x), (keep_y, got_y, new_y, end_y))):
            span = slice(k * half, (k + 1) * half)
            total = refs[0][0].astype(F32)
            for ref in refs[1:3]:
                total = total + ref[0].astype(F32)
            total = total + refs[3][...].astype(F32)
            column = 0
            for width, out_ref in zip(widths, out_refs):
                out_ref[span, :] = total[:, column : column + width]
                column += width
            if turned:
                out_refs[-1][:, span] = jnp.transpose(total[:, column : column + turned])

    block = (1, half, columns)
    first = pl.BlockSpec(block, lambda j: (0, 0, 0))
    second = pl.BlockSpec(block, lambda j: (0, 1, 0))
    end = pl.BlockSpec((half, columns), lambda j: (0, 0))
    shapes = [(rows, width) for width in widths] + [(turned, rows)] * (turned > 0)
    return pl.pallas_call(
        kernel,
        out_shape=[shape(dims, F32) for dims in shapes],
        grid=(1,),
        in_specs=[first, first, first, end, second, second, first, end],
        out_specs=[pl.BlockSpec(dims, lambda j: (0, 0)) for dims in shapes],
        compiler_params=params(),
        cost_estimate=cost(0.1),
        name="column_sums",
    )(keep, got, from_x, last_x, keep, got, from_y, last_y)


def halve(array, deps=()):
    rows, columns = array.shape
    half = columns // 2

    def kernel(ref, left_ref, right_ref):
        left_ref[...] = ref[:, :half]
        right_ref[...] = ref[:, half:]

    return pl.pallas_call(
        without(kernel, 1, len(deps)),
        out_shape=[shape((rows, half), array.dtype)] * 2,
        grid=(2,),
        in_specs=[pl.BlockSpec((rows // 2, columns), lambda j: (j, 0))] + [HBM] * len(deps),
        out_specs=[pl.BlockSpec((rows // 2, half), lambda j: (j, 0))] * 2,
        compiler_params=params(60),
        cost_estimate=cost(0.1),
        name="halve",
    )(array, *deps)


class Reduce:
    def __init__(self, keep, send, size):
        self.keep, self.send, self.size = keep, send, size
        if size == 8:
            self.got = swap(send, "fsdp", size, 1)

    def first(self, deps=()):
        if self.size != 8:
            return []
        self.pair = pair_sums(self.keep, self.got, deps)
        self.from_x = swap(self.pair[0], "fsdp", self.size, 2)
        self.from_y = swap(self.pair[1], "fsdp", self.size, 4)
        return list(self.pair[:1])

    def second(self, deps=(), micros=0.1):
        if self.size != 8:
            return []
        sums = next_sums(self.keep, self.got, self.from_x, self.from_y, deps, micros)
        self.last_x = swap(sums[0], "fsdp", self.size, 4)
        self.last_y = swap(sums[1], "fsdp", self.size, 2)
        return list(sums[:1])

    def total(self):
        if self.size != 8:
            total = self.keep[0].astype(F32)
            for p in range(1, self.size):
                block = self.keep[p // 2] if p % 2 == 0 else self.send[p // 2]
                total = total + swap(block, "fsdp", self.size, p).astype(F32)
            return total
        half = self.keep.shape[1] // 2
        sums = []
        for rows, new, last in (
            (slice(0, half), self.from_x, self.last_x),
            (slice(half, None), self.from_y, self.last_y),
        ):
            sums.append(
                self.keep[0, rows].astype(F32)
                + self.got[0, rows].astype(F32)
                + new[0].astype(F32)
                + last.astype(F32)
            )
        return jnp.concatenate(sums, axis=0)

    def columns(self, widths, turned=0):
        if self.size == 8:
            return column_sums(
                self.keep, self.got, self.from_x, self.from_y, self.last_x, self.last_y, widths, turned
            )
        total, found, column = self.total(), [], 0
        for width in widths:
            found.append(total[:, column : column + width])
            column += width
        return found + [total[:, column : column + turned].T] * (turned > 0)

    def rows(self, count, deps=()):
        if self.size != 8:
            return jnp.split(self.total().astype(BF16), count, axis=0)
        return last_sums(
            self.keep, self.got, self.from_x, self.from_y, self.last_x, self.last_y, count, deps
        )


def attend_forward(pos, tokens, cosine, sine, pieces, nf, nt, deps=()):
    length = tokens.shape[0]
    block = D // nf
    rows = length // nt
    columns = pieces[0][2].shape[1]
    width = (columns - SIDE) // 4
    heads = width // HD
    arrays = arrays_of(pieces)
    count = len(arrays)

    def kernel(pos_ref, x_ref, cos_ref, sin_ref, *refs):
        piece_refs, refs = refs[:count], refs[count:]
        n1_ref, qk_ref, rot_ref, v_ref, prob_ref, att_ref, side_ref, gain_ref, head_gain_ref = refs[:9]
        part_refs, (w, out, sems) = refs[9 : 9 + nt], refs[9 + nt :]
        f, t = pos_ref[0], pos_ref[1]

        def place(index, row, number):
            start = pl.multiple_of((f ^ index) * block + row, 16)
            return w.at[pl.ds(start, number), :]

        copies = start_fetch(pieces, piece_refs, place, sems)
        x = x_ref[...].astype(F32)
        normed = x * rms_inverse(x)
        for copy in copies:
            copy.wait()
        side_ref[...] = w[:, 4 * width :]
        turned = jnp.transpose(w[:, 4 * width :].astype(F32))
        gain_ref[...] = turned[EXPERTS : EXPERTS + 8]
        head_rows = turned[EXPERTS : EXPERTS + 8, :block]
        for p in range(1, nf):
            head_rows = head_rows + turned[EXPERTS : EXPERTS + 8, p * block : (p + 1) * block]
        head_gains = head_rows[:, :HD]
        head_gain_ref[...] = head_gains
        n1 = (normed * turned[EXPERTS : EXPERTS + 1]).astype(BF16)
        n1_ref[...] = n1
        raw = dot(n1, w[:, : 3 * width])
        qk_ref[...] = raw[:, : 2 * width]
        v_ref[...] = raw[:, 2 * width :].astype(BF16)
        cos, sin = cos_ref[...], sin_ref[...]
        for h in range(heads):
            span = slice(h * HD, (h + 1) * HD)
            turned_rows = []
            for which in range(2):
                values = raw[:, which * width + h * HD : which * width + (h + 1) * HD]
                scaled = values * rms_inverse(values) * head_gains[2 + which : 3 + which]
                low = (scaled * cos + half_turn(scaled) * sin).astype(BF16)
                rot_ref[:, which * width + h * HD : which * width + (h + 1) * HD] = low
                turned_rows.append(low)
            scores = dot_nt(turned_rows[0], turned_rows[1]) * (HD**-0.5)
            shifted = jnp.exp(scores - jnp.max(scores, axis=-1, keepdims=True))
            probs = shifted / jnp.sum(shifted, axis=-1, keepdims=True)
            prob_ref[h] = probs
            att_ref[:, span] = dot(probs.astype(BF16), v_ref[:, span]).astype(BF16)
        out[...] = dot_nt(att_ref[...], w[:, 3 * width : 4 * width]).astype(BF16)
        for d in range(nt):
            start = pl.multiple_of((t ^ d) * rows, 16)
            part_refs[d][...] = out[pl.ds(start, rows), :]

    results = pl.pallas_call(
        without(kernel, 4 + count, len(deps)),
        out_shape=[
            shape((length, D), BF16),
            shape((length, 2 * width), F32),
            shape((length, 2 * width), BF16),
            shape((length, width), BF16),
            shape((heads, length, length), F32),
            shape((length, width), BF16),
            shape((D, SIDE), BF16),
            shape((8, D), F32),
            shape((8, HD), F32),
        ]
        + [shape((rows, D), BF16)] * nt,
        in_specs=[SMEM, VMEM, VMEM, VMEM] + [HBM] * (count + len(deps)),
        out_specs=[VMEM] * (9 + nt),
        scratch_shapes=[
            pltpu.VMEM((D, columns), BF16),
            pltpu.VMEM((length, D), BF16),
            pltpu.SemaphoreType.DMA((len(pieces),)),
        ],
        compiler_params=params(60),
        cost_estimate=cost(5),
        name="attend_forward",
    )(pos, tokens, cosine, sine, *arrays, *deps)
    return results[:9], results[9:]


def attend_backward(pos, grad_rows, ffn_row, layer_sum, pieces, saved, tokens, cosine, sine, nf, nt, deps=()):
    _, qk, rot, values, probs, _, _, gains, head_gains = saved
    length = tokens.shape[0]
    block = D // nf
    rows = length // nt
    columns = pieces[0][2].shape[1]
    width = (columns - SIDE) // 4
    heads = width // HD
    more = gain_columns(rows)
    arrays = arrays_of(pieces)
    count = len(arrays)

    def kernel(pos_ref, x_ref, cos_ref, sin_ref, qk_ref, rot_ref, v_ref, prob_ref, gain_ref, head_gain_ref, ffn_ref, layer_ref, *refs):
        grad_refs, refs = refs[:nt], refs[nt:]
        piece_refs, refs = refs[:count], refs[count:]
        dqkv_ref = refs[0]
        part_refs, (w, out, db_ref, sems) = refs[1 : 1 + nt], refs[1 + nt :]
        f, t = pos_ref[0], pos_ref[1]

        def place(index, row, number):
            start = pl.multiple_of((f ^ index) * block + row, 16)
            return w.at[pl.ds(start, number), :]

        copies = start_fetch(pieces, piece_refs, place, sems)
        for d in range(nt):
            start = pl.multiple_of((t ^ d) * rows, 16)
            db_ref[pl.ds(start, rows), :] = grad_refs[d][:, :D]
        for copy in copies:
            copy.wait()
        cos, sin = cos_ref[...], sin_ref[...]
        head_gains = head_gain_ref[...]
        grad_att = dot(db_ref[...], w[:, 3 * width : 4 * width]).astype(BF16)
        gain_rows = [jnp.zeros((1, HD), F32), jnp.zeros((1, HD), F32)]
        for h in range(heads):
            span = slice(h * HD, (h + 1) * HD)
            query_low = rot_ref[:, span]
            key_low = rot_ref[:, width + h * HD : width + (h + 1) * HD]
            grad_out = grad_att[:, span]
            exact = prob_ref[h]
            grad_probs = dot_nt(grad_out, v_ref[:, span])
            row_terms = jnp.sum(exact * grad_probs, axis=-1, keepdims=True)
            grad_scores = (exact * (grad_probs - row_terms)).astype(BF16)
            dqkv_ref[:, 2 * width + h * HD : 2 * width + (h + 1) * HD] = dot_tn(
                exact.astype(BF16), grad_out
            ).astype(BF16)
            both = (dot(grad_scores, key_low), dot_tn(grad_scores, query_low))
            for which in range(2):
                span_w = slice(which * width + h * HD, which * width + (h + 1) * HD)
                grads = both[which] * (HD**-0.5)
                grads = grads * cos - half_turn(grads) * sin
                raw = qk_ref[:, span_w]
                inverse = rms_inverse(raw)
                gain_rows[which] = gain_rows[which] + jnp.sum(
                    grads * raw * inverse, axis=0, keepdims=True
                )
                dqkv_ref[:, span_w] = norm_backward(
                    raw, inverse, head_gains[2 + which : 3 + which], grads
                ).astype(BF16)
        grad_normed = dot_nt(dqkv_ref[...], w[:, : 3 * width])
        out[...] = grad_normed.astype(BF16)
        x = x_ref[...].astype(F32)
        row = jnp.sum(grad_normed * (x * rms_inverse(x)), axis=0, keepdims=True)
        lines = [row[:, k * SIDE : (k + 1) * SIDE] for row in (ffn_ref[0:1, :], row) for k in range(D // SIDE)]
        lines = lines + gain_rows
        gain_blocks = []
        for k in range(more // SIDE):
            own = lines[k * rows : (k + 1) * rows]
            blank = [jnp.zeros((rows - len(own), SIDE), F32)] if len(own) < rows else []
            gain_blocks.append(jnp.concatenate(own + blank, axis=0).astype(BF16))
        for d in range(nt):
            start = pl.multiple_of((t ^ d) * rows, 16)
            part_refs[d][:, :D] = out[pl.ds(start, rows), :]
            for k, gain_block in enumerate(gain_blocks):
                part_refs[d][:, D + k * SIDE : D + (k + 1) * SIDE] = gain_block
            part_refs[d][:, D + more :] = layer_ref[pl.ds(start, rows), :]

    results = pl.pallas_call(
        without(kernel, 12 + nt + count, len(deps)),
        out_shape=[
            shape((length, 3 * width), BF16),
        ]
        + [shape((rows, 2 * D + more), BF16)] * nt,
        in_specs=[SMEM] + [VMEM] * (11 + nt) + [HBM] * (count + len(deps)),
        out_specs=[VMEM] * (1 + nt),
        scratch_shapes=[
            pltpu.VMEM((D, columns), BF16),
            pltpu.VMEM((length, D), BF16),
            pltpu.VMEM((length, D), BF16),
            pltpu.SemaphoreType.DMA((len(pieces),)),
        ],
        compiler_params=params(60),
        cost_estimate=cost(0.1),
        name="attend_backward",
    )(
        pos, tokens, cosine, sine, qk, rot, values, probs, gains, head_gains, ffn_row, layer_sum,
        *grad_rows, *arrays, *deps,
    )
    return results[0], results[1:]


def projection_gradients(pos, normed, dqkv, nf, deps=()):
    length = normed.shape[0]
    block = D // nf
    width = dqkv.shape[1]

    def kernel(pos_ref, n1_ref, dqkv_ref, keep_ref, send_ref):
        for p in range(nf):
            start = pl.multiple_of((pos_ref[0] ^ p) * block, 128)
            to = (keep_ref if p % 2 == 0 else send_ref).at[p // 2]
            to[...] = dot_tn(n1_ref[:, pl.ds(start, block)], dqkv_ref[...]).astype(BF16)

    return pl.pallas_call(
        without(kernel, 3, len(deps)),
        out_shape=[shape((nf // 2, block, width), BF16)] * 2,
        in_specs=[SMEM, VMEM, VMEM] + [HBM] * len(deps),
        out_specs=[VMEM] * 2,
        compiler_params=params(40),
        cost_estimate=cost(0.1),
        name="projection_gradients",
    )(pos, normed, dqkv, *deps)


def output_gradients(pos, attended, grad_parts, normed_parts, gain_parts, group, nf, nt, deps=()):
    length, width = attended.shape
    rows = length // nt
    block = D // nf
    columns = width + SIDE
    more = gain_columns(rows)
    count = D // SIDE

    def kernel(pos_ref, att_ref, *refs):
        grad_refs, normed_refs, part_refs = refs[:nt], refs[nt : 2 * nt], refs[2 * nt : 3 * nt]
        keep_ref, send_ref, db, n2, held, gain_ref = refs[3 * nt :]
        f, t = pos_ref[0], pos_ref[1]
        for d in range(nt):
            start = pl.multiple_of((t ^ d) * rows, 16)
            db[pl.ds(start, rows), :] = grad_refs[d][...]
            n2[pl.ds(start, rows), :] = normed_refs[d][:, :D]
            held[t ^ d] = part_refs[d][:, D : D + more].astype(F32)
        total = held[0]
        for k in range(1, nt):
            total = total + held[k]
        for line in range(2 * count + 2):
            column, at = line // rows * SIDE, line % rows
            to = line // count if line < 2 * count else line - 2 * count + 2
            lane = line % count * SIDE if line < 2 * count else 0
            gain_ref[to : to + 1, lane : lane + SIDE] = total[at : at + 1, column : column + SIDE]
        lane = lanes((block, SIDE))
        sub = lax.broadcasted_iota(jnp.int32, (block, SIDE), 0)
        for p in range(nf):
            owner = f ^ p
            start = pl.multiple_of(owner * block, 128)
            to = (keep_ref if p % 2 == 0 else send_ref).at[p // 2]
            to[:, :width] = dot_tn(db[:, pl.ds(start, block)], att_ref[...]).astype(BF16)
            side = dot_tn(n2[:, pl.ds(start, block)], db[:, D:])
            for which in range(2):
                row = gain_ref[which : which + 1, pl.ds(start, block)]
                column = jnp.transpose(jnp.broadcast_to(row, (SIDE, block)))
                side = jnp.where(lane == EXPERTS + which, column, side)
            mine = (lane == owner * group + sub) & (sub < group)
            for which in range(2, 4):
                spread = jnp.where(mine, gain_ref[which : which + 1, :HD], 0.0)
                column = jnp.sum(spread, axis=1, keepdims=True)
                side = jnp.where(lane == EXPERTS + which, column, side)
            to[:, width:] = side.astype(BF16)

    return pl.pallas_call(
        without(kernel, 2 + 3 * nt, len(deps)),
        out_shape=[shape((nf // 2, block, columns), BF16)] * 2,
        in_specs=[SMEM] + [VMEM] * (1 + 3 * nt) + [HBM] * len(deps),
        out_specs=[VMEM] * 2,
        scratch_shapes=[
            pltpu.VMEM((length, D + SIDE), BF16),
            pltpu.VMEM((length, D), BF16),
            pltpu.VMEM((nt, rows, more), F32),
            pltpu.VMEM((8, D), F32),
        ],
        compiler_params=params(40),
        cost_estimate=cost(0.1),
        name="output_gradients",
    )(pos, attended, *grad_parts, *normed_parts, *gain_parts, *deps)


def gain_columns(rows):
    return SIDE * -(-(2 * D // SIDE + 2) // rows)


def norm_and_route(pos, tokens, routes, parts, gains, side, nt, deps=()):
    rows = tokens.shape[0] // nt
    top = routes.shape[1]

    def kernel(pos_ref, x_ref, route_ref, gain_ref, side_ref, *refs):
        part_refs, (h_ref, next_ref, gate_ref) = refs[:nt], refs[nt:]
        h = x_ref[...].astype(F32)
        for ref in part_refs:
            h = h + ref[...].astype(F32)
        h_ref[...] = h
        n2 = (h * rms_inverse(h) * gain_ref[1:2]).astype(BF16)
        next_ref[:, :D] = n2
        logits = dot(n2, side_ref[...])
        lane = lanes((rows, SIDE))
        chosen = route_ref[:, 0:1] == lane
        for j in range(1, top):
            chosen = chosen | (route_ref[:, j : j + 1] == lane)
        highest = jnp.max(jnp.where(chosen, logits, -jnp.inf), axis=-1, keepdims=True)
        shifted = jnp.where(chosen, jnp.exp(jnp.where(chosen, logits - highest, 0.0)), 0.0)
        gates = shifted / jnp.sum(shifted, axis=-1, keepdims=True)
        gate_ref[...] = gates
        first = gates.astype(BF16).astype(F32)
        rest = (gates - first).astype(BF16).astype(F32)
        next_ref[:, D:] = (first + pltpu.roll(rest, EXPERTS, 1)).astype(BF16)

    whole = lambda i, pos: (0, 0)
    mine = lambda i, pos: (pos[1], 0)
    return pl.pallas_call(
        without(kernel, 5 + nt, len(deps)),
        out_shape=[shape((rows, D), F32), shape((rows, D + SIDE), BF16), shape((rows, SIDE), F32)],
        grid_spec=pltpu.PrefetchScalarGridSpec(
            num_scalar_prefetch=1,
            grid=(1,),
            in_specs=[
                pl.BlockSpec((rows, D), mine),
                pl.BlockSpec((rows, top), mine),
                pl.BlockSpec((8, D), whole),
                pl.BlockSpec((D, SIDE), whole),
            ]
            + [pl.BlockSpec((rows, D), whole)] * nt
            + [HBM] * len(deps),
            out_specs=[
                pl.BlockSpec((rows, D), whole),
                pl.BlockSpec((rows, D + SIDE), whole),
                pl.BlockSpec((rows, SIDE), whole),
            ],
        ),
        compiler_params=params(),
        cost_estimate=cost(100),
        name="norm_and_route",
    )(pos, tokens, routes, gains, side, *parts, *deps)


def norm_back(pos, cotangent, parts, h, gates, gains, side, nt, deps=()):
    rows = h.shape[0]

    def kernel(pos_ref, cot_ref, h_ref, gate_ref, gain_ref, side_ref, *refs):
        part_refs, (dh_ref, db_ref, row_ref) = refs[:nt], refs[nt:]
        total = part_refs[0][...].astype(F32)
        for ref in part_refs[1:]:
            total = total + ref[...].astype(F32)
        pair = total[:, D:]
        pair = pair + pltpu.roll(pair, EXPERTS, 1)
        gates = gate_ref[...]
        grads = gates * (pair - jnp.sum(gates * pair, axis=-1, keepdims=True))
        low = grads.astype(BF16)
        dn2 = total[:, :D] + dot_nt(low, side_ref[...])
        h = h_ref[...]
        inverse = rms_inverse(h)
        gain_row = jnp.sum(dn2 * h * inverse, axis=0, keepdims=True)
        row_ref[...] = jnp.broadcast_to(gain_row, (8, D))
        dh = cot_ref[...].astype(F32) + norm_backward(h, inverse, gain_ref[1:2], dn2)
        dh_ref[...] = dh
        db_ref[:, :D] = dh.astype(BF16)
        db_ref[:, D:] = low

    whole = lambda i, pos: (0, 0)
    mine = lambda i, pos: (pos[1], 0)
    return pl.pallas_call(
        without(kernel, 6 + nt, len(deps)),
        out_shape=[shape((rows, D), F32), shape((rows, D + SIDE), BF16), shape((8, D), F32)],
        grid_spec=pltpu.PrefetchScalarGridSpec(
            num_scalar_prefetch=1,
            grid=(1,),
            in_specs=[
                pl.BlockSpec((rows, D), mine),
                pl.BlockSpec((rows, D), whole),
                pl.BlockSpec((rows, SIDE), whole),
                pl.BlockSpec((8, D), whole),
                pl.BlockSpec((D, SIDE), whole),
            ]
            + [pl.BlockSpec((rows, D + SIDE), whole)] * nt
            + [HBM] * len(deps),
            out_specs=[
                pl.BlockSpec((rows, D), whole),
                pl.BlockSpec((rows, D + SIDE), whole),
                pl.BlockSpec((8, D), whole),
            ],
        ),
        compiler_params=params(),
        cost_estimate=cost(100),
        name="norm_back",
    )(pos, cotangent, h, gates, gains, side, *parts, *in_hbm(deps))


def last_rows(pos, tokens, parts, dh, h, gains, nt, deps=()):
    rows = dh.shape[0]
    columns = parts[0].shape[1]

    def kernel(pos_ref, x_ref, dh_ref, h_ref, gain_ref, *refs):
        part_refs, out_ref = refs[:nt], refs[nt]
        total = part_refs[0][:, :D].astype(F32)
        layer = h_ref[...] + part_refs[0][:, columns - D :].astype(F32)
        for ref in part_refs[1:]:
            total = total + ref[:, :D].astype(F32)
            layer = layer + ref[:, columns - D :].astype(F32)
        x = x_ref[...].astype(F32)
        out_ref[:, :D] = (
            dh_ref[...] + norm_backward(x, rms_inverse(x), gain_ref[0:1], total)
        ).astype(BF16)
        out_ref[:, D:] = layer.astype(BF16)

    whole = lambda i, pos: (0, 0)
    return pl.pallas_call(
        without(kernel, 5 + nt, len(deps)),
        out_shape=shape((rows, 2 * D), BF16),
        grid_spec=pltpu.PrefetchScalarGridSpec(
            num_scalar_prefetch=1,
            grid=(1,),
            in_specs=[
                pl.BlockSpec((rows, D), lambda i, pos: (pos[1], 0)),
                pl.BlockSpec((rows, D), whole),
                pl.BlockSpec((rows, D), whole),
                pl.BlockSpec((8, D), whole),
            ]
            + [pl.BlockSpec((rows, columns), whole)] * nt
            + [HBM] * len(deps),
            out_specs=pl.BlockSpec((rows, 2 * D), whole),
        ),
        compiler_params=params(60),
        cost_estimate=cost(100),
        name="last_rows",
    )(pos, tokens, dh, h, gains, *parts, *deps)


def place_rows(pos, parts):
    nt = len(parts)
    rows, columns = parts[0].shape
    half = columns // 2

    def kernel(pos_ref, *refs):
        left_ref, right_ref = refs[nt:]
        for d in range(nt):
            start = pl.multiple_of((pos_ref[1] ^ d) * rows, 16)
            left_ref[pl.ds(start, rows), :] = refs[d][:, :half]
            right_ref[pl.ds(start, rows), :] = refs[d][:, half:]

    return pl.pallas_call(
        kernel,
        out_shape=[shape((rows * nt, half), parts[0].dtype)] * 2,
        in_specs=[SMEM] + [VMEM] * nt,
        out_specs=[VMEM] * 2,
        compiler_params=params(),
        cost_estimate=cost(0.1),
        name="place_rows",
    )(pos, *parts)


def spread_rows(slots, source, target, pair, number, cut):
    for begin in range(0, source.shape[2], cut):
        span = slice(begin, min(begin + cut, source.shape[2]))
        two = [dot_tn(slots[2 * pair + k], source[2 * pair + k, :, span]) for k in range(2)]
        for e in range(number):
            joined = jnp.concatenate([rows[e * CAP : (e + 1) * CAP] for rows in two], axis=0)
            target(e, span, joined)


def sum_rows(slots, results, target, pair, number, total, cut):
    at = slice(pair * 2 * CAP, (pair + 1) * 2 * CAP)
    for begin in range(0, total, cut):
        span = slice(begin, min(begin + cut, total))
        blocks = [results[e, at, span].astype(F32) for e in range(number)]
        for k in range(2):
            rows = jnp.concatenate([b[k * CAP : (k + 1) * CAP] for b in blocks], axis=0)
            target[2 * pair + k, :, span] = dot(slots[2 * pair + k], rows.astype(BF16)).astype(BF16)


def route_cotangent(pos, pieces, weights, nf, top, deps=()):
    number = weights.shape[0]
    length = sum(rows for index, _, _, _, rows in pieces if index == 0)
    slots = number * CAP
    arrays = arrays_of(pieces)
    count = len(arrays)

    def kernel(pos_ref, *refs):
        piece_refs, (slot_ref, rows_ref, cot, spread, sems, out_sems) = refs[:count], refs[count:]
        f = pos_ref[0]
        copies = start_fetch(
            pieces, piece_refs, lambda i, row, n: cot.at[i, pl.ds(row, n), :], sems, f
        )
        column = lanes((length, slots))
        expert = jnp.zeros((length, slots), jnp.int32)
        for k in range(1, number):
            expert = expert + (column >= k * CAP).astype(jnp.int32)
        rank = (column - expert * CAP + 1).astype(F32)
        expert = (expert + f * number).astype(F32)
        lower = (
            lax.broadcasted_iota(jnp.int32, (length, length), 0) >= lanes((length, length))
        ).astype(F32).astype(BF16)
        for copy in copies:
            copy.wait()

        def leave(pair):
            span = pl.ds(pl.multiple_of(pair * 2 * CAP, 16), 2 * CAP)
            return pltpu.make_async_copy(
                spread.at[:, span, :], rows_ref.at[:, span, :], out_sems.at[pair]
            )

        @pl.loop(0, nf // 2)
        def _(pair):
            for s in (2 * pair, 2 * pair + 1):
                named = cot[s, :, D:].astype(F32)
                hit = named[:, 0:1] == expert
                for j in range(1, top):
                    hit = hit | (named[:, j : j + 1] == expert)
                hit = jnp.where(hit, 1.0, 0.0)
                so_far = dot(lower, hit.astype(BF16))
                slot_ref[s] = jnp.where((so_far == rank) & (hit > 0.0), 1.0, 0.0).astype(BF16)
            at = pl.ds(pl.multiple_of(pair * 2 * CAP, 16), 2 * CAP)

            def put(k, span, rows):
                spread[k, at, span] = rows.astype(BF16)

            spread_rows(slot_ref, cot.at[:, :, :D], put, pair, number, 512)
            leave(pair).start()

        for pair in range(nf // 2):
            leave(pair).wait()

    return pl.pallas_call(
        without(kernel, 1 + count, len(deps)),
        out_shape=[
            shape((nf, length, slots), BF16),
            shape((number, nf * CAP, D), BF16),
        ],
        in_specs=[SMEM] + [HBM] * (count + len(deps)),
        out_specs=[VMEM, HBM],
        scratch_shapes=[
            pltpu.VMEM((nf, length, D + SIDE), BF16),
            pltpu.VMEM((number, nf * CAP, D), BF16),
            pltpu.SemaphoreType.DMA((len(pieces),)),
            pltpu.SemaphoreType.DMA((nf // 2,)),
        ],
        compiler_params=params(60),
        cost_estimate=cost(0.1),
        name="route_cotangent",
    )(pos, *arrays, *deps)


def down_back(grad_rows, weights, deps=()):
    number, filled, _ = grad_rows.shape
    width = weights.shape[3]

    def kernel(rows_ref, w_ref, out_ref):
        for k in range(2):
            out_ref[k] = dot(rows_ref[k], w_ref[k, 0])

    return pl.pallas_call(
        without(kernel, 2, len(deps)),
        out_shape=shape((number, filled, width), F32),
        grid=(number // 2,),
        in_specs=[
            pl.BlockSpec((2, filled, D), lambda e: (e, 0, 0)),
            pl.BlockSpec((2, 1, D, width), lambda e: (e, 2, 0, 0)),
        ]
        + [HBM] * len(deps),
        out_specs=pl.BlockSpec((2, filled, width), lambda e: (e, 0, 0)),
        compiler_params=params(60),
        cost_estimate=cost(0.1),
        name="down_back",
    )(grad_rows, weights, *deps)


def run_experts(pos, pieces, slot_table, down, weights, nf, cut):
    number, _, _, width = weights.shape
    length, slots = slot_table.shape[1:]
    filled = nf * CAP
    arrays = arrays_of(pieces)
    count = len(arrays)

    def kernel(pos_ref, slot_ref, down_ref, gate_w, up_w, *refs):
        piece_refs, refs = refs[:count], refs[count:]
        rows_ref, dg_ref, du_ref, hidden_ref = refs[:4]
        sums_refs = (refs[4:6], refs[6:8])
        wide, spread, gates, results, sems, rows_sem, out_sems = refs[8:]
        e = pl.program_id(0)
        f = pos_ref[0]
        rows_out = pltpu.make_async_copy(spread, rows_ref, rows_sem)

        @pl.when(e == 0)
        def _():
            copies = start_fetch(
                pieces, piece_refs, lambda i, row, n: wide.at[i, pl.ds(row, n), :], sems
            )
            for pair in range(nf // 2):
                for (index, _, _, _, _), copy in zip(pieces, copies):
                    if index // 2 == pair:
                        copy.wait()
                at = slice(pair * 2 * CAP, (pair + 1) * 2 * CAP)

                def put(k, span, rows):
                    if span.start < D:
                        spread[k, at, span] = rows.astype(BF16)
                    else:
                        lane = lanes((2 * CAP, SIDE))
                        own = f * number + k
                        gate = jnp.where((lane == own) | (lane == own + EXPERTS), rows, 0.0)
                        gates[k, at, :] = jnp.broadcast_to(
                            jnp.sum(gate, axis=-1, keepdims=True), (2 * CAP, SIDE)
                        )

                spread_rows(slot_ref, wide, put, pair, number, 512)
            rows_out.start()

        for k in range(2):
            index = 2 * e + k
            rows = spread[index]
            first, second = gate_w[k, 0], up_w[k, 0]
            gate_pre = dot(rows, first)
            up_pre = dot(rows, second)
            gate = gates[index][:, 0:1]
            sigma = jax.nn.sigmoid(gate_pre)
            swish = gate_pre * sigma
            hidden = (swish * up_pre).astype(BF16).astype(F32)
            hidden_ref[k] = (gate * hidden).astype(BF16)
            unscaled = down_ref[k]
            grad_hidden = gate * unscaled
            dg = (grad_hidden * up_pre * sigma * (1.0 + gate_pre * (1.0 - sigma))).astype(BF16)
            du = (grad_hidden * swish).astype(BF16)
            dg_ref[k] = dg
            du_ref[k] = du
            results[index, :, :D] = (dot_nt(dg, first) + dot_nt(du, second)).astype(BF16)
            pair_grad = jnp.sum(unscaled * hidden, axis=-1, keepdims=True)
            high = pair_grad.astype(BF16).astype(F32)
            lane = lanes((filled, SIDE))
            own = f * number + index
            results[index, :, D:] = jnp.where(
                lane == own, high, jnp.where(lane == own + EXPERTS, pair_grad - high, 0.0)
            ).astype(BF16)

        @pl.when(e == number // 2 - 1)
        def _():
            copies = []
            for pair in range(nf // 2):
                sum_rows(slot_ref, results, wide, pair, number, D + SIDE, 512)
                for k, to in enumerate(sums_refs):
                    index = 2 * pair + k
                    for g, span in enumerate((pl.ds(0, cut), pl.ds(cut, length - cut))):
                        copy = pltpu.make_async_copy(
                            wide.at[index, span, :], to[g].at[pair], out_sems.at[2 * index + g]
                        )
                        copy.start()
                        copies.append(copy)
            for copy in copies:
                copy.wait()
            rows_out.wait()

    return pl.pallas_call(
        kernel,
        out_shape=[
            shape((number, filled, D), BF16),
            shape((number, filled, width), BF16),
            shape((number, filled, width), BF16),
            shape((number, filled, width), BF16),
        ]
        + [shape((nf // 2, number, D + SIDE), BF16) for number in (cut, length - cut)] * 2,
        grid_spec=pltpu.PrefetchScalarGridSpec(
            num_scalar_prefetch=1,
            grid=(number // 2,),
            in_specs=[
                pl.BlockSpec((nf, length, slots), lambda e, pos: (0, 0, 0)),
                pl.BlockSpec((2, filled, width), lambda e, pos: (e, 0, 0)),
                pl.BlockSpec((2, 1, D, width), lambda e, pos: (e, 0, 0, 0)),
                pl.BlockSpec((2, 1, D, width), lambda e, pos: (e, 1, 0, 0)),
            ]
            + [HBM] * count,
            out_specs=[
                HBM,
                pl.BlockSpec((2, filled, width), lambda e, pos: (e, 0, 0)),
                pl.BlockSpec((2, filled, width), lambda e, pos: (e, 0, 0)),
                pl.BlockSpec((2, filled, width), lambda e, pos: (e, 0, 0)),
            ]
            + [HBM] * 4,
            scratch_shapes=[
                pltpu.VMEM((nf, length, D + SIDE), BF16),
                pltpu.VMEM((number, filled, D), BF16),
                pltpu.VMEM((number, filled, SIDE), F32),
                pltpu.VMEM((number, filled, D + SIDE), BF16),
                pltpu.SemaphoreType.DMA((len(pieces),)),
                pltpu.SemaphoreType.DMA,
                pltpu.SemaphoreType.DMA((2 * nf,)),
            ],
        ),
        compiler_params=params(60),
        cost_estimate=cost(5),
        name="run_experts",
    )(pos, slot_table, down, weights, weights, *arrays)


def expert_outputs(pos, slot_table, hidden, weights, nt, deps=()):
    number, filled, width = hidden.shape
    nf, length, slots = slot_table.shape

    rows = length // nt

    def kernel(pos_ref, slot_ref, hidden_ref, w_ref, out_ref, results, out, sems):
        e = pl.program_id(0)
        for k in range(2):
            results[2 * e + k] = dot_nt(hidden_ref[k], w_ref[k, 0]).astype(BF16)

        @pl.when(e == number // 2 - 1)
        def _():
            copies = []
            for pair in range(nf // 2):
                sum_rows(slot_ref, results, out, pair, number, D, 512)
                for index in (2 * pair, 2 * pair + 1):
                    for d in range(nt):
                        start = pl.multiple_of((pos_ref[1] ^ d) * rows, 16)
                        copy = pltpu.make_async_copy(
                            out.at[index, pl.ds(d * rows, rows), :],
                            out_ref.at[pos_ref[0] ^ index, pl.ds(start, rows), :],
                            sems.at[index * nt + d],
                        )
                        copy.start()
                        copies.append(copy)
            for copy in copies:
                copy.wait()

    return pl.pallas_call(
        without(kernel, 4, len(deps)),
        out_shape=shape((nf, length, D), BF16),
        grid_spec=pltpu.PrefetchScalarGridSpec(
            num_scalar_prefetch=1,
            grid=(number // 2,),
            in_specs=[
                pl.BlockSpec((nf, length, slots), lambda e, pos: (0, 0, 0)),
                pl.BlockSpec((2, filled, width), lambda e, pos: (e, 0, 0)),
                pl.BlockSpec((2, 1, D, width), lambda e, pos: (e, 2, 0, 0)),
            ]
            + [HBM] * len(deps),
            out_specs=HBM,
            scratch_shapes=[
                pltpu.VMEM((number, filled, D), BF16),
                pltpu.VMEM((nf, length, D), BF16),
                pltpu.SemaphoreType.DMA((nf * nt,)),
            ],
        ),
        compiler_params=params(48),
        cost_estimate=cost(0.1),
        name="expert_outputs",
    )(pos, slot_table, hidden, weights, *deps)


def expert_gradients(rows, grad_rows, dg, du, hidden, first, number, so_far=None, deps=()):
    everyone, filled, width = dg.shape

    def kernel(rows_ref, grad_ref, dg_ref, du_ref, hidden_ref, *refs):
        out_ref, done_ref = refs
        done_ref[...] = jnp.zeros_like(done_ref)
        rows = rows_ref[0]
        out_ref[0, 0] = dot_tn(rows, dg_ref[0])
        out_ref[0, 1] = dot_tn(rows, du_ref[0])
        out_ref[0, 2] = dot_tn(grad_ref[0], hidden_ref[0])

    tall = pl.BlockSpec((1, filled, D), lambda e: (first + e, 0, 0))
    thin = pl.BlockSpec((1, filled, width), lambda e: (first + e, 0, 0))
    before = [] if so_far is None else [so_far]
    return pl.pallas_call(
        without(kernel, 5, len(before) + len(deps)),
        out_shape=[shape((everyone, 3, D, width), F32), shape((8, SIDE), F32)],
        grid=(number,),
        in_specs=[tall, tall, thin, thin, thin] + [HBM] * (len(before) + len(deps)),
        out_specs=[
            pl.BlockSpec((1, 3, D, width), lambda e: (first + e, 0, 0, 0)),
            pl.BlockSpec((8, SIDE), lambda e: (0, 0)),
        ],
        input_output_aliases={5: 0} if before else {},
        compiler_params=params(48),
        cost_estimate=cost(0.1),
        name="expert_gradients",
    )(rows, grad_rows, dg, du, hidden, *before, *deps)


def on_device(
    nf,
    nt,
    tokens,
    cotangent,
    routes,
    w_query,
    w_key,
    w_value,
    w_output,
    w_router,
    attn_gain,
    ffn_gain,
    query_gain,
    key_gain,
    expert_weights,
):
    length = tokens.shape[0]
    rows = length // nt
    block = D // nf
    group = query_gain.shape[0]
    top = routes.shape[1]
    f = lax.axis_index("fsdp").astype(jnp.int32)
    t = lax.axis_index("tensor").astype(jnp.int32)
    pos = jnp.stack([f, t])

    def placed(gain):
        return lax.dynamic_update_slice(jnp.zeros((block,), BF16), gain, (f * group,))[:, None]

    columns = [
        w_query,
        w_key,
        w_value,
        w_output,
        w_router,
        attn_gain[:, None],
        ffn_gain[:, None],
        placed(query_gain),
        placed(key_gain),
        jnp.zeros((block, SIDE - EXPERTS - 4), BF16),
    ]
    number = expert_weights.shape[0]
    cut = 2 * rows

    def around(block):
        return [block] + [swap(block, "tensor", nt, d) for d in range(1, nt)]

    def sent(parts):
        return [parts[0]] + [swap(parts[d], "tensor", nt, d) for d in range(1, nt)]

    if nf == 8:
        packed = [
            jnp.concatenate([part[half : half + block // 2] for part in columns], axis=1)
            for half in (0, block // 2)
        ]
        weights_near = [gather_near(part, nf) for part in packed]
    else:
        packed = jnp.concatenate(columns, axis=1)

    wide_cot = jnp.concatenate(
        [cotangent, routes.astype(BF16), jnp.zeros((length, SIDE - top), BF16)], axis=1
    )
    wide_cot = jnp.concatenate(
        [lax.dynamic_slice_in_dim(wide_cot, (t ^ d) * rows, rows, 0) for d in range(nt)], axis=0
    )
    position = jnp.arange(length, dtype=F32)[:, None]
    inverse = ROPE_BASE ** (-jnp.arange(HD // 2, dtype=F32) / (HD // 2))
    angles = position * inverse[None, :]
    cosine = jnp.concatenate([jnp.cos(angles)] * 2, axis=1)
    sine = jnp.concatenate([-jnp.sin(angles), jnp.sin(angles)], axis=1)

    if nf == 8:
        weights = gather_two(packed, weights_near, nf)
        wide_cot = join(
            [wide_cot],
            weights_near[0]
            + weights_near[1]
            + [w[2] for w in weights if w[0] == nf - 2]
            + [cosine, sine],
        )
    else:
        weights = gather_rest(packed, gather_near(packed, nf), nf)
    all_cot = lax.all_gather(wide_cot, "fsdp", axis=0, tiled=True)
    cot = [(p, 0, all_cot, None, length) for p in range(nf)]
    saved, parts = attend_forward(pos, tokens, cosine, sine, weights, nf, nt)
    normed_one, _, _, _, _, attended, side, gains, _ = saved
    parts = sent(parts)
    h, normed_two, gates = norm_and_route(pos, tokens, routes, parts, gains, side, nt)

    normed_parts = around(normed_two)
    if nf == 8:
        blocks = [join(normed_parts[:2])]
        near = [gather_near(blocks[0], nf)]
        slot_table, cot_rows = route_cotangent(pos, cot, expert_weights, nf, top, deps=blocks)
        blocks.append(join(normed_parts[2:], deps=[slot_table]))
        near.append(gather_near(blocks[1], nf))
        down = down_back(cot_rows, expert_weights, deps=blocks[1:])
        sources = [near[0][1]] + list(relay(near[1][:1], [down]))
        n2_pieces = gather_two(blocks, near, nf, sources)
    else:
        slot_table, cot_rows = route_cotangent(pos, cot, expert_weights, nf, top)
        down = down_back(cot_rows, expert_weights)
        joined = join(normed_parts)
        n2_pieces = gather_rest(joined, gather_near(joined, nf), nf)
    n2_rows, dg, du, hidden, keep_near, keep_far, send_near, send_far = run_experts(
        pos, n2_pieces, slot_table, down, expert_weights, nf, cut
    )

    far, near = Reduce(keep_far, send_far, nf), Reduce(keep_near, send_near, nf)
    began = far.first() + near.first()
    outputs = expert_outputs(pos, slot_table, hidden, expert_weights, nt, deps=began)
    layer_sum = lax.psum_scatter(
        outputs.reshape(nf * length, D), "fsdp", scatter_dimension=0, tiled=True
    )
    went = far.second(deps=[outputs], micros=20)
    near.second(deps=went, micros=20)
    far_rows = list(far.rows(nt - 2))
    near_rows = list(near.rows(2, deps=far_rows[:1]))
    grad_parts = sent(near_rows + far_rows)
    each = number // 2

    def expert_part(k, deps=()):
        return expert_gradients(
            n2_rows, cot_rows, dg, du, hidden, k * each, each, grad_experts, deps
        )

    grad_experts = None
    grad_experts, done = expert_part(0, near_rows[:1])
    dh, db, ffn_row = norm_back(
        pos, cotangent, grad_parts, h, gates, gains, side, nt, deps=[done]
    )
    db_parts = around(db)
    grad_experts, done = expert_part(1, [db])
    dqkv, parts = attend_backward(
        pos, db_parts, ffn_row, layer_sum, weights, saved, tokens, cosine, sine, nf, nt,
        deps=[done],
    )
    parts = sent(parts)
    keep, send = projection_gradients(pos, normed_one, dqkv, nf)
    projections = Reduce(keep, send, nf)
    both_rows = last_rows(pos, tokens, parts, dh, h, gains, nt, deps=[keep])
    gathered = lax.all_gather(both_rows, "tensor", axis=0, tiled=True)
    pairs = projections.first(deps=[both_rows])
    keep, send = output_gradients(
        pos, attended, db_parts, normed_parts, parts, group, nf, nt, deps=pairs
    )
    output = Reduce(keep, send, nf)
    output.first()
    projections.second()
    output.second()
    width = attended.shape[1]
    grad_query, grad_key, grad_value = projections.columns([width] * 3)
    grad_output, side_grads = output.columns([width], SIDE)
    grad_tokens, layer_out = halve(gathered, deps=[grad_output, grad_query])
    return (
        layer_out,
        grad_tokens,
        grad_query,
        grad_key,
        grad_value,
        grad_output,
        side_grads[:EXPERTS].T,
        side_grads[EXPERTS + 1],
        side_grads[EXPERTS],
        side_grads[EXPERTS + 2, :group],
        side_grads[EXPERTS + 3, :group],
        grad_experts,
    )


def solution(mesh):
    nf, nt = mesh.shape["fsdp"], mesh.shape["tensor"]
    rows, both, line = P("fsdp", None), P("fsdp", "tensor"), P("fsdp")
    experts = P("fsdp", None, None, "tensor")
    return jax.shard_map(
        functools.partial(on_device, nf, nt),
        mesh=mesh,
        in_specs=(rows, rows, rows, both, both, both, both, rows, line, line, line, line, experts),
        out_specs=(rows, rows, both, both, both, both, rows, line, line, line, line, experts),
        check_vma=False,
    )
```

```python
import functools

import jax
import jax.numpy as jnp
from jax import lax
from jax.experimental import pallas as pl
from jax.experimental.pallas import tpu as pltpu
from jax.sharding import PartitionSpec as P

D = 2048
HD = 128
EXPERTS = 64
CAP = 40
SIDE = 128
EPSILON = 1e-06
ROPE_BASE = 10000.0

F32 = jnp.float32
BF16 = jnp.bfloat16
VMEM = pl.BlockSpec(memory_space=pltpu.VMEM)
SMEM = pl.BlockSpec(memory_space=pltpu.SMEM)
HBM = pl.BlockSpec(memory_space=pltpu.HBM)
MIB = 1024 * 1024


def shape(dims, dtype):
    return jax.ShapeDtypeStruct(tuple(dims), dtype)


def params(mebibytes=16):
    return pltpu.CompilerParams(vmem_limit_bytes=mebibytes * MIB)


def near_core(array):
    return pltpu.with_memory_space_constraint(array, pltpu.VMEM)


def cost(micros):
    return pl.CostEstimate(
        flops=int(micros * 1e9), bytes_accessed=int(micros * 3e6), transcendentals=0
    )


def in_hbm(arrays):
    return [pltpu.with_memory_space_constraint(array, pltpu.HBM) for array in arrays]


def dot(left, right):
    return jnp.dot(left, right, preferred_element_type=F32)


def dot_nt(left, right):
    return lax.dot_general(left, right, (((1,), (1,)), ((), ())), preferred_element_type=F32)


def dot_tn(left, right):
    return lax.dot_general(left, right, (((0,), (0,)), ((), ())), preferred_element_type=F32)


def rms_inverse(values):
    return lax.rsqrt(jnp.mean(values * values, axis=-1, keepdims=True) + EPSILON)


def norm_backward(values, inverse, gain, upstream):
    scaled = gain * upstream
    return inverse * scaled - values * (inverse * inverse * inverse) * jnp.mean(
        values * scaled, axis=-1, keepdims=True
    )


def half_turn(values):
    return pltpu.roll(values, HD // 2, 1)


def lanes(dims):
    return lax.broadcasted_iota(jnp.int32, dims, len(dims) - 1)


def swap(block, axis, size, step):
    return lax.ppermute(block, axis, [(i, i ^ step) for i in range(size)])


def without(kernel, at, number):
    def body(*refs):
        kernel(*refs[:at], *refs[at + number :])

    return body


def through(moves, buffer, sems):
    arriving, leaving, row = [], [], 0
    for k, (source, target) in enumerate(moves):
        here = buffer.at[pl.ds(row, source.shape[0]), :]
        arriving.append(pltpu.make_async_copy(source, here, sems.at[2 * k]))
        leaving.append(pltpu.make_async_copy(here, target, sems.at[2 * k + 1]))
        arriving[-1].start()
        row += source.shape[0]
    for arrives, leaves in zip(arriving, leaving):
        arrives.wait()
        leaves.start()
    for leaves in leaving:
        leaves.wait()


def joins(groups, deps=()):
    parts = [part for group in groups for part in group]
    count = len(parts)
    features, dtype = parts[0].shape[1], parts[0].dtype
    totals = [sum(part.shape[0] for part in group) for group in groups]

    def kernel(*refs):
        out_refs, (buffer, sems) = refs[count:-2], refs[-2:]
        moves, k = [], 0
        for out_ref, group in zip(out_refs, groups):
            row = 0
            for part in group:
                moves.append((refs[k], out_ref.at[pl.ds(row, part.shape[0]), :]))
                row, k = row + part.shape[0], k + 1
        through(moves, buffer, sems)

    return pl.pallas_call(
        without(kernel, count, len(deps)),
        out_shape=[shape((total, features), dtype) for total in totals],
        in_specs=[HBM] * (count + len(deps)),
        out_specs=[HBM] * len(groups),
        scratch_shapes=[
            pltpu.VMEM((sum(totals), features), dtype),
            pltpu.SemaphoreType.DMA((2 * count,)),
        ],
        compiler_params=params(60),
        cost_estimate=cost(0.1),
        name="joins",
    )(*parts, *deps)


def join(parts, deps=()):
    return joins([parts], deps)[0]


def relay(parts, deps):
    return joins([[part] for part in parts], deps)


def halves(upper_of, lower_of, deps=()):
    rows, features = upper_of.shape
    half = rows // 2

    def kernel(upper_ref, lower_ref, upper_out, lower_out, buffer, sems):
        through(
            [
                (upper_ref.at[pl.ds(0, half), :], upper_out),
                (lower_ref.at[pl.ds(half, half), :], lower_out),
            ],
            buffer,
            sems,
        )

    return pl.pallas_call(
        without(kernel, 2, len(deps)),
        out_shape=[shape((half, features), upper_of.dtype)] * 2,
        in_specs=[HBM] * (2 + len(deps)),
        out_specs=[HBM] * 2,
        scratch_shapes=[
            pltpu.VMEM((rows, features), upper_of.dtype),
            pltpu.SemaphoreType.DMA((4,)),
        ],
        compiler_params=params(),
        cost_estimate=cost(0.1),
        name="halves",
    )(upper_of, lower_of, *deps)


def gather_near(block, size):
    if size != 8:
        return [swap(block, "fsdp", size, p) for p in range(1, size)]
    return [swap(block, "fsdp", size, 2), swap(block, "fsdp", size, 4)]


def gather_rest(block, near, size, deps=()):
    rows = block.shape[0]
    if size != 8:
        return [(p, 0, part, 0, rows) for p, part in enumerate([block] + near)]
    half = rows // 2
    upper, lower = halves(near[1], near[0], deps)
    front = swap(upper, "fsdp", size, 2)
    back = swap(lower, "fsdp", size, 4)
    pieces = []
    for k, part in enumerate([block] + near):
        pieces.append((2 * k, 0, part, 0, rows))
        pieces.append((2 * k + 1, 0, swap(part, "fsdp", size, 1), 0, rows))
    for row, part in ((0, front), (half, back)):
        pieces.append((6, row, part, 0, half))
        pieces.append((7, row, swap(part, "fsdp", size, 1), 0, half))
    return pieces


def gather_two(blocks, near, size, sources=None):
    pieces = []
    start = 0
    sources = sources or [near[0][1], near[1][0]]
    for block, (along_x, along_y), source, step in zip(blocks, near, sources, (2, 4)):
        rows = block.shape[0]
        last = swap(source, "fsdp", size, step)
        for index, part in ((0, block), (2, along_x), (4, along_y), (6, last)):
            pieces.append((index, start, part, 0, rows))
            pieces.append((index + 1, start, swap(part, "fsdp", size, 1), 0, rows))
        start += rows
    return pieces


def arrays_of(pieces):
    found = []
    for _, _, part, _, _ in pieces:
        if not any(part is other for other in found):
            found.append(part)
    return found


def start_fetch(pieces, refs, place, sems, own=None, columns=None):
    arrays = arrays_of(pieces)
    span = slice(None) if columns is None else pl.ds(*columns)
    copies = []
    for k, (index, row, part, at, rows) in enumerate(pieces):
        ref = next(ref for other, ref in zip(arrays, refs) if other is part)
        if at is None:
            at = pl.multiple_of((own ^ index) * rows, 16)
        copy = pltpu.make_async_copy(
            ref.at[pl.ds(at, rows), span], place(index, row, rows), sems.at[k]
        )
        copy.start()
        copies.append(copy)
    return copies


def pair_sums(keep, got, deps=()):
    _, rows, columns = keep.shape
    half = rows // 2

    def kernel(keep_ref, got_ref, out_x, out_y, held, sems):
        upper, lower = pl.ds(0, half), pl.ds(half, half)
        places = [(1, upper), (3, upper), (2, lower), (3, lower)]
        copies = fetch_parts([keep_ref.at[place] for place in places], held, sems)
        for k, place in enumerate(places):
            copies[k].wait()
            (out_x, out_y)[k // 2][k % 2] = (
                held[k].astype(F32) + got_ref[place].astype(F32)
            ).astype(BF16)

    return pl.pallas_call(
        without(kernel, 2, len(deps)),
        out_shape=[shape((2, half, columns), BF16)] * 2,
        in_specs=[HBM, VMEM] + [HBM] * len(deps),
        out_specs=[VMEM] * 2,
        scratch_shapes=[pltpu.VMEM((4, half, columns), BF16), pltpu.SemaphoreType.DMA((4,))],
        compiler_params=params(),
        cost_estimate=cost(0.1),
        name="pair_sums",
    )(*in_hbm([keep]), near_core(got), *in_hbm(deps))


def fetch_parts(parts, buffer, sems):
    copies = []
    for k, part in enumerate(parts):
        copies.append(pltpu.make_async_copy(part, buffer.at[k], sems.at[k]))
        copies[-1].start()
    return copies


def next_sums(keep, got, from_x, from_y, deps, micros):
    _, rows, columns = keep.shape
    half = rows // 2

    def kernel(keep_ref, got_ref, new_x, new_y, out_x, out_y, held, sems):
        upper, lower = pl.ds(0, half), pl.ds(half, half)
        places = [(2, upper), (1, lower)]
        copies = fetch_parts([keep_ref.at[place] for place in places], held, sems)
        for k, (new, out) in enumerate(((new_x, out_x), (new_y, out_y))):
            copies[k].wait()
            out[...] = (
                held[k].astype(F32) + got_ref[places[k]].astype(F32) + new[1].astype(F32)
            ).astype(BF16)

    return pl.pallas_call(
        without(kernel, 4, len(deps)),
        out_shape=[shape((half, columns), BF16)] * 2,
        in_specs=[HBM, VMEM, VMEM, VMEM] + [HBM] * len(deps),
        out_specs=[VMEM] * 2,
        scratch_shapes=[pltpu.VMEM((2, half, columns), BF16), pltpu.SemaphoreType.DMA((2,))],
        compiler_params=params(),
        cost_estimate=cost(micros),
        name="next_sums",
    )(*in_hbm([keep]), near_core(got), near_core(from_x), near_core(from_y), *in_hbm(deps))


def last_sums(keep, got, from_x, from_y, last_x, last_y, count, deps=()):
    _, rows, columns = keep.shape
    half = rows // 2
    part = rows // count
    each = half // part

    def kernel(keep_ref, got_ref, new_x, end_x, new_y, end_y, *refs):
        out_refs, (held, sems) = refs[:count], refs[count:]
        upper, lower = pl.ds(0, half), pl.ds(half, half)
        places = [(0, upper), (0, lower)]
        copies = fetch_parts([keep_ref.at[place] for place in places], held, sems)
        for k in range(count):
            side = k // each
            new, end = (new_x, end_x) if side == 0 else (new_y, end_y)
            if k % each == 0:
                copies[side].wait()
            first = (k % each) * part
            span = slice(first, first + part)
            from_got = slice(side * half + first, side * half + first + part)
            total = held[side, span].astype(F32) + got_ref[0, from_got].astype(F32)
            total = total + new[0, span].astype(F32) + end[span].astype(F32)
            out_refs[k][...] = total.astype(BF16)

    return pl.pallas_call(
        without(kernel, 6, len(deps)),
        out_shape=[shape((part, columns), BF16)] * count,
        in_specs=[HBM] + [VMEM] * 5 + [HBM] * len(deps),
        out_specs=[VMEM] * count,
        scratch_shapes=[pltpu.VMEM((2, half, columns), BF16), pltpu.SemaphoreType.DMA((2,))],
        compiler_params=params(),
        cost_estimate=cost(20),
        name="last_sums",
    )(
        *in_hbm([keep]), near_core(got), near_core(from_x), near_core(last_x), near_core(from_y), near_core(last_y),
        *in_hbm(deps),
    )


def column_sums(keep, got, from_x, from_y, last_x, last_y, widths, turned):
    _, rows, columns = keep.shape
    half = rows // 2

    def kernel(keep_x, got_x, new_x, end_x, keep_y, got_y, new_y, end_y, *out_refs):
        for k, refs in enumerate(((keep_x, got_x, new_x, end_x), (keep_y, got_y, new_y, end_y))):
            span = slice(k * half, (k + 1) * half)
            total = refs[0][0].astype(F32)
            for ref in refs[1:3]:
                total = total + ref[0].astype(F32)
            total = total + refs[3][...].astype(F32)
            column = 0
            for width, out_ref in zip(widths, out_refs):
                out_ref[span, :] = total[:, column : column + width]
                column += width
            if turned:
                out_refs[-1][:, span] = jnp.transpose(total[:, column : column + turned])

    block = (1, half, columns)
    first = pl.BlockSpec(block, lambda j: (0, 0, 0))
    second = pl.BlockSpec(block, lambda j: (0, 1, 0))
    end = pl.BlockSpec((half, columns), lambda j: (0, 0))
    shapes = [(rows, width) for width in widths] + [(turned, rows)] * (turned > 0)
    return pl.pallas_call(
        kernel,
        out_shape=[shape(dims, F32) for dims in shapes],
        grid=(1,),
        in_specs=[first, first, first, end, second, second, first, end],
        out_specs=[pl.BlockSpec(dims, lambda j: (0, 0)) for dims in shapes],
        compiler_params=params(),
        cost_estimate=cost(0.1),
        name="column_sums",
    )(keep, got, from_x, last_x, keep, got, from_y, last_y)


def halve(array, deps=()):
    rows, columns = array.shape
    half = columns // 2

    def kernel(ref, left_ref, right_ref):
        left_ref[...] = ref[:, :half]
        right_ref[...] = ref[:, half:]

    return pl.pallas_call(
        without(kernel, 1, len(deps)),
        out_shape=[shape((rows, half), array.dtype)] * 2,
        grid=(2,),
        in_specs=[pl.BlockSpec((rows // 2, columns), lambda j: (j, 0))] + [HBM] * len(deps),
        out_specs=[pl.BlockSpec((rows // 2, half), lambda j: (j, 0))] * 2,
        compiler_params=params(60),
        cost_estimate=cost(0.1),
        name="halve",
    )(array, *deps)


class Reduce:
    def __init__(self, keep, send, size):
        self.keep, self.send, self.size = keep, send, size
        if size == 8:
            self.got = swap(send, "fsdp", size, 1)

    def first(self, deps=()):
        if self.size != 8:
            return []
        self.pair = pair_sums(self.keep, self.got, deps)
        self.from_x = swap(self.pair[0], "fsdp", self.size, 2)
        self.from_y = swap(self.pair[1], "fsdp", self.size, 4)
        return list(self.pair[:1])

    def second(self, deps=(), micros=0.1):
        if self.size != 8:
            return []
        sums = next_sums(self.keep, self.got, self.from_x, self.from_y, deps, micros)
        self.last_x = swap(sums[0], "fsdp", self.size, 4)
        self.last_y = swap(sums[1], "fsdp", self.size, 2)
        return list(sums[:1])

    def total(self):
        if self.size != 8:
            total = self.keep[0].astype(F32)
            for p in range(1, self.size):
                block = self.keep[p // 2] if p % 2 == 0 else self.send[p // 2]
                total = total + swap(block, "fsdp", self.size, p).astype(F32)
            return total
        half = self.keep.shape[1] // 2
        sums = []
        for rows, new, last in (
            (slice(0, half), self.from_x, self.last_x),
            (slice(half, None), self.from_y, self.last_y),
        ):
            sums.append(
                self.keep[0, rows].astype(F32)
                + self.got[0, rows].astype(F32)
                + new[0].astype(F32)
                + last.astype(F32)
            )
        return jnp.concatenate(sums, axis=0)

    def columns(self, widths, turned=0):
        if self.size == 8:
            return column_sums(
                self.keep, self.got, self.from_x, self.from_y, self.last_x, self.last_y, widths, turned
            )
        total, found, column = self.total(), [], 0
        for width in widths:
            found.append(total[:, column : column + width])
            column += width
        return found + [total[:, column : column + turned].T] * (turned > 0)

    def rows(self, count, deps=()):
        if self.size != 8:
            return jnp.split(self.total().astype(BF16), count, axis=0)
        return last_sums(
            self.keep, self.got, self.from_x, self.from_y, self.last_x, self.last_y, count, deps
        )


def attend_forward(pos, tokens, cosine, sine, pieces, nf, nt, deps=()):
    length = tokens.shape[0]
    block = D // nf
    rows = length // nt
    columns = pieces[0][2].shape[1]
    width = (columns - SIDE) // 4
    heads = width // HD
    arrays = arrays_of(pieces)
    count = len(arrays)

    def kernel(pos_ref, x_ref, cos_ref, sin_ref, *refs):
        piece_refs, refs = refs[:count], refs[count:]
        n1_ref, qk_ref, rot_ref, v_ref, prob_ref, att_ref, side_ref, gain_ref, head_gain_ref = refs[:9]
        part_refs, (w, out, sems) = refs[9 : 9 + nt], refs[9 + nt :]
        f, t = pos_ref[0], pos_ref[1]

        def place(index, row, number, span):
            start = pl.multiple_of((f ^ index) * block + row, 16)
            return w.at[pl.ds(start, number), pl.ds(*span)]

        spans = ((4 * width, SIDE), (0, 3 * width), (3 * width, width))
        side, copies, later = [
            start_fetch(
                pieces, piece_refs, functools.partial(place, span=span), sems.at[k], columns=span
            )
            for k, span in enumerate(spans)
        ]
        x = x_ref[...].astype(F32)
        normed = x * rms_inverse(x)
        for copy in side:
            copy.wait()
        side_ref[...] = w[:, 4 * width :]
        turned = jnp.transpose(w[:, 4 * width :].astype(F32))
        gain_ref[...] = turned[EXPERTS : EXPERTS + 8]
        head_rows = turned[EXPERTS : EXPERTS + 8, :block]
        for p in range(1, nf):
            head_rows = head_rows + turned[EXPERTS : EXPERTS + 8, p * block : (p + 1) * block]
        head_gains = head_rows[:, :HD]
        head_gain_ref[...] = head_gains
        n1 = (normed * turned[EXPERTS : EXPERTS + 1]).astype(BF16)
        n1_ref[...] = n1
        for copy in copies:
            copy.wait()
        raw = dot(n1, w[:, : 3 * width])
        qk_ref[...] = raw[:, : 2 * width]
        v_ref[...] = raw[:, 2 * width :].astype(BF16)
        cos, sin = cos_ref[...], sin_ref[...]
        for h in range(heads):
            span = slice(h * HD, (h + 1) * HD)
            turned_rows = []
            for which in range(2):
                values = raw[:, which * width + h * HD : which * width + (h + 1) * HD]
                scaled = values * rms_inverse(values) * head_gains[2 + which : 3 + which]
                low = (scaled * cos + half_turn(scaled) * sin).astype(BF16)
                rot_ref[:, which * width + h * HD : which * width + (h + 1) * HD] = low
                turned_rows.append(low)
            scores = dot_nt(turned_rows[0], turned_rows[1]) * (HD**-0.5)
            shifted = jnp.exp(scores - jnp.max(scores, axis=-1, keepdims=True))
            probs = shifted / jnp.sum(shifted, axis=-1, keepdims=True)
            prob_ref[h] = probs
            att_ref[:, span] = dot(probs.astype(BF16), v_ref[:, span]).astype(BF16)
        for copy in later:
            copy.wait()
        out[...] = dot_nt(att_ref[...], w[:, 3 * width : 4 * width]).astype(BF16)
        for d in range(nt):
            start = pl.multiple_of((t ^ d) * rows, 16)
            part_refs[d][...] = out[pl.ds(start, rows), :]

    results = pl.pallas_call(
        without(kernel, 4 + count, len(deps)),
        out_shape=[
            shape((length, D), BF16),
            shape((length, 2 * width), F32),
            shape((length, 2 * width), BF16),
            shape((length, width), BF16),
            shape((heads, length, length), F32),
            shape((length, width), BF16),
            shape((D, SIDE), BF16),
            shape((8, D), F32),
            shape((8, HD), F32),
        ]
        + [shape((rows, D), BF16)] * nt,
        in_specs=[SMEM, VMEM, VMEM, VMEM] + [HBM] * (count + len(deps)),
        out_specs=[VMEM] * (9 + nt),
        scratch_shapes=[
            pltpu.VMEM((D, columns), BF16),
            pltpu.VMEM((length, D), BF16),
            pltpu.SemaphoreType.DMA((3, len(pieces))),
        ],
        compiler_params=params(60),
        cost_estimate=cost(5),
        name="attend_forward",
    )(pos, tokens, cosine, sine, *in_hbm(arrays), *deps)
    return results[:9], results[9:]


def attend_backward(pos, grad_rows, ffn_row, layer_sum, pieces, saved, tokens, cosine, sine, nf, nt, deps=()):
    _, qk, rot, values, probs, _, _, gains, head_gains = saved
    length = tokens.shape[0]
    block = D // nf
    rows = length // nt
    columns = pieces[0][2].shape[1]
    width = (columns - SIDE) // 4
    heads = width // HD
    more = gain_columns(rows)
    arrays = arrays_of(pieces)
    count = len(arrays)

    def kernel(pos_ref, x_ref, cos_ref, sin_ref, qk_ref, rot_ref, v_ref, prob_ref, gain_ref, head_gain_ref, ffn_ref, layer_ref, *refs):
        grad_refs, refs = refs[:nt], refs[nt:]
        piece_refs, refs = refs[:count], refs[count:]
        dqkv_ref = refs[0]
        part_refs, (w, out, db_ref, sems) = refs[1 : 1 + nt], refs[1 + nt :]
        f, t = pos_ref[0], pos_ref[1]

        def place(index, row, number, span):
            start = pl.multiple_of((f ^ index) * block + row, 16)
            return w.at[pl.ds(start, number), pl.ds(*span)]

        spans = ((3 * width, width), (0, 3 * width))
        copies, later = [
            start_fetch(
                pieces, piece_refs, functools.partial(place, span=span), sems.at[k], columns=span
            )
            for k, span in enumerate(spans)
        ]
        for d in range(nt):
            start = pl.multiple_of((t ^ d) * rows, 16)
            db_ref[pl.ds(start, rows), :] = grad_refs[d][:, :D]
        for copy in copies:
            copy.wait()
        cos, sin = cos_ref[...], sin_ref[...]
        head_gains = head_gain_ref[...]
        grad_att = dot(db_ref[...], w[:, 3 * width : 4 * width]).astype(BF16)
        gain_rows = [jnp.zeros((1, HD), F32), jnp.zeros((1, HD), F32)]
        for h in range(heads):
            span = slice(h * HD, (h + 1) * HD)
            query_low = rot_ref[:, span]
            key_low = rot_ref[:, width + h * HD : width + (h + 1) * HD]
            grad_out = grad_att[:, span]
            exact = prob_ref[h]
            grad_probs = dot_nt(grad_out, v_ref[:, span])
            row_terms = jnp.sum(exact * grad_probs, axis=-1, keepdims=True)
            grad_scores = (exact * (grad_probs - row_terms)).astype(BF16)
            dqkv_ref[:, 2 * width + h * HD : 2 * width + (h + 1) * HD] = dot_tn(
                exact.astype(BF16), grad_out
            ).astype(BF16)
            both = (dot(grad_scores, key_low), dot_tn(grad_scores, query_low))
            for which in range(2):
                span_w = slice(which * width + h * HD, which * width + (h + 1) * HD)
                grads = both[which] * (HD**-0.5)
                grads = grads * cos - half_turn(grads) * sin
                raw = qk_ref[:, span_w]
                inverse = rms_inverse(raw)
                gain_rows[which] = gain_rows[which] + jnp.sum(
                    grads * raw * inverse, axis=0, keepdims=True
                )
                dqkv_ref[:, span_w] = norm_backward(
                    raw, inverse, head_gains[2 + which : 3 + which], grads
                ).astype(BF16)
        for copy in later:
            copy.wait()
        grad_normed = dot_nt(dqkv_ref[...], w[:, : 3 * width])
        out[...] = grad_normed.astype(BF16)
        x = x_ref[...].astype(F32)
        row = jnp.sum(grad_normed * (x * rms_inverse(x)), axis=0, keepdims=True)
        lines = [row[:, k * SIDE : (k + 1) * SIDE] for row in (ffn_ref[0:1, :], row) for k in range(D // SIDE)]
        lines = lines + gain_rows
        gain_blocks = []
        for k in range(more // SIDE):
            own = lines[k * rows : (k + 1) * rows]
            blank = [jnp.zeros((rows - len(own), SIDE), F32)] if len(own) < rows else []
            gain_blocks.append(jnp.concatenate(own + blank, axis=0).astype(BF16))
        for d in range(nt):
            start = pl.multiple_of((t ^ d) * rows, 16)
            part_refs[d][:, :D] = out[pl.ds(start, rows), :]
            for k, gain_block in enumerate(gain_blocks):
                part_refs[d][:, D + k * SIDE : D + (k + 1) * SIDE] = gain_block
            part_refs[d][:, D + more :] = layer_ref[pl.ds(start, rows), :]

    results = pl.pallas_call(
        without(kernel, 12 + nt + count, len(deps)),
        out_shape=[
            shape((length, 3 * width), BF16),
        ]
        + [shape((rows, 2 * D + more), BF16)] * nt,
        in_specs=[SMEM] + [VMEM] * (11 + nt) + [HBM] * (count + len(deps)),
        out_specs=[VMEM] * (1 + nt),
        scratch_shapes=[
            pltpu.VMEM((D, columns), BF16),
            pltpu.VMEM((length, D), BF16),
            pltpu.VMEM((length, D), BF16),
            pltpu.SemaphoreType.DMA((2, len(pieces))),
        ],
        compiler_params=params(60),
        cost_estimate=cost(0.1),
        name="attend_backward",
    )(
        pos, tokens, cosine, sine, qk, rot, values, probs, gains, head_gains, ffn_row, layer_sum,
        *grad_rows, *in_hbm(arrays), *deps,
    )
    return results[0], results[1:]


def projection_gradients(pos, normed, dqkv, nf, deps=()):
    length = normed.shape[0]
    block = D // nf
    width = dqkv.shape[1]

    def kernel(pos_ref, n1_ref, dqkv_ref, keep_ref, send_ref):
        for p in range(nf):
            start = pl.multiple_of((pos_ref[0] ^ p) * block, 128)
            to = (keep_ref if p % 2 == 0 else send_ref).at[p // 2]
            to[...] = dot_tn(n1_ref[:, pl.ds(start, block)], dqkv_ref[...]).astype(BF16)

    return pl.pallas_call(
        without(kernel, 3, len(deps)),
        out_shape=[shape((nf // 2, block, width), BF16)] * 2,
        in_specs=[SMEM, VMEM, VMEM] + [HBM] * len(deps),
        out_specs=[VMEM] * 2,
        compiler_params=params(40),
        cost_estimate=cost(0.1),
        name="projection_gradients",
    )(pos, normed, dqkv, *deps)


def output_gradients(pos, attended, grad_parts, normed_parts, gain_parts, group, nf, nt, deps=()):
    length, width = attended.shape
    rows = length // nt
    block = D // nf
    columns = width + SIDE
    more = gain_columns(rows)
    count = D // SIDE

    def kernel(pos_ref, att_ref, *refs):
        grad_refs, normed_refs, part_refs = refs[:nt], refs[nt : 2 * nt], refs[2 * nt : 3 * nt]
        keep_ref, send_ref, db, n2, held, gain_ref = refs[3 * nt :]
        f, t = pos_ref[0], pos_ref[1]
        for d in range(nt):
            start = pl.multiple_of((t ^ d) * rows, 16)
            db[pl.ds(start, rows), :] = grad_refs[d][...]
            n2[pl.ds(start, rows), :] = normed_refs[d][:, :D]
            held[t ^ d] = part_refs[d][:, D : D + more].astype(F32)
        total = held[0]
        for k in range(1, nt):
            total = total + held[k]
        for line in range(2 * count + 2):
            column, at = line // rows * SIDE, line % rows
            to = line // count if line < 2 * count else line - 2 * count + 2
            lane = line % count * SIDE if line < 2 * count else 0
            gain_ref[to : to + 1, lane : lane + SIDE] = total[at : at + 1, column : column + SIDE]
        lane = lanes((block, SIDE))
        sub = lax.broadcasted_iota(jnp.int32, (block, SIDE), 0)
        for p in range(nf):
            owner = f ^ p
            start = pl.multiple_of(owner * block, 128)
            to = (keep_ref if p % 2 == 0 else send_ref).at[p // 2]
            to[:, :width] = dot_tn(db[:, pl.ds(start, block)], att_ref[...]).astype(BF16)
            side = dot_tn(n2[:, pl.ds(start, block)], db[:, D:])
            for which in range(2):
                row = gain_ref[which : which + 1, pl.ds(start, block)]
                column = jnp.transpose(jnp.broadcast_to(row, (SIDE, block)))
                side = jnp.where(lane == EXPERTS + which, column, side)
            mine = (lane == owner * group + sub) & (sub < group)
            for which in range(2, 4):
                spread = jnp.where(mine, gain_ref[which : which + 1, :HD], 0.0)
                column = jnp.sum(spread, axis=1, keepdims=True)
                side = jnp.where(lane == EXPERTS + which, column, side)
            to[:, width:] = side.astype(BF16)

    return pl.pallas_call(
        without(kernel, 2 + 3 * nt, len(deps)),
        out_shape=[shape((nf // 2, block, columns), BF16)] * 2,
        in_specs=[SMEM] + [VMEM] * (1 + 3 * nt) + [HBM] * len(deps),
        out_specs=[VMEM] * 2,
        scratch_shapes=[
            pltpu.VMEM((length, D + SIDE), BF16),
            pltpu.VMEM((length, D), BF16),
            pltpu.VMEM((nt, rows, more), F32),
            pltpu.VMEM((8, D), F32),
        ],
        compiler_params=params(40),
        cost_estimate=cost(0.1),
        name="output_gradients",
    )(pos, attended, *grad_parts, *normed_parts, *gain_parts, *deps)


def gain_columns(rows):
    return SIDE * -(-(2 * D // SIDE + 2) // rows)


def norm_and_route(pos, tokens, routes, parts, gains, side, nt, deps=()):
    rows = tokens.shape[0] // nt
    top = routes.shape[1]

    def kernel(pos_ref, route_all, x_all, gain_all, side_all, first_all, *refs):
        part_refs, refs = refs[: nt - 1], refs[nt - 1 :]
        h_ref, next_ref, gate_ref, x_ref, gain_ref, side_ref, first_ref, sems = refs
        mine = pl.ds(pl.multiple_of(pos_ref[1] * rows, 16), rows)
        copies = [
            pltpu.make_async_copy(source, target, sems.at[k])
            for k, (source, target) in enumerate(
                (
                    (x_all.at[mine, :], x_ref),
                    (first_all, first_ref),
                    (gain_all, gain_ref),
                    (side_all, side_ref),
                )
            )
        ]
        for copy in copies:
            copy.start()
        route_ref = route_all.at[mine, :]
        copies[0].wait()
        copies[1].wait()
        h = x_ref[...].astype(F32) + first_ref[...].astype(F32)
        for ref in part_refs:
            h = h + ref[...].astype(F32)
        h_ref[...] = h
        copies[2].wait()
        copies[3].wait()
        n2 = (h * rms_inverse(h) * gain_ref[1:2]).astype(BF16)
        next_ref[:, :D] = n2
        logits = dot(n2, side_ref[...])
        lane = lanes((rows, SIDE))
        chosen = route_ref[:, 0:1] == lane
        for j in range(1, top):
            chosen = chosen | (route_ref[:, j : j + 1] == lane)
        highest = jnp.max(jnp.where(chosen, logits, -jnp.inf), axis=-1, keepdims=True)
        shifted = jnp.where(chosen, jnp.exp(jnp.where(chosen, logits - highest, 0.0)), 0.0)
        gates = shifted / jnp.sum(shifted, axis=-1, keepdims=True)
        gate_ref[...] = gates
        first = gates.astype(BF16).astype(F32)
        rest = (gates - first).astype(BF16).astype(F32)
        next_ref[:, D:] = (first + pltpu.roll(rest, EXPERTS, 1)).astype(BF16)

    return pl.pallas_call(
        without(kernel, 5 + nt, len(deps)),
        out_shape=[shape((rows, D), F32), shape((rows, D + SIDE), BF16), shape((rows, SIDE), F32)],
        in_specs=[SMEM, VMEM] + [HBM] * 4 + [VMEM] * (nt - 1) + [HBM] * len(deps),
        out_specs=[VMEM] * 3,
        scratch_shapes=[
            pltpu.VMEM((rows, D), BF16),
            pltpu.VMEM((8, D), F32),
            pltpu.VMEM((D, SIDE), BF16),
            pltpu.VMEM((rows, D), BF16),
            pltpu.SemaphoreType.DMA((4,)),
        ],
        compiler_params=params(60),
        cost_estimate=cost(100),
        name="norm_and_route",
    )(
        pos, routes, *in_hbm([tokens, gains, side, parts[0]]),
        *[near_core(part) for part in parts[1:]], *in_hbm(deps),
    )


def norm_back(pos, cotangent, parts, h, gates, gains, side, nt, deps=()):
    rows = h.shape[0]

    def kernel(pos_ref, cot_ref, h_ref, gate_ref, gain_ref, side_ref, *refs):
        part_refs, (dh_ref, db_ref, row_ref) = refs[:nt], refs[nt:]
        total = part_refs[0][...].astype(F32)
        for ref in part_refs[1:]:
            total = total + ref[...].astype(F32)
        pair = total[:, D:]
        pair = pair + pltpu.roll(pair, EXPERTS, 1)
        gates = gate_ref[...]
        grads = gates * (pair - jnp.sum(gates * pair, axis=-1, keepdims=True))
        low = grads.astype(BF16)
        dn2 = total[:, :D] + dot_nt(low, side_ref[...])
        h = h_ref[...]
        inverse = rms_inverse(h)
        gain_row = jnp.sum(dn2 * h * inverse, axis=0, keepdims=True)
        row_ref[...] = jnp.broadcast_to(gain_row, (8, D))
        dh = cot_ref[...].astype(F32) + norm_backward(h, inverse, gain_ref[1:2], dn2)
        dh_ref[...] = dh
        db_ref[:, :D] = dh.astype(BF16)
        db_ref[:, D:] = low

    whole = lambda i, pos: (0, 0)
    mine = lambda i, pos: (pos[1], 0)
    return pl.pallas_call(
        without(kernel, 6 + nt, len(deps)),
        out_shape=[shape((rows, D), F32), shape((rows, D + SIDE), BF16), shape((8, D), F32)],
        grid_spec=pltpu.PrefetchScalarGridSpec(
            num_scalar_prefetch=1,
            grid=(1,),
            in_specs=[
                pl.BlockSpec((rows, D), mine),
                pl.BlockSpec((rows, D), whole),
                pl.BlockSpec((rows, SIDE), whole),
                pl.BlockSpec((8, D), whole),
                pl.BlockSpec((D, SIDE), whole),
            ]
            + [pl.BlockSpec((rows, D + SIDE), whole)] * nt
            + [HBM] * len(deps),
            out_specs=[
                pl.BlockSpec((rows, D), whole),
                pl.BlockSpec((rows, D + SIDE), whole),
                pl.BlockSpec((8, D), whole),
            ],
        ),
        compiler_params=params(),
        cost_estimate=cost(100),
        name="norm_back",
    )(pos, cotangent, h, gates, gains, side, *parts, *in_hbm(deps))


def last_rows(pos, tokens, parts, dh, h, gains, nt, deps=()):
    rows = dh.shape[0]
    columns = parts[0].shape[1]

    def kernel(pos_ref, x_all, dh_all, h_all, gain_all, first_all, *refs):
        part_refs, refs = refs[: nt - 1], refs[nt - 1 :]
        out_ref, x_ref, dh_ref, h_ref, gain_ref, first_ref, sems = refs
        mine = pl.ds(pl.multiple_of(pos_ref[1] * rows, 16), rows)
        copies = [
            pltpu.make_async_copy(source, target, sems.at[k])
            for k, (source, target) in enumerate(
                (
                    (first_all, first_ref),
                    (x_all.at[mine, :], x_ref),
                    (gain_all, gain_ref),
                    (h_all, h_ref),
                    (dh_all, dh_ref),
                )
            )
        ]
        for copy in copies:
            copy.start()
        for copy in copies:
            copy.wait()
        total = first_ref[:, :D].astype(F32)
        layer = h_ref[...] + first_ref[:, columns - D :].astype(F32)
        for ref in part_refs:
            total = total + ref[:, :D].astype(F32)
            layer = layer + ref[:, columns - D :].astype(F32)
        x = x_ref[...].astype(F32)
        out_ref[:, :D] = (
            dh_ref[...] + norm_backward(x, rms_inverse(x), gain_ref[0:1], total)
        ).astype(BF16)
        out_ref[:, D:] = layer.astype(BF16)

    return pl.pallas_call(
        without(kernel, 5 + nt, len(deps)),
        out_shape=shape((rows, 2 * D), BF16),
        in_specs=[SMEM] + [HBM] * 5 + [VMEM] * (nt - 1) + [HBM] * len(deps),
        out_specs=VMEM,
        scratch_shapes=[
            pltpu.VMEM((rows, D), BF16),
            pltpu.VMEM((rows, D), F32),
            pltpu.VMEM((rows, D), F32),
            pltpu.VMEM((8, D), F32),
            pltpu.VMEM((rows, columns), BF16),
            pltpu.SemaphoreType.DMA((5,)),
        ],
        compiler_params=params(60),
        cost_estimate=cost(100),
        name="last_rows",
    )(
        pos, *in_hbm([tokens, dh, h, gains, parts[0]]),
        *[near_core(part) for part in parts[1:]], *in_hbm(deps),
    )


def place_rows(pos, parts):
    nt = len(parts)
    rows, columns = parts[0].shape
    half = columns // 2

    def kernel(pos_ref, *refs):
        left_ref, right_ref = refs[nt:]
        for d in range(nt):
            start = pl.multiple_of((pos_ref[1] ^ d) * rows, 16)
            left_ref[pl.ds(start, rows), :] = refs[d][:, :half]
            right_ref[pl.ds(start, rows), :] = refs[d][:, half:]

    return pl.pallas_call(
        kernel,
        out_shape=[shape((rows * nt, half), parts[0].dtype)] * 2,
        in_specs=[SMEM] + [VMEM] * nt,
        out_specs=[VMEM] * 2,
        compiler_params=params(),
        cost_estimate=cost(0.1),
        name="place_rows",
    )(pos, *parts)


def spread_rows(slots, source, target, pair, number, cut):
    for begin in range(0, source.shape[2], cut):
        span = slice(begin, min(begin + cut, source.shape[2]))
        two = [dot_tn(slots[2 * pair + k], source[2 * pair + k, :, span]) for k in range(2)]
        for e in range(number):
            joined = jnp.concatenate([rows[e * CAP : (e + 1) * CAP] for rows in two], axis=0)
            target(e, span, joined)


def sum_rows(slots, results, target, pair, number, total, cut):
    at = slice(pair * 2 * CAP, (pair + 1) * 2 * CAP)
    for begin in range(0, total, cut):
        span = slice(begin, min(begin + cut, total))
        blocks = [results[e, at, span].astype(F32) for e in range(number)]
        for k in range(2):
            rows = jnp.concatenate([b[k * CAP : (k + 1) * CAP] for b in blocks], axis=0)
            target[2 * pair + k, :, span] = dot(slots[2 * pair + k], rows.astype(BF16)).astype(BF16)


def route_cotangent(pos, pieces, weights, nf, top, deps=()):
    number = weights.shape[0]
    length = sum(rows for index, _, _, _, rows in pieces if index == 0)
    slots = number * CAP
    arrays = arrays_of(pieces)
    count = len(arrays)

    def kernel(pos_ref, *refs):
        piece_refs, (slot_ref, rows_ref, cot, spread, sems, out_sems) = refs[:count], refs[count:]
        f = pos_ref[0]
        copies = start_fetch(
            pieces, piece_refs, lambda i, row, n: cot.at[i, pl.ds(row, n), :], sems, f
        )
        column = lanes((length, slots))
        expert = jnp.zeros((length, slots), jnp.int32)
        for k in range(1, number):
            expert = expert + (column >= k * CAP).astype(jnp.int32)
        rank = (column - expert * CAP + 1).astype(F32)
        expert = (expert + f * number).astype(F32)
        lower = (
            lax.broadcasted_iota(jnp.int32, (length, length), 0) >= lanes((length, length))
        ).astype(F32).astype(BF16)
        for copy in copies:
            copy.wait()

        def leave(pair):
            span = pl.ds(pl.multiple_of(pair * 2 * CAP, 16), 2 * CAP)
            return pltpu.make_async_copy(
                spread.at[:, span, :], rows_ref.at[:, span, :], out_sems.at[pair]
            )

        @pl.loop(0, nf // 2)
        def _(pair):
            for s in (2 * pair, 2 * pair + 1):
                named = cot[s, :, D:].astype(F32)
                hit = named[:, 0:1] == expert
                for j in range(1, top):
                    hit = hit | (named[:, j : j + 1] == expert)
                hit = jnp.where(hit, 1.0, 0.0)
                so_far = dot(lower, hit.astype(BF16))
                slot_ref[s] = jnp.where((so_far == rank) & (hit > 0.0), 1.0, 0.0).astype(BF16)
            at = pl.ds(pl.multiple_of(pair * 2 * CAP, 16), 2 * CAP)

            def put(k, span, rows):
                spread[k, at, span] = rows.astype(BF16)

            spread_rows(slot_ref, cot.at[:, :, :D], put, pair, number, 512)
            leave(pair).start()

        for pair in range(nf // 2):
            leave(pair).wait()

    return pl.pallas_call(
        without(kernel, 1 + count, len(deps)),
        out_shape=[
            shape((nf, length, slots), BF16),
            shape((number, nf * CAP, D), BF16),
        ],
        in_specs=[SMEM] + [HBM] * (count + len(deps)),
        out_specs=[VMEM, HBM],
        scratch_shapes=[
            pltpu.VMEM((nf, length, D + SIDE), BF16),
            pltpu.VMEM((number, nf * CAP, D), BF16),
            pltpu.SemaphoreType.DMA((len(pieces),)),
            pltpu.SemaphoreType.DMA((nf // 2,)),
        ],
        compiler_params=params(60),
        cost_estimate=cost(0.1),
        name="route_cotangent",
    )(pos, *in_hbm(arrays), *deps)


def down_back(grad_rows, weights, deps=()):
    number, filled, _ = grad_rows.shape
    width = weights.shape[3]

    def kernel(rows_ref, w_ref, out_ref):
        for k in range(2):
            out_ref[k] = dot(rows_ref[k], w_ref[k, 0])

    return pl.pallas_call(
        without(kernel, 2, len(deps)),
        out_shape=shape((number, filled, width), F32),
        grid=(number // 2,),
        in_specs=[
            pl.BlockSpec((2, filled, D), lambda e: (e, 0, 0)),
            pl.BlockSpec((2, 1, D, width), lambda e: (e, 2, 0, 0)),
        ]
        + [HBM] * len(deps),
        out_specs=pl.BlockSpec((2, filled, width), lambda e: (e, 0, 0)),
        compiler_params=params(60),
        cost_estimate=cost(0.1),
        name="down_back",
    )(grad_rows, weights, *deps)


def run_experts(pos, pieces, slot_table, down, weights, nf, cut):
    number, _, _, width = weights.shape
    length, slots = slot_table.shape[1:]
    filled = nf * CAP
    arrays = arrays_of(pieces)
    count = len(arrays)

    def kernel(pos_ref, slot_ref, down_ref, gate_w, up_w, *refs):
        piece_refs, refs = refs[:count], refs[count:]
        rows_ref, dg_ref, du_ref, hidden_ref = refs[:4]
        sums_refs = (refs[4:6], refs[6:8])
        wide, spread, gates, results, sems, rows_sem, out_sems = refs[8:]
        e = pl.program_id(0)
        f = pos_ref[0]
        rows_out = pltpu.make_async_copy(spread, rows_ref, rows_sem)

        @pl.when(e == 0)
        def _():
            copies = start_fetch(
                pieces, piece_refs, lambda i, row, n: wide.at[i, pl.ds(row, n), :], sems
            )
            for pair in range(nf // 2):
                for (index, _, _, _, _), copy in zip(pieces, copies):
                    if index // 2 == pair:
                        copy.wait()
                at = slice(pair * 2 * CAP, (pair + 1) * 2 * CAP)

                def put(k, span, rows):
                    if span.start < D:
                        spread[k, at, span] = rows.astype(BF16)
                    else:
                        lane = lanes((2 * CAP, SIDE))
                        own = f * number + k
                        gate = jnp.where((lane == own) | (lane == own + EXPERTS), rows, 0.0)
                        gates[k, at, :] = jnp.broadcast_to(
                            jnp.sum(gate, axis=-1, keepdims=True), (2 * CAP, SIDE)
                        )

                spread_rows(slot_ref, wide, put, pair, number, 512)
            rows_out.start()

        for k in range(2):
            index = 2 * e + k
            rows = spread[index]
            first, second = gate_w[k, 0], up_w[k, 0]
            gate_pre = dot(rows, first)
            up_pre = dot(rows, second)
            gate = gates[index][:, 0:1]
            sigma = jax.nn.sigmoid(gate_pre)
            swish = gate_pre * sigma
            hidden = (swish * up_pre).astype(BF16).astype(F32)
            hidden_ref[k] = (gate * hidden).astype(BF16)
            unscaled = down_ref[k]
            grad_hidden = gate * unscaled
            dg = (grad_hidden * up_pre * sigma * (1.0 + gate_pre * (1.0 - sigma))).astype(BF16)
            du = (grad_hidden * swish).astype(BF16)
            dg_ref[k] = dg
            du_ref[k] = du
            results[index, :, :D] = (dot_nt(dg, first) + dot_nt(du, second)).astype(BF16)
            pair_grad = jnp.sum(unscaled * hidden, axis=-1, keepdims=True)
            high = pair_grad.astype(BF16).astype(F32)
            lane = lanes((filled, SIDE))
            own = f * number + index
            results[index, :, D:] = jnp.where(
                lane == own, high, jnp.where(lane == own + EXPERTS, pair_grad - high, 0.0)
            ).astype(BF16)

        @pl.when(e == number // 2 - 1)
        def _():
            copies = []
            for pair in range(nf // 2):
                sum_rows(slot_ref, results, wide, pair, number, D + SIDE, 512)
                for k, to in enumerate(sums_refs):
                    index = 2 * pair + k
                    for g, span in enumerate((pl.ds(0, cut), pl.ds(cut, length - cut))):
                        copy = pltpu.make_async_copy(
                            wide.at[index, span, :], to[g].at[pair], out_sems.at[2 * index + g]
                        )
                        copy.start()
                        copies.append(copy)
            for copy in copies:
                copy.wait()
            rows_out.wait()

    return pl.pallas_call(
        kernel,
        out_shape=[
            shape((number, filled, D), BF16),
            shape((number, filled, width), BF16),
            shape((number, filled, width), BF16),
            shape((number, filled, width), BF16),
        ]
        + [shape((nf // 2, number, D + SIDE), BF16) for number in (cut, length - cut)] * 2,
        grid_spec=pltpu.PrefetchScalarGridSpec(
            num_scalar_prefetch=1,
            grid=(number // 2,),
            in_specs=[
                pl.BlockSpec((nf, length, slots), lambda e, pos: (0, 0, 0)),
                pl.BlockSpec((2, filled, width), lambda e, pos: (e, 0, 0)),
                pl.BlockSpec((2, 1, D, width), lambda e, pos: (e, 0, 0, 0)),
                pl.BlockSpec((2, 1, D, width), lambda e, pos: (e, 1, 0, 0)),
            ]
            + [HBM] * count,
            out_specs=[
                HBM,
                pl.BlockSpec((2, filled, width), lambda e, pos: (e, 0, 0)),
                pl.BlockSpec((2, filled, width), lambda e, pos: (e, 0, 0)),
                pl.BlockSpec((2, filled, width), lambda e, pos: (e, 0, 0)),
            ]
            + [HBM] * 4,
            scratch_shapes=[
                pltpu.VMEM((nf, length, D + SIDE), BF16),
                pltpu.VMEM((number, filled, D), BF16),
                pltpu.VMEM((number, filled, SIDE), F32),
                pltpu.VMEM((number, filled, D + SIDE), BF16),
                pltpu.SemaphoreType.DMA((len(pieces),)),
                pltpu.SemaphoreType.DMA,
                pltpu.SemaphoreType.DMA((2 * nf,)),
            ],
        ),
        compiler_params=params(60),
        cost_estimate=cost(5),
        name="run_experts",
    )(pos, slot_table, down, weights, weights, *in_hbm(arrays))


def expert_outputs(pos, slot_table, hidden, weights, nt, deps=()):
    number, filled, width = hidden.shape
    nf, length, slots = slot_table.shape

    rows = length // nt

    def kernel(pos_ref, slot_ref, hidden_ref, w_ref, out_ref, results, out, sems):
        e = pl.program_id(0)
        for k in range(2):
            results[2 * e + k] = dot_nt(hidden_ref[k], w_ref[k, 0]).astype(BF16)

        @pl.when(e == number // 2 - 1)
        def _():
            copies = []
            for pair in range(nf // 2):
                sum_rows(slot_ref, results, out, pair, number, D, 512)
                for index in (2 * pair, 2 * pair + 1):
                    for d in range(nt):
                        start = pl.multiple_of((pos_ref[1] ^ d) * rows, 16)
                        copy = pltpu.make_async_copy(
                            out.at[index, pl.ds(d * rows, rows), :],
                            out_ref.at[pos_ref[0] ^ index, pl.ds(start, rows), :],
                            sems.at[index * nt + d],
                        )
                        copy.start()
                        copies.append(copy)
            for copy in copies:
                copy.wait()

    return pl.pallas_call(
        without(kernel, 4, len(deps)),
        out_shape=shape((nf, length, D), BF16),
        grid_spec=pltpu.PrefetchScalarGridSpec(
            num_scalar_prefetch=1,
            grid=(number // 2,),
            in_specs=[
                pl.BlockSpec((nf, length, slots), lambda e, pos: (0, 0, 0)),
                pl.BlockSpec((2, filled, width), lambda e, pos: (e, 0, 0)),
                pl.BlockSpec((2, 1, D, width), lambda e, pos: (e, 2, 0, 0)),
            ]
            + [HBM] * len(deps),
            out_specs=HBM,
            scratch_shapes=[
                pltpu.VMEM((number, filled, D), BF16),
                pltpu.VMEM((nf, length, D), BF16),
                pltpu.SemaphoreType.DMA((nf * nt,)),
            ],
        ),
        compiler_params=params(48),
        cost_estimate=cost(0.1),
        name="expert_outputs",
    )(pos, slot_table, hidden, weights, *deps)


def expert_gradients(rows, grad_rows, dg, du, hidden, first, number, so_far=None, deps=()):
    everyone, filled, width = dg.shape

    def kernel(rows_ref, grad_ref, dg_ref, du_ref, hidden_ref, *refs):
        out_ref, done_ref = refs
        done_ref[...] = jnp.zeros_like(done_ref)
        rows = rows_ref[0]
        out_ref[0, 0] = dot_tn(rows, dg_ref[0])
        out_ref[0, 1] = dot_tn(rows, du_ref[0])
        out_ref[0, 2] = dot_tn(grad_ref[0], hidden_ref[0])

    tall = pl.BlockSpec((1, filled, D), lambda e: (first + e, 0, 0))
    thin = pl.BlockSpec((1, filled, width), lambda e: (first + e, 0, 0))
    before = [] if so_far is None else [so_far]
    return pl.pallas_call(
        without(kernel, 5, len(before) + len(deps)),
        out_shape=[shape((everyone, 3, D, width), F32), shape((8, SIDE), F32)],
        grid=(number,),
        in_specs=[tall, tall, thin, thin, thin] + [HBM] * (len(before) + len(deps)),
        out_specs=[
            pl.BlockSpec((1, 3, D, width), lambda e: (first + e, 0, 0, 0)),
            pl.BlockSpec((8, SIDE), lambda e: (0, 0)),
        ],
        input_output_aliases={5: 0} if before else {},
        compiler_params=params(48),
        cost_estimate=cost(0.1),
        name="expert_gradients",
    )(rows, grad_rows, dg, du, hidden, *before, *deps)


def on_device(
    nf,
    nt,
    tokens,
    cotangent,
    routes,
    w_query,
    w_key,
    w_value,
    w_output,
    w_router,
    attn_gain,
    ffn_gain,
    query_gain,
    key_gain,
    expert_weights,
):
    length = tokens.shape[0]
    rows = length // nt
    block = D // nf
    group = query_gain.shape[0]
    top = routes.shape[1]
    f = lax.axis_index("fsdp").astype(jnp.int32)
    t = lax.axis_index("tensor").astype(jnp.int32)
    pos = jnp.stack([f, t])

    def placed(gain):
        return lax.dynamic_update_slice(jnp.zeros((block,), BF16), gain, (f * group,))[:, None]

    columns = [
        w_query,
        w_key,
        w_value,
        w_output,
        w_router,
        attn_gain[:, None],
        ffn_gain[:, None],
        placed(query_gain),
        placed(key_gain),
        jnp.zeros((block, SIDE - EXPERTS - 4), BF16),
    ]
    number = expert_weights.shape[0]
    cut = 2 * rows

    def around(block):
        return [block] + [swap(block, "tensor", nt, d) for d in range(1, nt)]

    def sent(parts):
        return [parts[0]] + [swap(parts[d], "tensor", nt, d) for d in range(1, nt)]

    if nf == 8:
        packed = [
            jnp.concatenate([part[half : half + block // 2] for part in columns], axis=1)
            for half in (0, block // 2)
        ]
        weights_near = [gather_near(part, nf) for part in packed]
    else:
        packed = jnp.concatenate(columns, axis=1)

    wide_cot = jnp.concatenate(
        [cotangent, routes.astype(BF16), jnp.zeros((length, SIDE - top), BF16)], axis=1
    )
    wide_cot = jnp.concatenate(
        [lax.dynamic_slice_in_dim(wide_cot, (t ^ d) * rows, rows, 0) for d in range(nt)], axis=0
    )
    position = jnp.arange(length, dtype=F32)[:, None]
    inverse = ROPE_BASE ** (-jnp.arange(HD // 2, dtype=F32) / (HD // 2))
    angles = position * inverse[None, :]
    cosine = jnp.concatenate([jnp.cos(angles)] * 2, axis=1)
    sine = jnp.concatenate([-jnp.sin(angles), jnp.sin(angles)], axis=1)

    if nf == 8:
        weights = gather_two(packed, weights_near, nf)
        wide_cot = join(
            [wide_cot],
            [w[2] for w in weights if w[0] not in (0, nf - 1)] + [cosine, sine],
        )
    else:
        weights = gather_rest(packed, gather_near(packed, nf), nf)
    all_cot = lax.all_gather(wide_cot, "fsdp", axis=0, tiled=True)
    cot = [(p, 0, all_cot, None, length) for p in range(nf)]
    saved, parts = attend_forward(pos, tokens, cosine, sine, weights, nf, nt)
    normed_one, _, _, _, _, attended, side, gains, _ = saved
    parts = sent(parts)
    h, normed_two, gates = norm_and_route(pos, tokens, routes, parts, gains, side, nt)

    normed_parts = around(normed_two)
    if nf == 8:
        blocks = [join(normed_parts[:2])]
        near = [gather_near(blocks[0], nf)]
        slot_table, cot_rows = route_cotangent(pos, cot, expert_weights, nf, top, deps=blocks)
        blocks.append(join(normed_parts[2:], deps=[slot_table]))
        near.append(gather_near(blocks[1], nf))
        down = down_back(cot_rows, expert_weights, deps=blocks[1:])
        sources = [near[0][1]] + list(relay(near[1][:1], [down]))
        n2_pieces = gather_two(blocks, near, nf, sources)
    else:
        slot_table, cot_rows = route_cotangent(pos, cot, expert_weights, nf, top)
        down = down_back(cot_rows, expert_weights)
        joined = join(normed_parts)
        n2_pieces = gather_rest(joined, gather_near(joined, nf), nf)
    n2_rows, dg, du, hidden, keep_near, keep_far, send_near, send_far = run_experts(
        pos, n2_pieces, slot_table, down, expert_weights, nf, cut
    )

    far, near = Reduce(keep_far, send_far, nf), Reduce(keep_near, send_near, nf)
    began = far.first() + near.first()
    outputs = expert_outputs(pos, slot_table, hidden, expert_weights, nt, deps=began)
    layer_sum = lax.psum_scatter(
        outputs.reshape(nf * length, D), "fsdp", scatter_dimension=0, tiled=True
    )
    went = far.second(deps=[outputs], micros=20)
    near.second(deps=went, micros=20)
    far_rows = list(far.rows(nt - 2))
    near_rows = list(near.rows(2, deps=far_rows[:1]))
    grad_parts = sent(near_rows + far_rows)
    each = number // 2

    def expert_part(k, deps=()):
        return expert_gradients(
            n2_rows, cot_rows, dg, du, hidden, k * each, each, grad_experts, deps
        )

    grad_experts = None
    grad_experts, done = expert_part(0, near_rows[:1])
    dh, db, ffn_row = norm_back(
        pos, cotangent, grad_parts, h, gates, gains, side, nt, deps=[done]
    )
    db_parts = around(db)
    grad_experts, done = expert_part(1, [db])
    dqkv, parts = attend_backward(
        pos, db_parts, ffn_row, layer_sum, weights, saved, tokens, cosine, sine, nf, nt,
        deps=[done],
    )
    parts = sent(parts)
    keep, send = projection_gradients(pos, normed_one, dqkv, nf)
    projections = Reduce(keep, send, nf)
    both_rows = last_rows(pos, tokens, parts, dh, h, gains, nt, deps=[keep])
    gathered = lax.all_gather(both_rows, "tensor", axis=0, tiled=True)
    pairs = projections.first(deps=[both_rows])
    keep, send = output_gradients(
        pos, attended, db_parts, normed_parts, parts, group, nf, nt, deps=pairs
    )
    output = Reduce(keep, send, nf)
    output.first()
    projections.second()
    output.second()
    width = attended.shape[1]
    grad_query, grad_key, grad_value = projections.columns([width] * 3)
    grad_output, side_grads = output.columns([width], SIDE)
    grad_tokens, layer_out = halve(gathered, deps=[grad_output, grad_query])
    return (
        layer_out,
        grad_tokens,
        grad_query,
        grad_key,
        grad_value,
        grad_output,
        side_grads[:EXPERTS].T,
        side_grads[EXPERTS + 1],
        side_grads[EXPERTS],
        side_grads[EXPERTS + 2, :group],
        side_grads[EXPERTS + 3, :group],
        grad_experts,
    )


def solution(mesh):
    nf, nt = mesh.shape["fsdp"], mesh.shape["tensor"]
    rows, both, line = P("fsdp", None), P("fsdp", "tensor"), P("fsdp")
    experts = P("fsdp", None, None, "tensor")
    return jax.shard_map(
        functools.partial(on_device, nf, nt),
        mesh=mesh,
        in_specs=(rows, rows, rows, both, both, both, both, rows, line, line, line, line, experts),
        out_specs=(rows, rows, both, both, both, both, rows, line, line, line, line, experts),
        check_vma=False,
    )
```

```python
import functools

import jax
import jax.numpy as jnp
import numpy as np
from jax import lax
from jax.experimental import pallas as pl
from jax.experimental.pallas import tpu as pltpu
from jax.sharding import PartitionSpec as P

D = 2048
HD = 128
EXPERTS = 64
CAP = 40
SIDE = 128
EPSILON = 1e-06
ROPE_BASE = 10000.0

F32 = jnp.float32
BF16 = jnp.bfloat16
VMEM = pl.BlockSpec(memory_space=pltpu.VMEM)
SMEM = pl.BlockSpec(memory_space=pltpu.SMEM)
HBM = pl.BlockSpec(memory_space=pltpu.HBM)
MIB = 1024 * 1024


def shape(dims, dtype):
    return jax.ShapeDtypeStruct(tuple(dims), dtype)


def params(mebibytes=16):
    return pltpu.CompilerParams(vmem_limit_bytes=mebibytes * MIB)


def near_core(array):
    return pltpu.with_memory_space_constraint(array, pltpu.VMEM)


def cost(micros):
    return pl.CostEstimate(
        flops=int(micros * 1e9), bytes_accessed=int(micros * 3e6), transcendentals=0
    )


def in_hbm(arrays):
    return [pltpu.with_memory_space_constraint(array, pltpu.HBM) for array in arrays]


def dot(left, right):
    return jnp.dot(left, right, preferred_element_type=F32)


def dot_nt(left, right):
    return lax.dot_general(left, right, (((1,), (1,)), ((), ())), preferred_element_type=F32)


def dot_tn(left, right):
    return lax.dot_general(left, right, (((0,), (0,)), ((), ())), preferred_element_type=F32)


def rms_inverse(values):
    return lax.rsqrt(jnp.mean(values * values, axis=-1, keepdims=True) + EPSILON)


def norm_backward(values, inverse, gain, upstream):
    scaled = gain * upstream
    return inverse * scaled - values * (inverse * inverse * inverse) * jnp.mean(
        values * scaled, axis=-1, keepdims=True
    )


def half_turn(values):
    return pltpu.roll(values, HD // 2, 1)


def lanes(dims):
    return lax.broadcasted_iota(jnp.int32, dims, len(dims) - 1)


def swap(block, axis, size, step):
    return lax.ppermute(block, axis, [(i, i ^ step) for i in range(size)])


def without(kernel, at, number):
    def body(*refs):
        kernel(*refs[:at], *refs[at + number :])

    return body


def through(moves, buffer, sems):
    arriving, leaving, row = [], [], 0
    for k, (source, target) in enumerate(moves):
        here = buffer.at[pl.ds(row, source.shape[0]), :]
        arriving.append(pltpu.make_async_copy(source, here, sems.at[2 * k]))
        leaving.append(pltpu.make_async_copy(here, target, sems.at[2 * k + 1]))
        arriving[-1].start()
        row += source.shape[0]
    for arrives, leaves in zip(arriving, leaving):
        arrives.wait()
        leaves.start()
    for leaves in leaving:
        leaves.wait()


def joins(groups, deps=()):
    parts = [part for group in groups for part in group]
    count = len(parts)
    features, dtype = parts[0].shape[1], parts[0].dtype
    totals = [sum(part.shape[0] for part in group) for group in groups]

    def kernel(*refs):
        out_refs, (buffer, sems) = refs[count:-2], refs[-2:]
        moves, k = [], 0
        for out_ref, group in zip(out_refs, groups):
            row = 0
            for part in group:
                moves.append((refs[k], out_ref.at[pl.ds(row, part.shape[0]), :]))
                row, k = row + part.shape[0], k + 1
        through(moves, buffer, sems)

    return pl.pallas_call(
        without(kernel, count, len(deps)),
        out_shape=[shape((total, features), dtype) for total in totals],
        in_specs=[HBM] * (count + len(deps)),
        out_specs=[HBM] * len(groups),
        scratch_shapes=[
            pltpu.VMEM((sum(totals), features), dtype),
            pltpu.SemaphoreType.DMA((2 * count,)),
        ],
        compiler_params=params(60),
        cost_estimate=cost(0.1),
        name="joins",
    )(*parts, *deps)


def join(parts, deps=()):
    return joins([parts], deps)[0]


def turn_rows(pos, array, routes, nt, deps):
    total, features = array.shape
    rows = total // nt
    top = routes.shape[1]

    def kernel(pos_ref, array_ref, route_ref, out_ref, held, sems, out_sem):
        starts = [pl.multiple_of((pos_ref[1] ^ d) * rows, 16) for d in range(nt)]
        copies = []
        for d, start in enumerate(starts):
            to = held.at[pl.ds(d * rows, rows), pl.ds(0, features)]
            copies.append(
                pltpu.make_async_copy(array_ref.at[pl.ds(start, rows), :], to, sems.at[d])
            )
            copies[-1].start()
        held[:, features:] = jnp.zeros((total, SIDE), BF16)
        for d, start in enumerate(starts):
            named = route_ref[pl.ds(start, rows), :].astype(F32).astype(BF16)
            held[d * rows : (d + 1) * rows, features : features + top] = named
        for copy in copies:
            copy.wait()
        leaving = pltpu.make_async_copy(held, out_ref, out_sem)
        leaving.start()
        leaving.wait()

    return pl.pallas_call(
        without(kernel, 3, len(deps)),
        out_shape=shape((total, features + SIDE), BF16),
        in_specs=[SMEM, HBM, VMEM] + [HBM] * len(deps),
        out_specs=HBM,
        scratch_shapes=[
            pltpu.VMEM((total, features + SIDE), BF16),
            pltpu.SemaphoreType.DMA((nt,)),
            pltpu.SemaphoreType.DMA,
        ],
        compiler_params=params(60),
        cost_estimate=cost(0.1),
        name="turn_rows",
    )(pos, array, routes, *deps)


def relay(parts, deps):
    return joins([[part] for part in parts], deps)


def halves(upper_of, lower_of, deps=()):
    rows, features = upper_of.shape
    half = rows // 2

    def kernel(upper_ref, lower_ref, upper_out, lower_out, buffer, sems):
        through(
            [
                (upper_ref.at[pl.ds(0, half), :], upper_out),
                (lower_ref.at[pl.ds(half, half), :], lower_out),
            ],
            buffer,
            sems,
        )

    return pl.pallas_call(
        without(kernel, 2, len(deps)),
        out_shape=[shape((half, features), upper_of.dtype)] * 2,
        in_specs=[HBM] * (2 + len(deps)),
        out_specs=[HBM] * 2,
        scratch_shapes=[
            pltpu.VMEM((rows, features), upper_of.dtype),
            pltpu.SemaphoreType.DMA((4,)),
        ],
        compiler_params=params(),
        cost_estimate=cost(0.1),
        name="halves",
    )(upper_of, lower_of, *deps)


def gather_near(block, size):
    if size != 8:
        return [swap(block, "fsdp", size, p) for p in range(1, size)]
    return [swap(block, "fsdp", size, 2), swap(block, "fsdp", size, 4)]


def gather_rest(block, near, size, deps=()):
    rows = block.shape[0]
    if size != 8:
        return [(p, 0, part, 0, rows) for p, part in enumerate([block] + near)]
    half = rows // 2
    upper, lower = halves(near[1], near[0], deps)
    front = swap(upper, "fsdp", size, 2)
    back = swap(lower, "fsdp", size, 4)
    pieces = []
    for k, part in enumerate([block] + near):
        pieces.append((2 * k, 0, part, 0, rows))
        pieces.append((2 * k + 1, 0, swap(part, "fsdp", size, 1), 0, rows))
    for row, part in ((0, front), (half, back)):
        pieces.append((6, row, part, 0, half))
        pieces.append((7, row, swap(part, "fsdp", size, 1), 0, half))
    return pieces


def gather_two(blocks, near, size, sources=None):
    pieces = []
    start = 0
    sources = sources or [near[0][1], near[1][0]]
    for block, (along_x, along_y), source, step in zip(blocks, near, sources, (2, 4)):
        rows = block.shape[0]
        last = swap(source, "fsdp", size, step)
        for index, part in ((0, block), (2, along_x), (4, along_y), (6, last)):
            pieces.append((index, start, part, 0, rows))
            pieces.append((index + 1, start, swap(part, "fsdp", size, 1), 0, rows))
        start += rows
    return pieces


def arrays_of(pieces):
    found = []
    for _, _, part, _, _ in pieces:
        if not any(part is other for other in found):
            found.append(part)
    return found


def start_fetch(pieces, refs, place, sems, own=None, columns=None):
    arrays = arrays_of(pieces)
    span = slice(None) if columns is None else pl.ds(*columns)
    copies = []
    for k, (index, row, part, at, rows) in enumerate(pieces):
        ref = next(ref for other, ref in zip(arrays, refs) if other is part)
        if at is None:
            at = pl.multiple_of((own ^ index) * rows, 16)
        copy = pltpu.make_async_copy(
            ref.at[pl.ds(at, rows), span], place(index, row, rows), sems.at[k]
        )
        copy.start()
        copies.append(copy)
    return copies


def pair_sums(keep, got, deps=()):
    _, rows, columns = keep.shape
    half = rows // 2

    def kernel(keep_ref, got_ref, out_x, out_y, held, sems):
        upper, lower = pl.ds(0, half), pl.ds(half, half)
        places = [(1, upper), (3, upper), (2, lower), (3, lower)]
        copies = fetch_parts([keep_ref.at[place] for place in places], held, sems)
        for k, place in enumerate(places):
            copies[k].wait()
            (out_x, out_y)[k // 2][k % 2] = (
                held[k].astype(F32) + got_ref[place].astype(F32)
            ).astype(BF16)

    return pl.pallas_call(
        without(kernel, 2, len(deps)),
        out_shape=[shape((2, half, columns), BF16)] * 2,
        in_specs=[HBM, VMEM] + [HBM] * len(deps),
        out_specs=[VMEM] * 2,
        scratch_shapes=[pltpu.VMEM((4, half, columns), BF16), pltpu.SemaphoreType.DMA((4,))],
        compiler_params=params(),
        cost_estimate=cost(0.1),
        name="pair_sums",
    )(*in_hbm([keep]), near_core(got), *in_hbm(deps))


def fetch_parts(parts, buffer, sems):
    copies = []
    for k, part in enumerate(parts):
        copies.append(pltpu.make_async_copy(part, buffer.at[k], sems.at[k]))
        copies[-1].start()
    return copies


def next_sums(keep, got, from_x, from_y, deps, micros):
    _, rows, columns = keep.shape
    half = rows // 2

    def kernel(keep_ref, got_ref, new_x, new_y, out_x, out_y, held, sems):
        upper, lower = pl.ds(0, half), pl.ds(half, half)
        places = [(2, upper), (1, lower)]
        copies = fetch_parts([keep_ref.at[place] for place in places], held, sems)
        for k, (new, out) in enumerate(((new_x, out_x), (new_y, out_y))):
            copies[k].wait()
            out[...] = (
                held[k].astype(F32) + got_ref[places[k]].astype(F32) + new[1].astype(F32)
            ).astype(BF16)

    return pl.pallas_call(
        without(kernel, 4, len(deps)),
        out_shape=[shape((half, columns), BF16)] * 2,
        in_specs=[HBM, VMEM, VMEM, VMEM] + [HBM] * len(deps),
        out_specs=[VMEM] * 2,
        scratch_shapes=[pltpu.VMEM((2, half, columns), BF16), pltpu.SemaphoreType.DMA((2,))],
        compiler_params=params(),
        cost_estimate=cost(micros),
        name="next_sums",
    )(*in_hbm([keep]), near_core(got), near_core(from_x), near_core(from_y), *in_hbm(deps))


def last_sums(keep, got, from_x, from_y, last_x, last_y, count, deps=()):
    _, rows, columns = keep.shape
    half = rows // 2
    part = rows // count
    each = half // part

    def kernel(keep_ref, got_ref, new_x, end_x, new_y, end_y, *refs):
        out_refs, (held, sems) = refs[:count], refs[count:]
        upper, lower = pl.ds(0, half), pl.ds(half, half)
        places = [(0, upper), (0, lower)]
        copies = fetch_parts([keep_ref.at[place] for place in places], held, sems)
        for k in range(count):
            side = k // each
            new, end = (new_x, end_x) if side == 0 else (new_y, end_y)
            if k % each == 0:
                copies[side].wait()
            first = (k % each) * part
            span = slice(first, first + part)
            from_got = slice(side * half + first, side * half + first + part)
            total = held[side, span].astype(F32) + got_ref[0, from_got].astype(F32)
            total = total + new[0, span].astype(F32) + end[span].astype(F32)
            out_refs[k][...] = total.astype(BF16)

    return pl.pallas_call(
        without(kernel, 6, len(deps)),
        out_shape=[shape((part, columns), BF16)] * count,
        in_specs=[HBM] + [VMEM] * 5 + [HBM] * len(deps),
        out_specs=[VMEM] * count,
        scratch_shapes=[pltpu.VMEM((2, half, columns), BF16), pltpu.SemaphoreType.DMA((2,))],
        compiler_params=params(),
        cost_estimate=cost(20),
        name="last_sums",
    )(
        *in_hbm([keep]), near_core(got), near_core(from_x), near_core(last_x), near_core(from_y), near_core(last_y),
        *in_hbm(deps),
    )


def column_sums(keep, got, from_x, from_y, last_x, last_y, widths, turned):
    _, rows, columns = keep.shape
    half = rows // 2

    def kernel(keep_x, got_x, new_x, end_x, keep_y, got_y, new_y, end_y, *out_refs):
        for k, refs in enumerate(((keep_x, got_x, new_x, end_x), (keep_y, got_y, new_y, end_y))):
            span = slice(k * half, (k + 1) * half)
            total = refs[0][0].astype(F32)
            for ref in refs[1:3]:
                total = total + ref[0].astype(F32)
            total = total + refs[3][...].astype(F32)
            column = 0
            for width, out_ref in zip(widths, out_refs):
                out_ref[span, :] = total[:, column : column + width]
                column += width
            if turned:
                out_refs[-1][:, span] = jnp.transpose(total[:, column : column + turned])

    block = (1, half, columns)
    first = pl.BlockSpec(block, lambda j: (0, 0, 0))
    second = pl.BlockSpec(block, lambda j: (0, 1, 0))
    end = pl.BlockSpec((half, columns), lambda j: (0, 0))
    shapes = [(rows, width) for width in widths] + [(turned, rows)] * (turned > 0)
    return pl.pallas_call(
        kernel,
        out_shape=[shape(dims, F32) for dims in shapes],
        grid=(1,),
        in_specs=[first, first, first, end, second, second, first, end],
        out_specs=[pl.BlockSpec(dims, lambda j: (0, 0)) for dims in shapes],
        compiler_params=params(),
        cost_estimate=cost(0.1),
        name="column_sums",
    )(keep, got, from_x, last_x, keep, got, from_y, last_y)


def halve(array, deps=()):
    rows, columns = array.shape
    half = columns // 2

    def kernel(ref, left_ref, right_ref):
        left_ref[...] = ref[:, :half]
        right_ref[...] = ref[:, half:]

    return pl.pallas_call(
        without(kernel, 1, len(deps)),
        out_shape=[shape((rows, half), array.dtype)] * 2,
        grid=(2,),
        in_specs=[pl.BlockSpec((rows // 2, columns), lambda j: (j, 0))] + [HBM] * len(deps),
        out_specs=[pl.BlockSpec((rows // 2, half), lambda j: (j, 0))] * 2,
        compiler_params=params(60),
        cost_estimate=cost(0.1),
        name="halve",
    )(array, *deps)


class Reduce:
    def __init__(self, keep, send, size):
        self.keep, self.send, self.size = keep, send, size
        if size == 8:
            self.got = swap(send, "fsdp", size, 1)

    def first(self, deps=()):
        if self.size != 8:
            return []
        self.pair = pair_sums(self.keep, self.got, deps)
        self.from_x = swap(self.pair[0], "fsdp", self.size, 2)
        self.from_y = swap(self.pair[1], "fsdp", self.size, 4)
        return list(self.pair[:1])

    def second(self, deps=(), micros=0.1):
        if self.size != 8:
            return []
        sums = next_sums(self.keep, self.got, self.from_x, self.from_y, deps, micros)
        self.last_x = swap(sums[0], "fsdp", self.size, 4)
        self.last_y = swap(sums[1], "fsdp", self.size, 2)
        return list(sums[:1])

    def total(self):
        if self.size != 8:
            total = self.keep[0].astype(F32)
            for p in range(1, self.size):
                block = self.keep[p // 2] if p % 2 == 0 else self.send[p // 2]
                total = total + swap(block, "fsdp", self.size, p).astype(F32)
            return total
        half = self.keep.shape[1] // 2
        sums = []
        for rows, new, last in (
            (slice(0, half), self.from_x, self.last_x),
            (slice(half, None), self.from_y, self.last_y),
        ):
            sums.append(
                self.keep[0, rows].astype(F32)
                + self.got[0, rows].astype(F32)
                + new[0].astype(F32)
                + last.astype(F32)
            )
        return jnp.concatenate(sums, axis=0)

    def columns(self, widths, turned=0):
        if self.size == 8:
            return column_sums(
                self.keep, self.got, self.from_x, self.from_y, self.last_x, self.last_y, widths, turned
            )
        total, found, column = self.total(), [], 0
        for width in widths:
            found.append(total[:, column : column + width])
            column += width
        return found + [total[:, column : column + turned].T] * (turned > 0)

    def rows(self, count, deps=()):
        if self.size != 8:
            return jnp.split(self.total().astype(BF16), count, axis=0)
        return last_sums(
            self.keep, self.got, self.from_x, self.from_y, self.last_x, self.last_y, count, deps
        )


def attend_forward(pos, tokens, cosine, sine, pieces, nf, nt, deps=()):
    length = tokens.shape[0]
    block = D // nf
    rows = length // nt
    columns = pieces[0][2].shape[1]
    width = (columns - SIDE) // 4
    heads = width // HD
    arrays = arrays_of(pieces)
    count = len(arrays)

    def kernel(pos_ref, x_ref, cos_ref, sin_ref, *refs):
        piece_refs, refs = refs[:count], refs[count:]
        n1_ref, qk_ref, rot_ref, v_ref, prob_ref, att_ref, side_ref, gain_ref, head_gain_ref = refs[:9]
        part_refs, (w, out, sems) = refs[9 : 9 + nt], refs[9 + nt :]
        f, t = pos_ref[0], pos_ref[1]

        def place(index, row, number, span):
            start = pl.multiple_of((f ^ index) * block + row, 16)
            return w.at[pl.ds(start, number), pl.ds(*span)]

        spans = ((4 * width, SIDE), (0, 3 * width), (3 * width, width))
        side, copies, later = [
            start_fetch(
                pieces, piece_refs, functools.partial(place, span=span), sems.at[k], columns=span
            )
            for k, span in enumerate(spans)
        ]
        x = x_ref[...].astype(F32)
        normed = x * rms_inverse(x)
        for copy in side:
            copy.wait()
        side_ref[...] = w[:, 4 * width :]
        turned = jnp.transpose(w[:, 4 * width :].astype(F32))
        gain_ref[...] = turned[EXPERTS : EXPERTS + 8]
        head_rows = turned[EXPERTS : EXPERTS + 8, :block]
        for p in range(1, nf):
            head_rows = head_rows + turned[EXPERTS : EXPERTS + 8, p * block : (p + 1) * block]
        head_gains = head_rows[:, :HD]
        head_gain_ref[...] = head_gains
        n1 = (normed * turned[EXPERTS : EXPERTS + 1]).astype(BF16)
        n1_ref[...] = n1
        for copy in copies:
            copy.wait()
        raw = dot(n1, w[:, : 3 * width])
        qk_ref[...] = raw[:, : 2 * width]
        v_ref[...] = raw[:, 2 * width :].astype(BF16)
        cos, sin = cos_ref[...], sin_ref[...]
        for h in range(heads):
            span = slice(h * HD, (h + 1) * HD)
            turned_rows = []
            for which in range(2):
                values = raw[:, which * width + h * HD : which * width + (h + 1) * HD]
                scaled = values * rms_inverse(values) * head_gains[2 + which : 3 + which]
                low = (scaled * cos + half_turn(scaled) * sin).astype(BF16)
                rot_ref[:, which * width + h * HD : which * width + (h + 1) * HD] = low
                turned_rows.append(low)
            scores = dot_nt(turned_rows[0], turned_rows[1]) * (HD**-0.5)
            shifted = jnp.exp(scores - jnp.max(scores, axis=-1, keepdims=True))
            probs = shifted / jnp.sum(shifted, axis=-1, keepdims=True)
            prob_ref[h] = probs
            att_ref[:, span] = dot(probs.astype(BF16), v_ref[:, span]).astype(BF16)
        for copy in later:
            copy.wait()
        out[...] = dot_nt(att_ref[...], w[:, 3 * width : 4 * width]).astype(BF16)
        for d in range(nt):
            start = pl.multiple_of((t ^ d) * rows, 16)
            part_refs[d][...] = out[pl.ds(start, rows), :]

    results = pl.pallas_call(
        without(kernel, 4 + count, len(deps)),
        out_shape=[
            shape((length, D), BF16),
            shape((length, 2 * width), F32),
            shape((length, 2 * width), BF16),
            shape((length, width), BF16),
            shape((heads, length, length), F32),
            shape((length, width), BF16),
            shape((D, SIDE), BF16),
            shape((8, D), F32),
            shape((8, HD), F32),
        ]
        + [shape((rows, D), BF16)] * nt,
        in_specs=[SMEM, VMEM, VMEM, VMEM] + [HBM] * (count + len(deps)),
        out_specs=[VMEM] * (9 + nt),
        scratch_shapes=[
            pltpu.VMEM((D, columns), BF16),
            pltpu.VMEM((length, D), BF16),
            pltpu.SemaphoreType.DMA((3, len(pieces))),
        ],
        compiler_params=params(60),
        cost_estimate=cost(5),
        name="attend_forward",
    )(pos, tokens, cosine, sine, *in_hbm(arrays), *deps)
    return results[:9], results[9:]


def attend_backward(pos, grad_rows, ffn_row, layer_sum, pieces, saved, tokens, cosine, sine, nf, nt, deps=()):
    _, qk, rot, values, probs, _, _, gains, head_gains = saved
    length = tokens.shape[0]
    block = D // nf
    rows = length // nt
    columns = pieces[0][2].shape[1]
    width = (columns - SIDE) // 4
    heads = width // HD
    more = gain_columns(rows)
    arrays = arrays_of(pieces)
    count = len(arrays)

    def kernel(pos_ref, x_ref, cos_ref, sin_ref, qk_ref, rot_ref, v_ref, prob_ref, gain_ref, head_gain_ref, ffn_ref, layer_ref, *refs):
        grad_refs, refs = refs[:nt], refs[nt:]
        piece_refs, refs = refs[:count], refs[count:]
        dqkv_ref = refs[0]
        part_refs, (w, out, db_ref, sems) = refs[1 : 1 + nt], refs[1 + nt :]
        f, t = pos_ref[0], pos_ref[1]

        def place(index, row, number, span):
            start = pl.multiple_of((f ^ index) * block + row, 16)
            return w.at[pl.ds(start, number), pl.ds(*span)]

        spans = ((3 * width, width), (0, 3 * width))
        copies, later = [
            start_fetch(
                pieces, piece_refs, functools.partial(place, span=span), sems.at[k], columns=span
            )
            for k, span in enumerate(spans)
        ]
        for d in range(nt):
            start = pl.multiple_of((t ^ d) * rows, 16)
            db_ref[pl.ds(start, rows), :] = grad_refs[d][:, :D]
        for copy in copies:
            copy.wait()
        cos, sin = cos_ref[...], sin_ref[...]
        head_gains = head_gain_ref[...]
        grad_att = dot(db_ref[...], w[:, 3 * width : 4 * width]).astype(BF16)
        gain_rows = [jnp.zeros((1, HD), F32), jnp.zeros((1, HD), F32)]
        for h in range(heads):
            span = slice(h * HD, (h + 1) * HD)
            query_low = rot_ref[:, span]
            key_low = rot_ref[:, width + h * HD : width + (h + 1) * HD]
            grad_out = grad_att[:, span]
            exact = prob_ref[h]
            grad_probs = dot_nt(grad_out, v_ref[:, span])
            row_terms = jnp.sum(exact * grad_probs, axis=-1, keepdims=True)
            grad_scores = (exact * (grad_probs - row_terms)).astype(BF16)
            dqkv_ref[:, 2 * width + h * HD : 2 * width + (h + 1) * HD] = dot_tn(
                exact.astype(BF16), grad_out
            ).astype(BF16)
            both = (dot(grad_scores, key_low), dot_tn(grad_scores, query_low))
            for which in range(2):
                span_w = slice(which * width + h * HD, which * width + (h + 1) * HD)
                grads = both[which] * (HD**-0.5)
                grads = grads * cos - half_turn(grads) * sin
                raw = qk_ref[:, span_w]
                inverse = rms_inverse(raw)
                gain_rows[which] = gain_rows[which] + jnp.sum(
                    grads * raw * inverse, axis=0, keepdims=True
                )
                dqkv_ref[:, span_w] = norm_backward(
                    raw, inverse, head_gains[2 + which : 3 + which], grads
                ).astype(BF16)
        for copy in later:
            copy.wait()
        grad_normed = dot_nt(dqkv_ref[...], w[:, : 3 * width])
        out[...] = grad_normed.astype(BF16)
        x = x_ref[...].astype(F32)
        row = jnp.sum(grad_normed * (x * rms_inverse(x)), axis=0, keepdims=True)
        lines = [row[:, k * SIDE : (k + 1) * SIDE] for row in (ffn_ref[0:1, :], row) for k in range(D // SIDE)]
        lines = lines + gain_rows
        gain_blocks = []
        for k in range(more // SIDE):
            own = lines[k * rows : (k + 1) * rows]
            blank = [jnp.zeros((rows - len(own), SIDE), F32)] if len(own) < rows else []
            gain_blocks.append(jnp.concatenate(own + blank, axis=0).astype(BF16))
        for d in range(nt):
            start = pl.multiple_of((t ^ d) * rows, 16)
            part_refs[d][:, :D] = out[pl.ds(start, rows), :]
            for k, gain_block in enumerate(gain_blocks):
                part_refs[d][:, D + k * SIDE : D + (k + 1) * SIDE] = gain_block
            part_refs[d][:, D + more :] = layer_ref[pl.ds(start, rows), :]

    results = pl.pallas_call(
        without(kernel, 12 + nt + count, len(deps)),
        out_shape=[
            shape((length, 3 * width), BF16),
        ]
        + [shape((rows, 2 * D + more), BF16)] * nt,
        in_specs=[SMEM] + [VMEM] * (11 + nt) + [HBM] * (count + len(deps)),
        out_specs=[VMEM] * (1 + nt),
        scratch_shapes=[
            pltpu.VMEM((D, columns), BF16),
            pltpu.VMEM((length, D), BF16),
            pltpu.VMEM((length, D), BF16),
            pltpu.SemaphoreType.DMA((2, len(pieces))),
        ],
        compiler_params=params(60),
        cost_estimate=cost(0.1),
        name="attend_backward",
    )(
        pos, tokens, cosine, sine, qk, rot, values, probs, gains, head_gains, ffn_row, layer_sum,
        *grad_rows, *in_hbm(arrays), *deps,
    )
    return results[0], results[1:]


def projection_gradients(pos, normed, dqkv, nf, deps=()):
    length = normed.shape[0]
    block = D // nf
    width = dqkv.shape[1]

    def kernel(pos_ref, n1_ref, dqkv_ref, keep_ref, send_ref):
        for p in range(nf):
            start = pl.multiple_of((pos_ref[0] ^ p) * block, 128)
            to = (keep_ref if p % 2 == 0 else send_ref).at[p // 2]
            to[...] = dot_tn(n1_ref[:, pl.ds(start, block)], dqkv_ref[...]).astype(BF16)

    return pl.pallas_call(
        without(kernel, 3, len(deps)),
        out_shape=[shape((nf // 2, block, width), BF16)] * 2,
        in_specs=[SMEM, VMEM, VMEM] + [HBM] * len(deps),
        out_specs=[VMEM] * 2,
        compiler_params=params(40),
        cost_estimate=cost(0.1),
        name="projection_gradients",
    )(pos, normed, dqkv, *deps)


def output_gradients(pos, attended, grad_parts, normed_parts, gain_parts, group, nf, nt, deps=()):
    length, width = attended.shape
    rows = length // nt
    block = D // nf
    columns = width + SIDE
    more = gain_columns(rows)
    count = D // SIDE

    def kernel(pos_ref, att_ref, *refs):
        grad_refs, normed_refs, part_refs = refs[:nt], refs[nt : 2 * nt], refs[2 * nt : 3 * nt]
        keep_ref, send_ref, db, n2, held, gain_ref = refs[3 * nt :]
        f, t = pos_ref[0], pos_ref[1]
        for d in range(nt):
            start = pl.multiple_of((t ^ d) * rows, 16)
            db[pl.ds(start, rows), :] = grad_refs[d][...]
            n2[pl.ds(start, rows), :] = normed_refs[d][:, :D]
            held[t ^ d] = part_refs[d][:, D : D + more].astype(F32)
        total = held[0]
        for k in range(1, nt):
            total = total + held[k]
        for line in range(2 * count + 2):
            column, at = line // rows * SIDE, line % rows
            to = line // count if line < 2 * count else line - 2 * count + 2
            lane = line % count * SIDE if line < 2 * count else 0
            gain_ref[to : to + 1, lane : lane + SIDE] = total[at : at + 1, column : column + SIDE]
        lane = lanes((block, SIDE))
        sub = lax.broadcasted_iota(jnp.int32, (block, SIDE), 0)
        for p in range(nf):
            owner = f ^ p
            start = pl.multiple_of(owner * block, 128)
            to = (keep_ref if p % 2 == 0 else send_ref).at[p // 2]
            to[:, :width] = dot_tn(db[:, pl.ds(start, block)], att_ref[...]).astype(BF16)
            side = dot_tn(n2[:, pl.ds(start, block)], db[:, D:])
            for which in range(2):
                row = gain_ref[which : which + 1, pl.ds(start, block)]
                column = jnp.transpose(jnp.broadcast_to(row, (SIDE, block)))
                side = jnp.where(lane == EXPERTS + which, column, side)
            mine = (lane == owner * group + sub) & (sub < group)
            for which in range(2, 4):
                spread = jnp.where(mine, gain_ref[which : which + 1, :HD], 0.0)
                column = jnp.sum(spread, axis=1, keepdims=True)
                side = jnp.where(lane == EXPERTS + which, column, side)
            to[:, width:] = side.astype(BF16)

    return pl.pallas_call(
        without(kernel, 2 + 3 * nt, len(deps)),
        out_shape=[shape((nf // 2, block, columns), BF16)] * 2,
        in_specs=[SMEM] + [VMEM] * (1 + 3 * nt) + [HBM] * len(deps),
        out_specs=[VMEM] * 2,
        scratch_shapes=[
            pltpu.VMEM((length, D + SIDE), BF16),
            pltpu.VMEM((length, D), BF16),
            pltpu.VMEM((nt, rows, more), F32),
            pltpu.VMEM((8, D), F32),
        ],
        compiler_params=params(40),
        cost_estimate=cost(0.1),
        name="output_gradients",
    )(pos, attended, *grad_parts, *normed_parts, *gain_parts, *deps)


def gain_columns(rows):
    return SIDE * -(-(2 * D // SIDE + 2) // rows)


def norm_and_route(pos, tokens, routes, parts, gains, side, nt, deps=()):
    rows = tokens.shape[0] // nt
    top = routes.shape[1]

    def kernel(pos_ref, route_all, x_all, gain_all, side_all, first_all, *refs):
        part_refs, refs = refs[: nt - 1], refs[nt - 1 :]
        h_ref, next_ref, gate_ref, x_ref, gain_ref, side_ref, first_ref, sems = refs
        mine = pl.ds(pl.multiple_of(pos_ref[1] * rows, 16), rows)
        copies = [
            pltpu.make_async_copy(source, target, sems.at[k])
            for k, (source, target) in enumerate(
                (
                    (x_all.at[mine, :], x_ref),
                    (first_all, first_ref),
                    (gain_all, gain_ref),
                    (side_all, side_ref),
                )
            )
        ]
        for copy in copies:
            copy.start()
        route_ref = route_all.at[mine, :]
        copies[0].wait()
        copies[1].wait()
        h = x_ref[...].astype(F32) + first_ref[...].astype(F32)
        for ref in part_refs:
            h = h + ref[...].astype(F32)
        h_ref[...] = h
        copies[2].wait()
        copies[3].wait()
        n2 = (h * rms_inverse(h) * gain_ref[1:2]).astype(BF16)
        next_ref[:, :D] = n2
        logits = dot(n2, side_ref[...])
        lane = lanes((rows, SIDE))
        chosen = route_ref[:, 0:1] == lane
        for j in range(1, top):
            chosen = chosen | (route_ref[:, j : j + 1] == lane)
        highest = jnp.max(jnp.where(chosen, logits, -jnp.inf), axis=-1, keepdims=True)
        shifted = jnp.where(chosen, jnp.exp(jnp.where(chosen, logits - highest, 0.0)), 0.0)
        gates = shifted / jnp.sum(shifted, axis=-1, keepdims=True)
        gate_ref[...] = gates
        first = gates.astype(BF16).astype(F32)
        rest = (gates - first).astype(BF16).astype(F32)
        next_ref[:, D:] = (first + pltpu.roll(rest, EXPERTS, 1)).astype(BF16)

    return pl.pallas_call(
        without(kernel, 5 + nt, len(deps)),
        out_shape=[shape((rows, D), F32), shape((rows, D + SIDE), BF16), shape((rows, SIDE), F32)],
        in_specs=[SMEM, VMEM] + [HBM] * 4 + [VMEM] * (nt - 1) + [HBM] * len(deps),
        out_specs=[VMEM] * 3,
        scratch_shapes=[
            pltpu.VMEM((rows, D), BF16),
            pltpu.VMEM((8, D), F32),
            pltpu.VMEM((D, SIDE), BF16),
            pltpu.VMEM((rows, D), BF16),
            pltpu.SemaphoreType.DMA((4,)),
        ],
        compiler_params=params(60),
        cost_estimate=cost(100),
        name="norm_and_route",
    )(
        pos, routes, *in_hbm([tokens, gains, side, parts[0]]),
        *[near_core(part) for part in parts[1:]], *in_hbm(deps),
    )


def norm_back(pos, cotangent, parts, h, gates, gains, side, nt, deps=()):
    rows = h.shape[0]

    def kernel(pos_ref, cot_ref, h_ref, gate_ref, gain_ref, side_ref, *refs):
        part_refs, (dh_ref, db_ref, row_ref) = refs[:nt], refs[nt:]
        total = part_refs[0][...].astype(F32)
        for ref in part_refs[1:]:
            total = total + ref[...].astype(F32)
        pair = total[:, D:]
        pair = pair + pltpu.roll(pair, EXPERTS, 1)
        gates = gate_ref[...]
        grads = gates * (pair - jnp.sum(gates * pair, axis=-1, keepdims=True))
        low = grads.astype(BF16)
        dn2 = total[:, :D] + dot_nt(low, side_ref[...])
        h = h_ref[...]
        inverse = rms_inverse(h)
        gain_row = jnp.sum(dn2 * h * inverse, axis=0, keepdims=True)
        row_ref[...] = jnp.broadcast_to(gain_row, (8, D))
        dh = cot_ref[...].astype(F32) + norm_backward(h, inverse, gain_ref[1:2], dn2)
        dh_ref[...] = dh
        db_ref[:, :D] = dh.astype(BF16)
        db_ref[:, D:] = low

    whole = lambda i, pos: (0, 0)
    mine = lambda i, pos: (pos[1], 0)
    return pl.pallas_call(
        without(kernel, 6 + nt, len(deps)),
        out_shape=[shape((rows, D), F32), shape((rows, D + SIDE), BF16), shape((8, D), F32)],
        grid_spec=pltpu.PrefetchScalarGridSpec(
            num_scalar_prefetch=1,
            grid=(1,),
            in_specs=[
                pl.BlockSpec((rows, D), mine),
                pl.BlockSpec((rows, D), whole),
                pl.BlockSpec((rows, SIDE), whole),
                pl.BlockSpec((8, D), whole),
                pl.BlockSpec((D, SIDE), whole),
            ]
            + [pl.BlockSpec((rows, D + SIDE), whole)] * nt
            + [HBM] * len(deps),
            out_specs=[
                pl.BlockSpec((rows, D), whole),
                pl.BlockSpec((rows, D + SIDE), whole),
                pl.BlockSpec((8, D), whole),
            ],
        ),
        compiler_params=params(),
        cost_estimate=cost(100),
        name="norm_back",
    )(pos, cotangent, h, gates, gains, side, *parts, *in_hbm(deps))


def last_rows(pos, tokens, parts, dh, h, gains, nt, deps=()):
    rows = dh.shape[0]
    columns = parts[0].shape[1]

    def kernel(pos_ref, x_all, dh_all, h_all, gain_all, first_all, *refs):
        part_refs, refs = refs[: nt - 1], refs[nt - 1 :]
        out_ref, x_ref, dh_ref, h_ref, gain_ref, first_ref, sems = refs
        mine = pl.ds(pl.multiple_of(pos_ref[1] * rows, 16), rows)
        copies = [
            pltpu.make_async_copy(source, target, sems.at[k])
            for k, (source, target) in enumerate(
                (
                    (first_all, first_ref),
                    (x_all.at[mine, :], x_ref),
                    (gain_all, gain_ref),
                    (h_all, h_ref),
                    (dh_all, dh_ref),
                )
            )
        ]
        for copy in copies:
            copy.start()
        for copy in copies:
            copy.wait()
        total = first_ref[:, :D].astype(F32)
        layer = h_ref[...] + first_ref[:, columns - D :].astype(F32)
        for ref in part_refs:
            total = total + ref[:, :D].astype(F32)
            layer = layer + ref[:, columns - D :].astype(F32)
        x = x_ref[...].astype(F32)
        out_ref[:, :D] = (
            dh_ref[...] + norm_backward(x, rms_inverse(x), gain_ref[0:1], total)
        ).astype(BF16)
        out_ref[:, D:] = layer.astype(BF16)

    return pl.pallas_call(
        without(kernel, 5 + nt, len(deps)),
        out_shape=shape((rows, 2 * D), BF16),
        in_specs=[SMEM] + [HBM] * 5 + [VMEM] * (nt - 1) + [HBM] * len(deps),
        out_specs=VMEM,
        scratch_shapes=[
            pltpu.VMEM((rows, D), BF16),
            pltpu.VMEM((rows, D), F32),
            pltpu.VMEM((rows, D), F32),
            pltpu.VMEM((8, D), F32),
            pltpu.VMEM((rows, columns), BF16),
            pltpu.SemaphoreType.DMA((5,)),
        ],
        compiler_params=params(60),
        cost_estimate=cost(100),
        name="last_rows",
    )(
        pos, *in_hbm([tokens, dh, h, gains, parts[0]]),
        *[near_core(part) for part in parts[1:]], *in_hbm(deps),
    )


def place_rows(pos, parts):
    nt = len(parts)
    rows, columns = parts[0].shape
    half = columns // 2

    def kernel(pos_ref, *refs):
        left_ref, right_ref = refs[nt:]
        for d in range(nt):
            start = pl.multiple_of((pos_ref[1] ^ d) * rows, 16)
            left_ref[pl.ds(start, rows), :] = refs[d][:, :half]
            right_ref[pl.ds(start, rows), :] = refs[d][:, half:]

    return pl.pallas_call(
        kernel,
        out_shape=[shape((rows * nt, half), parts[0].dtype)] * 2,
        in_specs=[SMEM] + [VMEM] * nt,
        out_specs=[VMEM] * 2,
        compiler_params=params(),
        cost_estimate=cost(0.1),
        name="place_rows",
    )(pos, *parts)


def spread_rows(slots, source, target, pair, number, cut):
    for begin in range(0, source.shape[2], cut):
        span = slice(begin, min(begin + cut, source.shape[2]))
        two = [dot_tn(slots[2 * pair + k], source[2 * pair + k, :, span]) for k in range(2)]
        for e in range(number):
            joined = jnp.concatenate([rows[e * CAP : (e + 1) * CAP] for rows in two], axis=0)
            target(e, span, joined)


def sum_rows(slots, results, target, pair, number, total, cut):
    at = slice(pair * 2 * CAP, (pair + 1) * 2 * CAP)
    for begin in range(0, total, cut):
        span = slice(begin, min(begin + cut, total))
        blocks = [results[e, at, span].astype(F32) for e in range(number)]
        for k in range(2):
            rows = jnp.concatenate([b[k * CAP : (k + 1) * CAP] for b in blocks], axis=0)
            target[2 * pair + k, :, span] = dot(slots[2 * pair + k], rows.astype(BF16)).astype(BF16)


def route_cotangent(pos, pieces, weights, nf, top, deps=()):
    number = weights.shape[0]
    length = sum(rows for index, _, _, _, rows in pieces if index == 0)
    slots = number * CAP
    arrays = arrays_of(pieces)
    count = len(arrays)

    def kernel(pos_ref, *refs):
        piece_refs, (slot_ref, rows_ref, cot, spread, sems, out_sems) = refs[:count], refs[count:]
        f = pos_ref[0]
        copies = start_fetch(
            pieces, piece_refs, lambda i, row, n: cot.at[i, pl.ds(row, n), :], sems, f
        )
        column = lanes((length, slots))
        expert = jnp.zeros((length, slots), jnp.int32)
        for k in range(1, number):
            expert = expert + (column >= k * CAP).astype(jnp.int32)
        rank = (column - expert * CAP + 1).astype(F32)
        expert = (expert + f * number).astype(F32)
        lower = (
            lax.broadcasted_iota(jnp.int32, (length, length), 0) >= lanes((length, length))
        ).astype(F32).astype(BF16)
        for copy in copies:
            copy.wait()

        def leave(pair):
            span = pl.ds(pl.multiple_of(pair * 2 * CAP, 16), 2 * CAP)
            return pltpu.make_async_copy(
                spread.at[:, span, :], rows_ref.at[:, span, :], out_sems.at[pair]
            )

        @pl.loop(0, nf // 2)
        def _(pair):
            for s in (2 * pair, 2 * pair + 1):
                named = cot[s, :, D:].astype(F32)
                hit = named[:, 0:1] == expert
                for j in range(1, top):
                    hit = hit | (named[:, j : j + 1] == expert)
                hit = jnp.where(hit, 1.0, 0.0)
                so_far = dot(lower, hit.astype(BF16))
                slot_ref[s] = jnp.where((so_far == rank) & (hit > 0.0), 1.0, 0.0).astype(BF16)
            at = pl.ds(pl.multiple_of(pair * 2 * CAP, 16), 2 * CAP)

            def put(k, span, rows):
                spread[k, at, span] = rows.astype(BF16)

            spread_rows(slot_ref, cot.at[:, :, :D], put, pair, number, 512)
            leave(pair).start()

        for pair in range(nf // 2):
            leave(pair).wait()

    return pl.pallas_call(
        without(kernel, 1 + count, len(deps)),
        out_shape=[
            shape((nf, length, slots), BF16),
            shape((number, nf * CAP, D), BF16),
        ],
        in_specs=[SMEM] + [HBM] * (count + len(deps)),
        out_specs=[VMEM, HBM],
        scratch_shapes=[
            pltpu.VMEM((nf, length, D + SIDE), BF16),
            pltpu.VMEM((number, nf * CAP, D), BF16),
            pltpu.SemaphoreType.DMA((len(pieces),)),
            pltpu.SemaphoreType.DMA((nf // 2,)),
        ],
        compiler_params=params(60),
        cost_estimate=cost(0.1),
        name="route_cotangent",
    )(pos, *in_hbm(arrays), *deps)


def down_back(grad_rows, weights, deps=()):
    number, filled, _ = grad_rows.shape
    width = weights.shape[3]

    def kernel(rows_ref, w_ref, out_ref):
        for k in range(2):
            out_ref[k] = dot(rows_ref[k], w_ref[k, 0])

    return pl.pallas_call(
        without(kernel, 2, len(deps)),
        out_shape=shape((number, filled, width), F32),
        grid=(number // 2,),
        in_specs=[
            pl.BlockSpec((2, filled, D), lambda e: (e, 0, 0)),
            pl.BlockSpec((2, 1, D, width), lambda e: (e, 2, 0, 0)),
        ]
        + [HBM] * len(deps),
        out_specs=pl.BlockSpec((2, filled, width), lambda e: (e, 0, 0)),
        compiler_params=params(60),
        cost_estimate=cost(0.1),
        name="down_back",
    )(grad_rows, weights, *deps)


def run_experts(pos, pieces, slot_table, down, weights, nf, cut):
    number, _, _, width = weights.shape
    length, slots = slot_table.shape[1:]
    filled = nf * CAP
    arrays = arrays_of(pieces)
    count = len(arrays)

    def kernel(pos_ref, slot_ref, down_ref, gate_w, up_w, *refs):
        piece_refs, refs = refs[:count], refs[count:]
        rows_ref, dg_ref, du_ref, hidden_ref = refs[:4]
        sums_refs = (refs[4:6], refs[6:8])
        wide, spread, gates, results, sems, rows_sem, out_sems = refs[8:]
        e = pl.program_id(0)
        f = pos_ref[0]
        rows_out = pltpu.make_async_copy(spread, rows_ref, rows_sem)

        @pl.when(e == 0)
        def _():
            copies = start_fetch(
                pieces, piece_refs, lambda i, row, n: wide.at[i, pl.ds(row, n), :], sems
            )
            for pair in range(nf // 2):
                for (index, _, _, _, _), copy in zip(pieces, copies):
                    if index // 2 == pair:
                        copy.wait()
                at = slice(pair * 2 * CAP, (pair + 1) * 2 * CAP)

                def put(k, span, rows):
                    if span.start < D:
                        spread[k, at, span] = rows.astype(BF16)
                    else:
                        lane = lanes((2 * CAP, SIDE))
                        own = f * number + k
                        gate = jnp.where((lane == own) | (lane == own + EXPERTS), rows, 0.0)
                        gates[k, at, :] = jnp.broadcast_to(
                            jnp.sum(gate, axis=-1, keepdims=True), (2 * CAP, SIDE)
                        )

                spread_rows(slot_ref, wide, put, pair, number, 512)
            rows_out.start()

        for k in range(2):
            index = 2 * e + k
            rows = spread[index]
            first, second = gate_w[k, 0], up_w[k, 0]
            gate_pre = dot(rows, first)
            up_pre = dot(rows, second)
            gate = gates[index][:, 0:1]
            sigma = jax.nn.sigmoid(gate_pre)
            swish = gate_pre * sigma
            hidden = (swish * up_pre).astype(BF16).astype(F32)
            hidden_ref[k] = (gate * hidden).astype(BF16)
            unscaled = down_ref[k]
            grad_hidden = gate * unscaled
            dg = (grad_hidden * up_pre * sigma * (1.0 + gate_pre * (1.0 - sigma))).astype(BF16)
            du = (grad_hidden * swish).astype(BF16)
            dg_ref[k] = dg
            du_ref[k] = du
            results[index, :, :D] = (dot_nt(dg, first) + dot_nt(du, second)).astype(BF16)
            pair_grad = jnp.sum(unscaled * hidden, axis=-1, keepdims=True)
            high = pair_grad.astype(BF16).astype(F32)
            lane = lanes((filled, SIDE))
            own = f * number + index
            results[index, :, D:] = jnp.where(
                lane == own, high, jnp.where(lane == own + EXPERTS, pair_grad - high, 0.0)
            ).astype(BF16)

        @pl.when(e == number // 2 - 1)
        def _():
            copies = []
            for pair in range(nf // 2):
                sum_rows(slot_ref, results, wide, pair, number, D + SIDE, 512)
                for k, to in enumerate(sums_refs):
                    index = 2 * pair + k
                    for g, span in enumerate((pl.ds(0, cut), pl.ds(cut, length - cut))):
                        copy = pltpu.make_async_copy(
                            wide.at[index, span, :], to[g].at[pair], out_sems.at[2 * index + g]
                        )
                        copy.start()
                        copies.append(copy)
            for copy in copies:
                copy.wait()
            rows_out.wait()

    return pl.pallas_call(
        kernel,
        out_shape=[
            shape((number, filled, D), BF16),
            shape((number, filled, width), BF16),
            shape((number, filled, width), BF16),
            shape((number, filled, width), BF16),
        ]
        + [shape((nf // 2, number, D + SIDE), BF16) for number in (cut, length - cut)] * 2,
        grid_spec=pltpu.PrefetchScalarGridSpec(
            num_scalar_prefetch=1,
            grid=(number // 2,),
            in_specs=[
                pl.BlockSpec((nf, length, slots), lambda e, pos: (0, 0, 0)),
                pl.BlockSpec((2, filled, width), lambda e, pos: (e, 0, 0)),
                pl.BlockSpec((2, 1, D, width), lambda e, pos: (e, 0, 0, 0)),
                pl.BlockSpec((2, 1, D, width), lambda e, pos: (e, 1, 0, 0)),
            ]
            + [HBM] * count,
            out_specs=[
                HBM,
                pl.BlockSpec((2, filled, width), lambda e, pos: (e, 0, 0)),
                pl.BlockSpec((2, filled, width), lambda e, pos: (e, 0, 0)),
                pl.BlockSpec((2, filled, width), lambda e, pos: (e, 0, 0)),
            ]
            + [HBM] * 4,
            scratch_shapes=[
                pltpu.VMEM((nf, length, D + SIDE), BF16),
                pltpu.VMEM((number, filled, D), BF16),
                pltpu.VMEM((number, filled, SIDE), F32),
                pltpu.VMEM((number, filled, D + SIDE), BF16),
                pltpu.SemaphoreType.DMA((len(pieces),)),
                pltpu.SemaphoreType.DMA,
                pltpu.SemaphoreType.DMA((2 * nf,)),
            ],
        ),
        compiler_params=params(60),
        cost_estimate=cost(5),
        name="run_experts",
    )(pos, slot_table, down, weights, weights, *in_hbm(arrays))


def expert_outputs(pos, slot_table, hidden, weights, nt, deps=()):
    number, filled, width = hidden.shape
    nf, length, slots = slot_table.shape

    rows = length // nt

    def kernel(pos_ref, slot_ref, hidden_ref, w_ref, out_ref, results, out, sems):
        e = pl.program_id(0)
        for k in range(2):
            results[2 * e + k] = dot_nt(hidden_ref[k], w_ref[k, 0]).astype(BF16)

        @pl.when(e == number // 2 - 1)
        def _():
            copies = []
            for pair in range(nf // 2):
                sum_rows(slot_ref, results, out, pair, number, D, 512)
                for index in (2 * pair, 2 * pair + 1):
                    for d in range(nt):
                        start = pl.multiple_of((pos_ref[1] ^ d) * rows, 16)
                        copy = pltpu.make_async_copy(
                            out.at[index, pl.ds(d * rows, rows), :],
                            out_ref.at[pos_ref[0] ^ index, pl.ds(start, rows), :],
                            sems.at[index * nt + d],
                        )
                        copy.start()
                        copies.append(copy)
            for copy in copies:
                copy.wait()

    return pl.pallas_call(
        without(kernel, 4, len(deps)),
        out_shape=shape((nf, length, D), BF16),
        grid_spec=pltpu.PrefetchScalarGridSpec(
            num_scalar_prefetch=1,
            grid=(number // 2,),
            in_specs=[
                pl.BlockSpec((nf, length, slots), lambda e, pos: (0, 0, 0)),
                pl.BlockSpec((2, filled, width), lambda e, pos: (e, 0, 0)),
                pl.BlockSpec((2, 1, D, width), lambda e, pos: (e, 2, 0, 0)),
            ]
            + [HBM] * len(deps),
            out_specs=HBM,
            scratch_shapes=[
                pltpu.VMEM((number, filled, D), BF16),
                pltpu.VMEM((nf, length, D), BF16),
                pltpu.SemaphoreType.DMA((nf * nt,)),
            ],
        ),
        compiler_params=params(48),
        cost_estimate=cost(0.1),
        name="expert_outputs",
    )(pos, slot_table, hidden, weights, *deps)


def expert_gradients(rows, grad_rows, dg, du, hidden, first, number, so_far=None, deps=()):
    everyone, filled, width = dg.shape

    def kernel(rows_ref, grad_ref, dg_ref, du_ref, hidden_ref, *refs):
        out_ref, done_ref = refs
        done_ref[...] = jnp.zeros_like(done_ref)
        rows = rows_ref[0]
        out_ref[0, 0] = dot_tn(rows, dg_ref[0])
        out_ref[0, 1] = dot_tn(rows, du_ref[0])
        out_ref[0, 2] = dot_tn(grad_ref[0], hidden_ref[0])

    tall = pl.BlockSpec((1, filled, D), lambda e: (first + e, 0, 0))
    thin = pl.BlockSpec((1, filled, width), lambda e: (first + e, 0, 0))
    before = [] if so_far is None else [so_far]
    return pl.pallas_call(
        without(kernel, 5, len(before) + len(deps)),
        out_shape=[shape((everyone, 3, D, width), F32), shape((8, SIDE), F32)],
        grid=(number,),
        in_specs=[tall, tall, thin, thin, thin] + [HBM] * (len(before) + len(deps)),
        out_specs=[
            pl.BlockSpec((1, 3, D, width), lambda e: (first + e, 0, 0, 0)),
            pl.BlockSpec((8, SIDE), lambda e: (0, 0)),
        ],
        input_output_aliases={5: 0} if before else {},
        compiler_params=params(48),
        cost_estimate=cost(0.1),
        name="expert_gradients",
    )(rows, grad_rows, dg, du, hidden, *before, *deps)


def on_device(
    nf,
    nt,
    tokens,
    cotangent,
    routes,
    w_query,
    w_key,
    w_value,
    w_output,
    w_router,
    attn_gain,
    ffn_gain,
    query_gain,
    key_gain,
    expert_weights,
):
    length = tokens.shape[0]
    rows = length // nt
    block = D // nf
    group = query_gain.shape[0]
    top = routes.shape[1]
    f = lax.axis_index("fsdp").astype(jnp.int32)
    t = lax.axis_index("tensor").astype(jnp.int32)
    pos = jnp.stack([f, t])

    def placed(gain):
        return lax.dynamic_update_slice(jnp.zeros((block,), BF16), gain, (f * group,))[:, None]

    columns = [
        w_query,
        w_key,
        w_value,
        w_output,
        w_router,
        attn_gain[:, None],
        ffn_gain[:, None],
        placed(query_gain),
        placed(key_gain),
        jnp.zeros((block, SIDE - EXPERTS - 4), BF16),
    ]
    number = expert_weights.shape[0]
    cut = 2 * rows

    def around(block):
        return [block] + [swap(block, "tensor", nt, d) for d in range(1, nt)]

    def sent(parts):
        return [parts[0]] + [swap(parts[d], "tensor", nt, d) for d in range(1, nt)]

    if nf == 8:
        packed = [
            jnp.concatenate([part[half : half + block // 2] for part in columns], axis=1)
            for half in (0, block // 2)
        ]
        weights_near = [gather_near(part, nf) for part in packed]
    else:
        packed = jnp.concatenate(columns, axis=1)

    inverse = ROPE_BASE ** (-np.arange(HD // 2) / (HD // 2))
    angles = np.arange(length)[:, None] * inverse[None, :]
    cosine = jnp.asarray(np.concatenate([np.cos(angles)] * 2, axis=1), F32)
    sine = jnp.asarray(np.concatenate([-np.sin(angles), np.sin(angles)], axis=1), F32)

    if nf == 8:
        weights = gather_two(packed, weights_near, nf)
        ready = [w[2] for w in weights if w[0] not in (0, nf - 1)]
    else:
        weights = gather_rest(packed, gather_near(packed, nf), nf)
        ready = []
    wide_cot = turn_rows(pos, cotangent, routes, nt, ready)
    all_cot = lax.all_gather(wide_cot, "fsdp", axis=0, tiled=True)
    cot = [(p, 0, all_cot, None, length) for p in range(nf)]
    saved, parts = attend_forward(pos, tokens, cosine, sine, weights, nf, nt)
    normed_one, _, _, _, _, attended, side, gains, _ = saved
    parts = sent(parts)
    h, normed_two, gates = norm_and_route(pos, tokens, routes, parts, gains, side, nt)

    normed_parts = around(normed_two)
    if nf == 8:
        blocks = [join(normed_parts[:2])]
        near = [gather_near(blocks[0], nf)]
        slot_table, cot_rows = route_cotangent(pos, cot, expert_weights, nf, top, deps=blocks)
        blocks.append(join(normed_parts[2:], deps=[slot_table]))
        near.append(gather_near(blocks[1], nf))
        down = down_back(cot_rows, expert_weights, deps=blocks[1:])
        sources = [near[0][1]] + list(relay(near[1][:1], [down]))
        n2_pieces = gather_two(blocks, near, nf, sources)
    else:
        slot_table, cot_rows = route_cotangent(pos, cot, expert_weights, nf, top)
        down = down_back(cot_rows, expert_weights)
        joined = join(normed_parts)
        n2_pieces = gather_rest(joined, gather_near(joined, nf), nf)
    n2_rows, dg, du, hidden, keep_near, keep_far, send_near, send_far = run_experts(
        pos, n2_pieces, slot_table, down, expert_weights, nf, cut
    )

    far, near = Reduce(keep_far, send_far, nf), Reduce(keep_near, send_near, nf)
    began = far.first() + near.first()
    outputs = expert_outputs(pos, slot_table, hidden, expert_weights, nt, deps=began)
    layer_sum = lax.psum_scatter(
        outputs.reshape(nf * length, D), "fsdp", scatter_dimension=0, tiled=True
    )
    went = far.second(deps=[outputs], micros=20)
    near.second(deps=went, micros=20)
    far_rows = list(far.rows(nt - 2))
    near_rows = list(near.rows(2, deps=far_rows[:1]))
    grad_parts = sent(near_rows + far_rows)
    each = number // 2

    def expert_part(k, deps=()):
        return expert_gradients(
            n2_rows, cot_rows, dg, du, hidden, k * each, each, grad_experts, deps
        )

    grad_experts = None
    grad_experts, done = expert_part(0, near_rows[:1])
    dh, db, ffn_row = norm_back(
        pos, cotangent, grad_parts, h, gates, gains, side, nt, deps=[done]
    )
    db_parts = around(db)
    grad_experts, done = expert_part(1, [db])
    dqkv, parts = attend_backward(
        pos, db_parts, ffn_row, layer_sum, weights, saved, tokens, cosine, sine, nf, nt,
        deps=[done],
    )
    parts = sent(parts)
    keep, send = projection_gradients(pos, normed_one, dqkv, nf)
    projections = Reduce(keep, send, nf)
    both_rows = last_rows(pos, tokens, parts, dh, h, gains, nt, deps=[keep])
    gathered = lax.all_gather(both_rows, "tensor", axis=0, tiled=True)
    pairs = projections.first(deps=[both_rows])
    keep, send = output_gradients(
        pos, attended, db_parts, normed_parts, parts, group, nf, nt, deps=pairs
    )
    output = Reduce(keep, send, nf)
    output.first()
    projections.second()
    output.second()
    width = attended.shape[1]
    grad_query, grad_key, grad_value = projections.columns([width] * 3)
    grad_output, side_grads = output.columns([width], SIDE)
    grad_tokens, layer_out = halve(gathered, deps=[grad_output, grad_query])
    return (
        layer_out,
        grad_tokens,
        grad_query,
        grad_key,
        grad_value,
        grad_output,
        side_grads[:EXPERTS].T,
        side_grads[EXPERTS + 1],
        side_grads[EXPERTS],
        side_grads[EXPERTS + 2, :group],
        side_grads[EXPERTS + 3, :group],
        grad_experts,
    )


def solution(mesh):
    nf, nt = mesh.shape["fsdp"], mesh.shape["tensor"]
    rows, both, line = P("fsdp", None), P("fsdp", "tensor"), P("fsdp")
    experts = P("fsdp", None, None, "tensor")
    return jax.shard_map(
        functools.partial(on_device, nf, nt),
        mesh=mesh,
        in_specs=(rows, rows, rows, both, both, both, both, rows, line, line, line, line, experts),
        out_specs=(rows, rows, both, both, both, both, rows, line, line, line, line, experts),
        check_vma=False,
    )
```
